128 devices in a mesh: dp: 16 (over x, z_hi, core), tensor: 8 (over z_lo, y).
Axes of the slice: x: 4, y: 4, z: 4 (z_hi: 2, z_lo: 2; z = z_hi * 2 + z_lo), core: 2. Of those that a mesh axis runs over, the one named last changes fastest.
Arguments:
- resid: bfloat16 [8192, 4096], P('dp', 'tensor'), may hold values from -32 to 32
- hidden: bfloat16 [8192, 14336], P('dp', 'tensor'), may hold values from -6 to 6
- down_weight: bfloat16 [14336, 4096], P('tensor'), may hold values from -1 to 1
- gain: float32 [4096], replicated, may hold values from 0.1 to 1.9
- domain_ids: int32 [16], replicated, may hold values from 0 to 3
Outputs:
- grad_hidden: bfloat16 [8192, 14336], P('dp', 'tensor')
- grad_resid: bfloat16 [8192, 4096], P('dp', 'tensor')
- grad_down: float32 [14336, 4096], P('tensor', 'dp')
- grad_gain: float32 [4096], P('tensor')
The draws below stay inside these ranges and needn't reach their ends.
All inputs are finite; a program needn't handle non-finite values.
Results may differ from the reference program's by a relative error of at most 0.0034.
Values may be sent and summed in bfloat16 or wider, within the bound.
No kernel may reach another device: no remote copies, remote signals or barrier semaphores. Data moves between devices by JAX's collectives and lax.ppermute only.
A program may use at most 128 MiB of HBM per device.

```python
import math
import jax
import jax.numpy as jnp
from jax import lax

D = 4096
FF = 14336
SEQ = 128
PAIRS_DEV = 2
DOMAINS = 4
SHARDS = 16
NPAIRS = 32
TOKENS = 8192


def draw_resid(key, part):
    key = jax.random.fold_in(key, 7)
    base_key, row_key, col_key = jax.random.split(key, 3)
    row_scale = jnp.exp(jax.random.uniform(row_key, (TOKENS, 1), jnp.float32, math.log(0.1), 0.0))
    col_pos = jnp.arange(D, dtype=jnp.float32)[None, :] / D
    col_jitter = jax.random.uniform(col_key, (1, D), jnp.float32, 0.7, 1.4)
    col_scale = 0.5 * jnp.exp(math.log(10.0) * col_pos) * col_jitter
    base = jnp.clip(jax.random.normal(base_key, (TOKENS, D), jnp.float32), -4.0, 4.0)
    return (base * row_scale * col_scale).astype(jnp.bfloat16)


def draw_hidden(key, part):
    key = jax.random.fold_in(key, 11)
    base_key, shift_key = jax.random.split(key, 2)
    base = jnp.clip(jax.random.normal(base_key, (TOKENS, FF), jnp.float32), -4.0, 4.0)
    shift = jax.random.uniform(shift_key, (TOKENS, 1), jnp.float32, -0.15, 0.15)
    return (base + shift).astype(jnp.bfloat16)


def draw_down_weight(key, part):
    key = jax.random.fold_in(key, 13)
    base_key, common_key = jax.random.split(key, 2)
    base = jnp.clip(jax.random.normal(base_key, (FF, D), jnp.float32), -3.0, 3.0)
    common = jnp.clip(jax.random.normal(common_key, (1, D), jnp.float32), -3.0, 3.0)
    return (base / math.sqrt(FF) + common * (16.0 / FF)).astype(jnp.bfloat16)


def with_ends(array, own_key, least, high):
    extent = array.shape
    index_at = [jax.random.randint(jax.random.fold_in(own_key, axis), (), 0, extent[axis]) for axis in range(len(extent))]
    array = array.at[tuple(index_at)].set(least)
    longest = extent.index(max(extent))
    index_at[longest] = (index_at[longest] + 1) % extent[longest]
    return array.at[tuple(index_at)].set(high)


def setup_inputs(seed: int = 0) -> dict:
    arg_keys = jax.random.split(jax.random.key(seed), 6)
    return {
        "resid": draw_resid(jax.random.fold_in(arg_keys[5], 71), 0),
        "hidden": draw_hidden(jax.random.fold_in(arg_keys[5], 71), 0),
        "down_weight": draw_down_weight(jax.random.fold_in(arg_keys[5], 71), 0),
        "gain": jnp.clip(1.0 + 0.18 * jax.random.normal(arg_keys[3], (D,), jnp.float32), 0.1, 1.9),
        "domain_ids": with_ends(jax.random.randint(arg_keys[4], (SHARDS,), 0, DOMAINS), jax.random.fold_in(arg_keys[4], 1), 0, DOMAINS - 1).astype(jnp.int32),
    }


score_scale = 20.0
loss_scale = 8192.0
eps_norm = 1e-05
eps_embed = 1e-06

def pool_tokens(layer, gain):
    inverse = lax.rsqrt(lax.optimization_barrier(jnp.mean(layer * layer, axis=1, keepdims=True)) + eps_norm)
    normed = layer * inverse * gain[None, :]
    return lax.optimization_barrier(jnp.mean(normed.reshape(-1, SEQ, D), axis=1))

def objective(pooled, domain_ids):
    pair_view = pooled.reshape(NPAIRS, 2, D)
    pair_norm = jnp.sqrt(lax.optimization_barrier(jnp.sum(pair_view * pair_view, axis=2, keepdims=True)) + eps_embed)
    unit_vecs = pair_view / pair_norm
    scores = score_scale * jnp.dot(unit_vecs[:, 0], unit_vecs[:, 1].T, precision=lax.Precision.HIGHEST)
    owners = jnp.repeat(domain_ids, PAIRS_DEV)
    same_domain = owners[:, None] == owners[None, :]
    row_totals = lax.optimization_barrier(jnp.sum(jnp.where(same_domain, jnp.exp(scores), 0.0), axis=1))
    row_loss = jnp.log(row_totals) - jnp.diagonal(scores)
    return loss_scale * jnp.sum(row_loss)

def reference(resid, hidden, down_weight, gain, domain_ids):
    layer = resid.astype(jnp.float32) + jnp.dot(hidden, down_weight, preferred_element_type=jnp.float32)
    pooled, pull_back = jax.vjp(pool_tokens, layer, gain)
    d_pooled = jax.grad(objective)(pooled, domain_ids)
    d_layer, grad_gain = pull_back(d_pooled)
    grad_resid = d_layer.astype(jnp.bfloat16)
    grad_hidden = jnp.dot(grad_resid, down_weight.T, preferred_element_type=jnp.float32).astype(jnp.bfloat16)
    hidden_blocks = hidden.reshape(SHARDS, -1, FF)
    grad_blocks = grad_resid.reshape(SHARDS, -1, D)

    def add_shard(running, operands):
        hidden_blk, grad_blk = operands
        partial_sum = jnp.dot(hidden_blk.T, grad_blk, preferred_element_type=jnp.float32)
        return (running + partial_sum, None)
    grad_down, _ = lax.scan(add_shard, jnp.zeros((FF, D), jnp.float32), (hidden_blocks, grad_blocks))
    return (grad_hidden, grad_resid, grad_down, grad_gain)
```

```python
import functools
import jax
import jax.numpy as jnp
from jax import lax
from jax.experimental import pallas as pl
from jax.experimental.pallas import tpu as pltpu
from jax.sharding import PartitionSpec as P

SEQ = 128
NX, NZH, NCORE, NZL, NY = 4, 2, 2, 2, 4

score_scale = 20.0
loss_scale = 8192.0
eps_norm = 1e-05
eps_embed = 1e-06
highest = lax.Precision.HIGHEST
f32 = jnp.float32
bf16 = jnp.bfloat16
MIB = 1024 * 1024


def dp_route(dx, dz, dc):
    pairs = []
    for x in range(NX):
        for z in range(NZH):
            for c in range(NCORE):
                to = (((x + dx) % NX) * NZH + (z + dz) % NZH) * NCORE + (c + dc) % NCORE
                pairs.append(((x * NZH + z) * NCORE + c, to))
    return pairs


def tensor_route(dz, dy):
    pairs = []
    for z in range(NZL):
        for y in range(NY):
            pairs.append((z * NY + y, ((z + dz) % NZL) * NY + (y + dy) % NY))
    return pairs


def over_x(value, step):
    return lax.ppermute(value, "dp", dp_route(step, 0, 0))


def over_zh(value):
    return lax.ppermute(value, "dp", dp_route(0, 1, 0))


def over_core(value):
    return lax.ppermute(value, "dp", dp_route(0, 0, 1))


def over_y(value, step):
    return lax.ppermute(value, "tensor", tensor_route(0, step))


def over_zl(value):
    return lax.ppermute(value, "tensor", tensor_route(1, 0))


def gather_small(value, axis):
    n = lax.axis_size(axis)
    copies = jnp.broadcast_to(value[None], (n,) + value.shape)
    return lax.all_to_all(copies, axis, 0, 0)


def slab_dot_kernel(slab_ref, hidden_ref, weight_ref, out_ref):
    out_ref[0] = jnp.dot(
        hidden_ref[...], weight_ref[...], preferred_element_type=f32
    ).astype(out_ref.dtype)


def slab_dot(hidden, weight, slabs, width, out_dtype):
    tokens, units = hidden.shape
    count = slabs.shape[0]
    return pl.pallas_call(
        slab_dot_kernel,
        grid_spec=pltpu.PrefetchScalarGridSpec(
            num_scalar_prefetch=1,
            grid=(count,),
            in_specs=[
                pl.BlockSpec((tokens, units), lambda i, s: (0, 0)),
                pl.BlockSpec((units, width), lambda i, s: (0, s[i])),
            ],
            out_specs=pl.BlockSpec((1, tokens, width), lambda i, s: (i, 0, 0)),
        ),
        out_shape=jax.ShapeDtypeStruct((count, tokens, width), out_dtype),
        compiler_params=pltpu.CompilerParams(vmem_limit_bytes=24 * MIB),
        cost_estimate=pl.CostEstimate(
            flops=2 * count * tokens * units * width,
            bytes_accessed=2 * (tokens * units + count * units * width + count * tokens * width),
            transcendentals=0,
        ),
    )(slabs, hidden, weight)


def contrast_kernel(mean_ref, gain_ref, same_ref, scaled_ref, gain_grad_ref):
    slabs, seqs, _ = mean_ref.shape
    rows = lax.broadcasted_iota(jnp.int32, (seqs, seqs), 0)
    cols = lax.broadcasted_iota(jnp.int32, (seqs, seqs), 1)
    across = (((1,), (1,)), ((), ()))
    gram = jnp.zeros((seqs, seqs), f32)
    for b in range(slabs):
        pooled = mean_ref[b] * gain_ref[b]
        gram += lax.dot_general(pooled, pooled, across, precision=highest, preferred_element_type=f32)
    diagonal = jnp.where(rows == cols, gram, 0.0)
    norm_col = jnp.sqrt(jnp.sum(diagonal, axis=1, keepdims=True) + eps_embed)
    norm_row = jnp.sqrt(jnp.sum(diagonal, axis=0, keepdims=True) + eps_embed)
    norms = norm_col * norm_row
    scores = score_scale * gram / norms
    query = rows % 2 == 0
    valid = query & (cols % 2 == 1) & (same_ref[...] > 0.5)
    weights = jnp.where(valid, jnp.exp(scores), 0.0)
    totals = jnp.sum(weights, axis=1, keepdims=True)
    soft = weights / jnp.where(totals > 0.0, totals, 1.0)
    target = jnp.where(query & (cols == rows + 1), 1.0, 0.0)
    d_score = loss_scale * (soft - target)
    both = d_score + d_score.T
    coef = jnp.sum(both * scores, axis=1, keepdims=True)
    mix = score_scale * both / norms - jnp.where(rows == cols, coef / (norm_col * norm_col), 0.0)
    for b in range(slabs):
        gain = gain_ref[b]
        mean = mean_ref[b]
        d_pooled = jnp.dot(mix, mean * gain, precision=highest, preferred_element_type=f32)
        gain_grad_ref[b] = jnp.sum(d_pooled * mean, axis=0, keepdims=True)
        scaled_ref[b] = d_pooled * gain * (1.0 / SEQ)


def contrast(means, gain, same):
    slabs, seqs, width = means.shape
    return pl.pallas_call(
        contrast_kernel,
        out_shape=(
            jax.ShapeDtypeStruct((slabs, seqs, width), f32),
            jax.ShapeDtypeStruct((slabs, 1, width), f32),
        ),
        compiler_params=pltpu.CompilerParams(vmem_limit_bytes=24 * MIB),
        cost_estimate=pl.CostEstimate(
            flops=24 * seqs * seqs * slabs * width, bytes_accessed=8 * slabs * seqs * width, transcendentals=seqs * seqs
        ),
    )(means, gain.reshape(slabs, 1, width), same)


def layer_grad_kernel(first_ref, layer_ref, scaled_ref, inverse_ref, low_ref, coef_ref):
    slabs, _, width = layer_ref.shape
    seq = first_ref[0] + pl.program_id(0)
    along = None
    for b in range(slabs):
        term = layer_ref[b].astype(f32) * scaled_ref[b, pl.ds(seq, 1), :]
        along = term if along is None else along + term
    inverse = inverse_ref[...]
    model_width = slabs * width
    coef = inverse * inverse * inverse * jnp.sum(along, axis=1, keepdims=True) / model_width
    coef_ref[...] = coef
    for b in range(slabs):
        low_ref[b] = (
            inverse * scaled_ref[b, pl.ds(seq, 1), :] - layer_ref[b].astype(f32) * coef
        ).astype(bf16)


def layer_grad(layer, scaled, inverse, first):
    slabs, tokens, width = layer.shape
    whole = pl.BlockSpec(scaled.shape, lambda i, s: (0, 0, 0))
    rows = pl.BlockSpec((slabs, SEQ, width), lambda i, s: (0, i, 0))
    column = pl.BlockSpec((SEQ, 1), lambda i, s: (i, 0))
    return pl.pallas_call(
        layer_grad_kernel,
        grid_spec=pltpu.PrefetchScalarGridSpec(
            num_scalar_prefetch=1,
            grid=(tokens // SEQ,),
            in_specs=[rows, whole, column],
            out_specs=[rows, column],
        ),
        out_shape=(
            jax.ShapeDtypeStruct((slabs, tokens, width), bf16),
            jax.ShapeDtypeStruct((tokens, 1), f32),
        ),
        compiler_params=pltpu.CompilerParams(vmem_limit_bytes=24 * MIB),
        cost_estimate=pl.CostEstimate(
            flops=6 * slabs * tokens * width, bytes_accessed=4 * slabs * tokens * width, transcendentals=0
        ),
    )(first, layer, scaled, inverse)


def hidden_grad_kernel(low_ref, weight_ref, out_ref, total_ref):
    step = pl.program_id(0)
    part = lax.dot_general(
        low_ref[0], weight_ref[...], (((1,), (1,)), ((), ())), preferred_element_type=f32
    )

    @pl.when(step == 0)
    def _():
        total_ref[...] = part

    @pl.when(step > 0)
    def _():
        total_ref[...] += part

    @pl.when(step == pl.num_programs(0) - 1)
    def _():
        out_ref[...] = total_ref[...].astype(out_ref.dtype)


def hidden_grad(low, weight):
    slabs, tokens, width = low.shape
    units = weight.shape[0]
    return pl.pallas_call(
        hidden_grad_kernel,
        grid=(slabs,),
        in_specs=[
            pl.BlockSpec((1, tokens, width), lambda i: (i, 0, 0)),
            pl.BlockSpec((units, width), lambda i: (0, i)),
        ],
        out_specs=pl.BlockSpec((tokens, units), lambda i: (0, 0)),
        out_shape=jax.ShapeDtypeStruct((tokens, units), bf16),
        scratch_shapes=[pltpu.VMEM((tokens, units), f32)],
        compiler_params=pltpu.CompilerParams(vmem_limit_bytes=32 * MIB),
        cost_estimate=pl.CostEstimate(
            flops=2 * slabs * tokens * units * width,
            bytes_accessed=2 * (slabs * tokens * width + slabs * units * width + tokens * units),
            transcendentals=0,
        ),
    )(low, weight)


def per_device(resid, hidden, down_weight, gain, domain_ids):
    tokens, units = hidden.shape
    model_width = down_weight.shape[1]
    group = lax.axis_size("tensor")
    shards = lax.axis_size("dp")
    width = model_width // group
    seqs_here = tokens // SEQ
    seqs = seqs_here * shards
    rank = lax.axis_index("tensor")
    zl, y = rank // NY, rank % NY
    shard = lax.axis_index("dp")
    x, zh, core = shard // (NZH * NCORE), (shard // NCORE) % NZH, shard % NCORE

    def slab_pair(step):
        column = (y + step) % NY
        return jnp.stack([zl * NY + column, (1 - zl) * NY + column]).astype(jnp.int32)

    with jax.named_scope("hidden_exchange"):
        hidden_x = [hidden] + [over_x(hidden, step) for step in (1, -1, 2)]

    with jax.named_scope("layer_sum"):
        far = slab_dot(hidden, down_weight, slab_pair(2), width, bf16)
        from_left = over_y(far[0], 1)
        from_right = over_y(far[1], -1)
        right = slab_dot(hidden, down_weight, slab_pair(1), width, bf16)
        left = slab_dot(hidden, down_weight, slab_pair(3), width, bf16)
        got_right1 = over_y(right[1], 1)
        got_left0 = over_y(left[0], -1)
        right0 = (right[0].astype(f32) + from_left.astype(f32)).astype(bf16)
        left1 = (left[1].astype(f32) + from_right.astype(f32)).astype(bf16)
        got_right0 = over_y(right0, 1)
        got_left1 = over_y(left1, -1)
        own = slab_dot(hidden, down_weight, slab_pair(0), width, f32)
        other_sum = own[1] + got_right1.astype(f32) + got_left1.astype(f32)
        from_zl = over_zl(other_sum.astype(bf16))
        layer = (
            own[0]
            + resid.astype(f32)
            + got_right0.astype(f32)
            + got_left0.astype(f32)
            + from_zl.astype(f32)
        )

    with jax.named_scope("layer_gather"):
        low_layer = layer.astype(bf16)
        zl_slab = over_zl(low_layer)
        y_slabs = {(0, 0): low_layer, (1, 0): zl_slab}
        for part in (0, 1):
            y_slabs[part, 1] = over_y(y_slabs[part, 0], -1)
            y_slabs[part, 3] = over_y(y_slabs[part, 0], 1)
        y_slabs[0, 2] = over_y(y_slabs[0, 3], 1)
        y_slabs[1, 2] = over_y(y_slabs[1, 1], -1)
        layer_all = jnp.zeros((group, tokens, width), bf16)
        for (part, step), slab in y_slabs.items():
            index = ((zl + part) % NZL) * NY + (y + step) % NY
            layer_all = lax.dynamic_update_slice(layer_all, slab[None], (index, 0, 0))

    with jax.named_scope("layer_exchange"):
        per_x = group // NX
        layer_x = []
        for step in (0, 1, -1, 2):
            first = ((x + step) % NX) * per_x
            block = lax.dynamic_slice_in_dim(layer_all, first, per_x, 0)
            layer_x.append(block if step == 0 else over_x(block, step))

    with jax.named_scope("norm"):
        squares = jnp.sum(layer * layer, axis=1)
        squares = jnp.sum(gather_small(squares, "tensor"), axis=0)
        inverse = lax.rsqrt(squares / model_width + eps_norm)
        means = jnp.mean((layer * inverse[:, None]).reshape(seqs_here, SEQ, width), axis=1)

    with jax.named_scope("contrast"):
        means_all = gather_small(means, "dp").reshape(seqs, width)
        means_full = gather_small(means_all, "tensor")
        owners = jnp.repeat(domain_ids, seqs_here)
        same = (owners[:, None] == owners[None, :]).astype(f32)
        scaled, gain_grad = contrast(means_full, gain, same)
        grad_gain = lax.dynamic_slice_in_dim(gain_grad, rank, 1, 0).reshape(width)

    with jax.named_scope("layer_grad"):
        first_seq = shard * seqs_here
        inverse_col = inverse[:, None]
        low, coef = layer_grad(
            layer_all, scaled, inverse_col, first_seq.astype(jnp.int32).reshape(1)
        )
        grad_resid = lax.dynamic_slice_in_dim(low, rank, 1, 0)[0]

    with jax.named_scope("down_grad"):
        factors = jnp.stack([inverse, coef[:, 0]])
        factors_x = [factors] + [over_x(factors, step) for step in (1, -1, 2)]
        half = width // NCORE
        hidden_rows = jnp.concatenate(hidden_x, axis=0)

        def low_block(part, side):
            slab = (zh + part) % NZH
            column = ((core + side) % NCORE) * half
            blocks = []
            for i, step in enumerate((0, -1, 1, 2)):
                peer = ((x + step) % NX) * (NZH * NCORE) + zh * NCORE + core
                layer_block = lax.dynamic_slice(layer_x[i], (slab, 0, column), (1, tokens, half))[0]
                scaled_block = lax.dynamic_slice(
                    scaled, (x * per_x + slab, peer * seqs_here, column), (1, seqs_here, half)
                )[0]
                wide = jnp.broadcast_to(scaled_block[:, None], (seqs_here, SEQ, half)).reshape(tokens, half)
                blocks.append(
                    (
                        factors_x[i][0][:, None] * wide
                        - layer_block.astype(f32) * factors_x[i][1][:, None]
                    ).astype(bf16)
                )
            return jnp.concatenate(blocks, axis=0)

        def down(part, side):
            return lax.dot_general(
                hidden_rows,
                low_block(part, side),
                (((0,), (0,)), ((), ())),
                preferred_element_type=f32,
            )

        sent = over_core(down(1, 1).astype(bf16))
        across = over_zh((down(1, 0) + sent.astype(f32)).astype(bf16))
        near = over_core(down(0, 1).astype(bf16))
        grad_down = down(0, 0) + near.astype(f32) + across.astype(f32)

    with jax.named_scope("hidden_grad"):
        grad_hidden = hidden_grad(low, down_weight)

    return (grad_hidden, grad_resid, grad_down, grad_gain)


def solution(mesh):
    return jax.shard_map(
        per_device,
        mesh=mesh,
        in_specs=(P("dp", "tensor"), P("dp", "tensor"), P("tensor", None), P(), P()),
        out_specs=(P("dp", "tensor"), P("dp", "tensor"), P("tensor", "dp"), P("tensor")),
        check_vma=False,
    )
```

```python
import functools
import jax
import jax.numpy as jnp
from jax import lax
from jax.experimental import pallas as pl
from jax.experimental.pallas import tpu as pltpu
from jax.sharding import PartitionSpec as P

SEQ = 128
NX, NZH, NCORE, NZL, NY = 4, 2, 2, 2, 4

score_scale = 20.0
loss_scale = 8192.0
eps_norm = 1e-05
eps_embed = 1e-06
highest = lax.Precision.HIGHEST
f32 = jnp.float32
bf16 = jnp.bfloat16
MIB = 1024 * 1024


def dp_route(dx, dz, dc):
    pairs = []
    for x in range(NX):
        for z in range(NZH):
            for c in range(NCORE):
                to = (((x + dx) % NX) * NZH + (z + dz) % NZH) * NCORE + (c + dc) % NCORE
                pairs.append(((x * NZH + z) * NCORE + c, to))
    return pairs


def tensor_route(dz, dy):
    pairs = []
    for z in range(NZL):
        for y in range(NY):
            pairs.append((z * NY + y, ((z + dz) % NZL) * NY + (y + dy) % NY))
    return pairs


def resid_route(step):
    return [(r, (r % NY % 2) * NY + (r // 2 + step) % NY) for r in range(NZL * NY)]


def over_x(value, step):
    return lax.ppermute(value, "dp", dp_route(step, 0, 0))


def over_zh(value):
    return lax.ppermute(value, "dp", dp_route(0, 1, 0))


def over_core(value):
    return lax.ppermute(value, "dp", dp_route(0, 0, 1))


def over_y(value, step):
    return lax.ppermute(value, "tensor", tensor_route(0, step))


def over_zl(value):
    return lax.ppermute(value, "tensor", tensor_route(1, 0))


def gather_small(value, axis):
    n = lax.axis_size(axis)
    copies = jnp.broadcast_to(value[None], (n,) + value.shape)
    return lax.all_to_all(copies, axis, 0, 0)


def strip_dot_kernel(owner_ref, hidden_ref, *refs):
    *weight_refs, out_ref = refs
    weight = jnp.concatenate([ref[...] for ref in weight_refs], axis=1)
    total = jnp.dot(hidden_ref[...], weight, preferred_element_type=f32)
    lanes = out_ref.shape[-1]
    for b in range(len(weight_refs)):
        out_ref[0, b] = total[:, b * lanes : (b + 1) * lanes].astype(out_ref.dtype)


def strip_dot(hidden, weight, owners, group, out_dtype):
    tokens, units = hidden.shape
    count = owners.shape[0]
    lanes = weight.shape[1] // (NX * group)
    strips = [
        pl.BlockSpec((units, lanes), functools.partial(lambda b, i, s: (0, b * group + s[i]), b))
        for b in range(NX)
    ]
    return pl.pallas_call(
        strip_dot_kernel,
        grid_spec=pltpu.PrefetchScalarGridSpec(
            num_scalar_prefetch=1,
            grid=(count,),
            in_specs=[pl.BlockSpec((tokens, units), lambda i, s: (0, 0))] + strips,
            out_specs=pl.BlockSpec((1, NX, tokens, lanes), lambda i, s: (i, 0, 0, 0)),
        ),
        out_shape=jax.ShapeDtypeStruct((count, NX, tokens, lanes), out_dtype),
        compiler_params=pltpu.CompilerParams(vmem_limit_bytes=56 * MIB),
        cost_estimate=pl.CostEstimate(
            flops=2 * count * tokens * units * NX * lanes,
            bytes_accessed=2 * (tokens * units + count * (units + tokens) * NX * lanes),
            transcendentals=0,
        ),
    )(owners, hidden, *([weight] * NX))


def contrast_kernel(mean_ref, gain_ref, same_ref, scaled_ref, gain_grad_ref):
    slabs, seqs, _ = mean_ref.shape
    rows = lax.broadcasted_iota(jnp.int32, (seqs, seqs), 0)
    cols = lax.broadcasted_iota(jnp.int32, (seqs, seqs), 1)
    across = (((1,), (1,)), ((), ()))
    gram = jnp.zeros((seqs, seqs), f32)
    for b in range(slabs):
        pooled = mean_ref[b] * gain_ref[b]
        gram += lax.dot_general(pooled, pooled, across, precision=highest, preferred_element_type=f32)
    diagonal = jnp.where(rows == cols, gram, 0.0)
    norm_col = jnp.sqrt(jnp.sum(diagonal, axis=1, keepdims=True) + eps_embed)
    norm_row = jnp.sqrt(jnp.sum(diagonal, axis=0, keepdims=True) + eps_embed)
    norms = norm_col * norm_row
    scores = score_scale * gram / norms
    query = rows % 2 == 0
    valid = query & (cols % 2 == 1) & (same_ref[...] > 0.5)
    weights = jnp.where(valid, jnp.exp(scores), 0.0)
    totals = jnp.sum(weights, axis=1, keepdims=True)
    soft = weights / jnp.where(totals > 0.0, totals, 1.0)
    target = jnp.where(query & (cols == rows + 1), 1.0, 0.0)
    d_score = loss_scale * (soft - target)
    both = d_score + d_score.T
    coef = jnp.sum(both * scores, axis=1, keepdims=True)
    mix = score_scale * both / norms - jnp.where(rows == cols, coef / (norm_col * norm_col), 0.0)
    for b in range(slabs):
        gain = gain_ref[b]
        mean = mean_ref[b]
        d_pooled = jnp.dot(mix, mean * gain, precision=highest, preferred_element_type=f32)
        gain_grad_ref[b] = jnp.sum(d_pooled * mean, axis=0, keepdims=True)
        scaled_ref[b] = d_pooled * gain * (1.0 / SEQ)


def contrast(means, gain, same):
    slabs, seqs, width = means.shape
    return pl.pallas_call(
        contrast_kernel,
        out_shape=(
            jax.ShapeDtypeStruct((slabs, seqs, width), f32),
            jax.ShapeDtypeStruct((slabs, 1, width), f32),
        ),
        compiler_params=pltpu.CompilerParams(vmem_limit_bytes=24 * MIB),
        cost_estimate=pl.CostEstimate(
            flops=24 * seqs * seqs * slabs * width, bytes_accessed=8 * slabs * seqs * width, transcendentals=seqs * seqs
        ),
    )(means, gain, same)


def row_to_column(row):
    n = row.shape[1]
    eye = lax.broadcasted_iota(jnp.int32, (n, n), 0) == lax.broadcasted_iota(jnp.int32, (n, n), 1)
    return jnp.sum(jnp.where(eye, jnp.broadcast_to(row, (n, n)), 0.0), axis=1, keepdims=True)


def column_to_row(column):
    n = column.shape[0]
    eye = lax.broadcasted_iota(jnp.int32, (n, n), 0) == lax.broadcasted_iota(jnp.int32, (n, n), 1)
    return jnp.sum(jnp.where(eye, jnp.broadcast_to(column, (n, n)), 0.0), axis=0, keepdims=True)


def layer_grad_kernel(first_ref, layer_ref, scaled_ref, inverse_ref, low_ref, coef_ref):
    group, blocks, _, lanes = layer_ref.shape
    here = pl.program_id(0)
    seq = first_ref[0] + here
    along = None
    for r in range(group):
        scaled = scaled_ref[r, pl.ds(seq, 1), :]
        for b in range(blocks):
            term = layer_ref[r, b].astype(f32) * scaled[:, b * lanes : (b + 1) * lanes]
            along = term if along is None else along + term
    inverse = row_to_column(inverse_ref[pl.ds(here, 1), :])
    model_width = group * blocks * lanes
    coef = inverse * inverse * inverse * jnp.sum(along, axis=1, keepdims=True) / model_width
    coef_ref[pl.ds(here, 1), :] = column_to_row(coef)
    for r in range(group):
        scaled = scaled_ref[r, pl.ds(seq, 1), :]
        for b in range(blocks):
            column = (b * group + r) * lanes
            low_ref[:, column : column + lanes] = (
                inverse * scaled[:, b * lanes : (b + 1) * lanes] - layer_ref[r, b].astype(f32) * coef
            ).astype(bf16)


def layer_grad(strips, scaled, inverse, first):
    group, _, tokens, lanes = strips.shape
    seqs_here = tokens // SEQ
    model_width = group * NX * lanes
    return pl.pallas_call(
        layer_grad_kernel,
        grid_spec=pltpu.PrefetchScalarGridSpec(
            num_scalar_prefetch=1,
            grid=(seqs_here,),
            in_specs=[
                pl.BlockSpec((group, NX, SEQ, lanes), lambda i, s: (0, 0, i, 0)),
                pl.BlockSpec(scaled.shape, lambda i, s: (0, 0, 0)),
                pl.BlockSpec((seqs_here, SEQ), lambda i, s: (0, 0)),
            ],
            out_specs=[
                pl.BlockSpec((SEQ, model_width), lambda i, s: (i, 0)),
                pl.BlockSpec((seqs_here, SEQ), lambda i, s: (0, 0)),
            ],
        ),
        out_shape=(
            jax.ShapeDtypeStruct((tokens, model_width), bf16),
            jax.ShapeDtypeStruct((seqs_here, SEQ), f32),
        ),
        compiler_params=pltpu.CompilerParams(vmem_limit_bytes=24 * MIB),
        cost_estimate=pl.CostEstimate(
            flops=6 * tokens * model_width, bytes_accessed=4 * tokens * model_width, transcendentals=0
        ),
    )(first, strips, scaled, inverse)


def group_grad_kernel(plan_ref, layer_ref, scaled_ref, factor_ref, low_ref):
    group, _, tokens, lanes = layer_ref.shape
    here = pl.program_id(0)
    first, me = plan_ref[4 + here], plan_ref[9]
    seqs_here = tokens // SEQ
    for s in range(seqs_here):
        rows = slice(s * SEQ, (s + 1) * SEQ)
        inverse = row_to_column(factor_ref[here, s : s + 1, :])
        coef = row_to_column(factor_ref[here, seqs_here + s : seqs_here + s + 1, :])
        for r in range(group):
            scaled = scaled_ref[r, pl.ds(first + s, 1), :]
            low = inverse * scaled - layer_ref[r, 0, rows, :].astype(f32) * coef
            side = r % 2 * lanes
            low_ref[(r // 2) ^ me, rows, side : side + lanes] = low.astype(bf16)


def group_grad(strips, scaled, factors, plan):
    group, _, tokens, lanes = strips.shape
    quarter = group * lanes // 4
    return pl.pallas_call(
        group_grad_kernel,
        grid_spec=pltpu.PrefetchScalarGridSpec(
            num_scalar_prefetch=1,
            grid=(NX,),
            in_specs=[
                pl.BlockSpec((group, 1, tokens, lanes), lambda i, s: (0, s[i], 0, 0)),
                pl.BlockSpec(scaled.shape[:2] + (lanes,), lambda i, s: (0, 0, s[8])),
                pl.BlockSpec(factors.shape, lambda i, s: (0, 0, 0)),
            ],
            out_specs=pl.BlockSpec((4, tokens, quarter), lambda i, s: (0, i, 0)),
        ),
        out_shape=jax.ShapeDtypeStruct((4, NX * tokens, quarter), bf16),
        compiler_params=pltpu.CompilerParams(vmem_limit_bytes=24 * MIB),
        cost_estimate=pl.CostEstimate(
            flops=3 * NX * tokens * group * lanes, bytes_accessed=4 * NX * tokens * group * lanes, transcendentals=0
        ),
    )(plan, strips, scaled, factors)


def hidden_grad_kernel(low_ref, weight_ref, out_ref, total_ref):
    step = pl.program_id(0)
    part = lax.dot_general(
        low_ref[...], weight_ref[...], (((1,), (1,)), ((), ())), preferred_element_type=f32
    )

    @pl.when(step == 0)
    def _():
        total_ref[...] = part

    @pl.when(step > 0)
    def _():
        total_ref[...] += part

    @pl.when(step == pl.num_programs(0) - 1)
    def _():
        out_ref[...] = total_ref[...].astype(out_ref.dtype)


def hidden_grad(low, weight, steps):
    tokens, model_width = low.shape
    units = weight.shape[0]
    width = model_width // steps
    return pl.pallas_call(
        hidden_grad_kernel,
        grid=(steps,),
        in_specs=[
            pl.BlockSpec((tokens, width), lambda i: (0, i)),
            pl.BlockSpec((units, width), lambda i: (0, i)),
        ],
        out_specs=pl.BlockSpec((tokens, units), lambda i: (0, 0)),
        out_shape=jax.ShapeDtypeStruct((tokens, units), bf16),
        scratch_shapes=[pltpu.VMEM((tokens, units), f32)],
        compiler_params=pltpu.CompilerParams(vmem_limit_bytes=56 * MIB),
        cost_estimate=pl.CostEstimate(
            flops=2 * tokens * units * model_width,
            bytes_accessed=2 * (tokens * model_width + units * model_width + tokens * units),
            transcendentals=0,
        ),
    )(low, weight)


def per_device(resid, hidden, down_weight, gain, domain_ids):
    tokens, units = hidden.shape
    model_width = down_weight.shape[1]
    group = lax.axis_size("tensor")
    shards = lax.axis_size("dp")
    width = model_width // group
    lanes = width // NX
    seqs_here = tokens // SEQ
    seqs = seqs_here * shards
    rank = lax.axis_index("tensor")
    zl, y = rank // NY, rank % NY
    shard = lax.axis_index("dp")
    x, zh, core = shard // (NZH * NCORE), (shard // NCORE) % NZH, shard % NCORE

    def owners(step):
        column = (y + step) % NY
        return jnp.stack([zl * NY + column, (1 - zl) * NY + column]).astype(jnp.int32)

    with jax.named_scope("hidden_exchange"):
        hidden_left = over_x(hidden, 1)
        hidden_right = over_x(hidden, -1)
        hidden_far = (
            over_x(hidden_left[: tokens // 2], 1),
            over_x(hidden_right[tokens // 2 :], -1),
        )
        hidden_rows = jnp.concatenate((hidden, hidden_left, hidden_right) + hidden_far, axis=0)

    with jax.named_scope("resid_exchange"):
        block = rank // 2
        pieces = []
        for step in range(NY):
            first = ((block + step) % NY) * lanes
            piece = lax.dynamic_slice_in_dim(resid, first, lanes, 1)
            pieces.append(lax.ppermute(piece, "tensor", resid_route(step)))
        pieces = jnp.stack(pieces)
        resid_strips = jnp.concatenate(
            [lax.dynamic_slice_in_dim(pieces, (y - b) % NY, 1, 0) for b in range(NX)], axis=0
        )

    with jax.named_scope("layer_sum"):
        far = strip_dot(hidden, down_weight, owners(2), group, bf16)
        from_left = over_y(far[0], 1)
        from_right = over_y(far[1], -1)
        right = strip_dot(hidden, down_weight, owners(1), group, bf16)
        left = strip_dot(hidden, down_weight, owners(3), group, bf16)
        got_right1 = over_y(right[1], 1)
        got_left0 = over_y(left[0], -1)
        right0 = (right[0].astype(f32) + from_left.astype(f32)).astype(bf16)
        left1 = (left[1].astype(f32) + from_right.astype(f32)).astype(bf16)
        got_right0 = over_y(right0, 1)
        got_left1 = over_y(left1, -1)
        own = strip_dot(hidden, down_weight, owners(0), group, f32)
        other_sum = own[1] + got_right1.astype(f32) + got_left1.astype(f32)
        from_zl = over_zl(other_sum.astype(bf16))
        layer = (
            own[0]
            + resid_strips.astype(f32)
            + got_right0.astype(f32)
            + got_left0.astype(f32)
            + from_zl.astype(f32)
        )

    with jax.named_scope("strip_exchange"):
        low_layer = layer.astype(bf16)
        strips_x = [low_layer]
        for step in (1, -1, 2):
            strip = lax.dynamic_slice_in_dim(low_layer, (x + step) % NX, 1, 0)
            strips_x.append(over_x(strip, step))
        message = jnp.concatenate(strips_x, axis=0)

    with jax.named_scope("norm"):
        squares = jnp.sum(layer * layer, axis=(0, 2))
        squares = jnp.sum(gather_small(squares.reshape(seqs_here, SEQ), "tensor"), axis=0)
        squares, message, hidden_rows = lax.optimization_barrier((squares, message, hidden_rows))
        inverse = lax.rsqrt(squares / model_width + eps_norm)
        weighted = layer.reshape(NX, seqs_here, SEQ, lanes) * inverse[None, :, :, None]
        means = jnp.mean(weighted, axis=2).transpose(1, 0, 2)

    with jax.named_scope("strip_gather"):
        got = {(0, 0): message}
        got[1, 0] = over_zl(message)
        got[0, 1] = over_y(message, -1)
        got[0, 3] = over_y(message, 1)
        means_all = gather_small(means, "dp")
        means_all, got[1, 0], got[0, 1], got[0, 3] = lax.optimization_barrier(
            (means_all, got[1, 0], got[0, 1], got[0, 3])
        )
        means_all = means_all.reshape(seqs, width)
        got[1, 1] = over_y(got[1, 0], -1)
        got[1, 3] = over_y(got[1, 0], 1)
        got[0, 2] = over_y(got[0, 3], 1)
        means_full = gather_small(means_all, "tensor")
        got[1, 2] = over_y(got[1, 1], -1)
        strips = jnp.zeros((group,) + message.shape, bf16)
        for (part, step), value in got.items():
            index = ((zl + part) % NZL) * NY + (y + step) % NY
            strips = lax.dynamic_update_slice(strips, value[None], (index, 0, 0, 0))

    with jax.named_scope("contrast"):
        owner = jnp.repeat(domain_ids, seqs_here)
        same = (owner[:, None] == owner[None, :]).astype(f32)
        gain_strips = gain.reshape(NX, group, lanes).transpose(1, 0, 2).reshape(group, 1, width)
        scaled, gain_grad = contrast(means_full, gain_strips, same)
        gain_grad = gain_grad.reshape(group, NX, lanes)
        grad_gain = lax.dynamic_slice(
            gain_grad, ((rank % 2) * NX, rank // 2, 0), (NX, 1, lanes)
        ).reshape(width)

    with jax.named_scope("layer_grad"):
        first_seq = (shard * seqs_here).astype(jnp.int32)
        low, coef = layer_grad(strips, scaled, inverse, first_seq.reshape(1))
        grad_resid = lax.dynamic_slice_in_dim(low, rank * width, width, 1)

    with jax.named_scope("down_grad"):
        factors = jnp.concatenate([inverse, coef], axis=0)
        factors_x = jnp.stack([factors] + [over_x(factors, step) for step in (1, -1, 2)])
        peers = [((x + step) % NX) * (NZH * NCORE) + zh * NCORE + core for step in (0, -1, 1, 2)]
        plan = [x, NX, NX + 1, NX + 2] + [p * seqs_here for p in peers] + [x, zh * NCORE + core]
        plan = jnp.stack([jnp.asarray(v, jnp.int32) for v in plan])
        low_x = group_grad(strips, scaled, factors_x, plan)

        def down(block):
            return lax.dot_general(
                hidden_rows, low_x[block], (((0,), (0,)), ((), ())), preferred_element_type=f32
            )

        from_core = over_core(down(3))
        across = over_zh((down(2) + from_core).astype(bf16))
        near = down(0) + over_core(down(1))
        near, across = lax.optimization_barrier((near, across))
        grad_down = near + across.astype(f32)

    with jax.named_scope("hidden_grad"):
        grad_hidden = hidden_grad(low, down_weight, group)

    return (grad_hidden, grad_resid, grad_down, grad_gain)


def solution(mesh):
    return jax.shard_map(
        per_device,
        mesh=mesh,
        in_specs=(P("dp", "tensor"), P("dp", "tensor"), P("tensor", None), P(), P()),
        out_specs=(P("dp", "tensor"), P("dp", "tensor"), P("tensor", "dp"), P("tensor")),
        check_vma=False,
    )
```

```python
import functools
import jax
import jax.numpy as jnp
from jax import lax
from jax.experimental import pallas as pl
from jax.experimental.pallas import tpu as pltpu
from jax.sharding import PartitionSpec as P

SEQ = 128
NX, NZH, NCORE, NZL, NY = 4, 2, 2, 2, 4

score_scale = 20.0
loss_scale = 8192.0
eps_norm = 1e-05
eps_embed = 1e-06
highest = lax.Precision.HIGHEST
f32 = jnp.float32
bf16 = jnp.bfloat16
MIB = 1024 * 1024


def dp_route(dx, dz, dc):
    pairs = []
    for x in range(NX):
        for z in range(NZH):
            for c in range(NCORE):
                to = (((x + dx) % NX) * NZH + (z + dz) % NZH) * NCORE + (c + dc) % NCORE
                pairs.append(((x * NZH + z) * NCORE + c, to))
    return pairs


def tensor_route(dz, dy):
    pairs = []
    for z in range(NZL):
        for y in range(NY):
            pairs.append((z * NY + y, ((z + dz) % NZL) * NY + (y + dy) % NY))
    return pairs


def resid_route(step):
    pairs = []
    for r in range(NZL * NY):
        j = (r // 2 + step) % NY
        pairs.append((r, (j % 2) * NY + (r % 2) * 2 + j // 2))
    return pairs


def over_x(value, step):
    return lax.ppermute(value, "dp", dp_route(step, 0, 0))


def over_zh(value):
    return lax.ppermute(value, "dp", dp_route(0, 1, 0))


def over_core(value):
    return lax.ppermute(value, "dp", dp_route(0, 0, 1))


def over_y(value, step):
    return lax.ppermute(value, "tensor", tensor_route(0, step))


def over_zl(value):
    return lax.ppermute(value, "tensor", tensor_route(1, 0))


def gather_small(value, axis):
    n = lax.axis_size(axis)
    copies = jnp.broadcast_to(value[None], (n,) + value.shape)
    return lax.all_to_all(copies, axis, 0, 0)


def pair_dot_kernel(plan_ref, hidden_ref, weight_ref, same_ref, other_ref):
    total = jnp.dot(hidden_ref[...], weight_ref[...], preferred_element_type=f32)
    lanes = same_ref.shape[-1]
    first, second = total[:, :lanes], total[:, lanes:]
    flip = plan_ref[1] == 1
    same_ref[0] = jnp.where(flip, second, first).astype(same_ref.dtype)
    other_ref[0] = jnp.where(flip, first, second).astype(other_ref.dtype)


def pair_dot(hidden, weight, column, zl, group, out_dtype):
    tokens, units = hidden.shape
    lanes = weight.shape[1] // (NX * group)
    strips = jax.ShapeDtypeStruct((NX, tokens, lanes), out_dtype)
    out = pl.BlockSpec((1, tokens, lanes), lambda b, s: (b, 0, 0))
    return pl.pallas_call(
        pair_dot_kernel,
        grid_spec=pltpu.PrefetchScalarGridSpec(
            num_scalar_prefetch=1,
            grid=(NX,),
            in_specs=[
                pl.BlockSpec((tokens, units), lambda b, s: (0, 0)),
                pl.BlockSpec((units, 2 * lanes), lambda b, s: (0, b * NY + s[0])),
            ],
            out_specs=[out, out],
        ),
        out_shape=(strips, strips),
        compiler_params=pltpu.CompilerParams(vmem_limit_bytes=56 * MIB),
        cost_estimate=pl.CostEstimate(
            flops=4 * tokens * units * NX * lanes,
            bytes_accessed=2 * (tokens * units + 2 * (units + tokens) * NX * lanes),
            transcendentals=0,
        ),
    )(jnp.stack([column, zl]).astype(jnp.int32), hidden, weight)


def gram_kernel(plan_ref, mean_ref, gain_ref, strip_ref, out_ref):
    pooled = mean_ref[...] * gain_ref[...]
    gram = lax.dot_general(
        pooled, pooled, (((1,), (1,)), ((), ())), precision=highest, preferred_element_type=f32
    )
    out_ref[0] = jnp.concatenate([gram, jnp.zeros_like(gram)], axis=1)
    out_ref[1] = strip_ref[...]


def gram_part(means, gain, x):
    seqs, width = means.shape
    lanes = 2 * seqs
    return pl.pallas_call(
        gram_kernel,
        grid_spec=pltpu.PrefetchScalarGridSpec(
            num_scalar_prefetch=1,
            grid=(1,),
            in_specs=[
                pl.BlockSpec((seqs, width), lambda i, s: (0, 0)),
                pl.BlockSpec((1, width), lambda i, s: (0, 0)),
                pl.BlockSpec((seqs, lanes), lambda i, s: (0, s[0])),
            ],
            out_specs=pl.BlockSpec((2, seqs, lanes), lambda i, s: (0, 0, 0)),
        ),
        out_shape=jax.ShapeDtypeStruct((2, seqs, lanes), f32),
        compiler_params=pltpu.CompilerParams(vmem_limit_bytes=16 * MIB),
        cost_estimate=pl.CostEstimate(
            flops=12 * seqs * seqs * width, bytes_accessed=4 * seqs * (width + 3 * lanes), transcendentals=0
        ),
    )(x.astype(jnp.int32).reshape(1), means, gain, means)


def contrast_kernel(
    plan_ref, part_ref, same_ref, gain_block_ref, mean_ref, gain_ref, block_ref, own_ref, gain_grad_ref
):
    group = part_ref.shape[0]
    seqs = mean_ref.shape[0]
    rows = lax.broadcasted_iota(jnp.int32, (seqs, seqs), 0)
    cols = lax.broadcasted_iota(jnp.int32, (seqs, seqs), 1)
    gram = part_ref[0, 0]
    for r in range(1, group):
        gram += part_ref[r, 0]
    gram = gram[:, :seqs]
    diagonal = jnp.where(rows == cols, gram, 0.0)
    norm_col = jnp.sqrt(jnp.sum(diagonal, axis=1, keepdims=True) + eps_embed)
    norm_row = jnp.sqrt(jnp.sum(diagonal, axis=0, keepdims=True) + eps_embed)
    norms = norm_col * norm_row
    scores = score_scale * gram / norms
    query = rows % 2 == 0
    valid = query & (cols % 2 == 1) & (same_ref[...] > 0.5)
    weights = jnp.where(valid, jnp.exp(scores), 0.0)
    totals = jnp.sum(weights, axis=1, keepdims=True)
    soft = weights / jnp.where(totals > 0.0, totals, 1.0)
    target = jnp.where(query & (cols == rows + 1), 1.0, 0.0)
    d_score = loss_scale * (soft - target)
    both = d_score + d_score.T
    coef = jnp.sum(both * scores, axis=1, keepdims=True)
    mix = score_scale * both / norms - jnp.where(rows == cols, coef / (norm_col * norm_col), 0.0)
    mean, gain = mean_ref[...], gain_ref[...]
    d_pooled = jnp.dot(mix, mean * gain, precision=highest, preferred_element_type=f32)
    gain_grad_ref[...] = jnp.sum(d_pooled * mean, axis=0, keepdims=True)
    own_ref[...] = d_pooled * gain * (1.0 / SEQ)
    for place in range(group):
        part = part_ref[(place % NZL) * NY + place // NZL, 1]
        gain = gain_block_ref[0, place : place + 1, :]
        d_pooled = jnp.dot(mix, part * gain, precision=highest, preferred_element_type=f32)
        block_ref[place] = d_pooled * gain * (1.0 / SEQ)


def contrast(parts, same, gain_blocks, means, gain, x):
    group, _, seqs, lanes = parts.shape
    width = means.shape[1]
    whole = lambda shape: pl.BlockSpec(shape, lambda i, s: (0,) * len(shape))
    return pl.pallas_call(
        contrast_kernel,
        grid_spec=pltpu.PrefetchScalarGridSpec(
            num_scalar_prefetch=1,
            grid=(1,),
            in_specs=[
                whole(parts.shape),
                whole(same.shape),
                pl.BlockSpec((1, group, lanes), lambda i, s: (s[0], 0, 0)),
                whole(means.shape),
                whole(gain.shape),
            ],
            out_specs=[whole((group, seqs, lanes)), whole((seqs, width)), whole((1, width))],
        ),
        out_shape=(
            jax.ShapeDtypeStruct((group, seqs, lanes), f32),
            jax.ShapeDtypeStruct((seqs, width), f32),
            jax.ShapeDtypeStruct((1, width), f32),
        ),
        compiler_params=pltpu.CompilerParams(vmem_limit_bytes=16 * MIB),
        cost_estimate=pl.CostEstimate(
            flops=12 * seqs * seqs * (group * lanes + width), bytes_accessed=16 * group * seqs * lanes, transcendentals=seqs * seqs
        ),
    )(x.astype(jnp.int32).reshape(1), parts, same, gain_blocks, means, gain)


def row_to_column(row):
    n = row.shape[1]
    eye = lax.broadcasted_iota(jnp.int32, (n, n), 0) == lax.broadcasted_iota(jnp.int32, (n, n), 1)
    return jnp.sum(jnp.where(eye, jnp.broadcast_to(row, (n, n)), 0.0), axis=1, keepdims=True)


def column_to_row(column):
    n = column.shape[0]
    eye = lax.broadcasted_iota(jnp.int32, (n, n), 0) == lax.broadcasted_iota(jnp.int32, (n, n), 1)
    return jnp.sum(jnp.where(eye, jnp.broadcast_to(column, (n, n)), 0.0), axis=0, keepdims=True)


def along_kernel(plan_ref, layer_ref, scaled_ref, out_ref):
    group, _, tokens, _ = layer_ref.shape
    first = plan_ref[pl.program_id(0)]
    for s in range(tokens // SEQ):
        rows = slice(s * SEQ, (s + 1) * SEQ)
        along = None
        for p in range(group):
            term = layer_ref[p, 0, rows, :].astype(f32) * scaled_ref[p, pl.ds(first + s, 1), :]
            along = term if along is None else along + term
        out_ref[0, s : s + 1, :] = column_to_row(jnp.sum(along, axis=1, keepdims=True))


def along_part(strips, scaled, plan):
    group, _, tokens, lanes = strips.shape
    seqs_here = tokens // SEQ
    return pl.pallas_call(
        along_kernel,
        grid_spec=pltpu.PrefetchScalarGridSpec(
            num_scalar_prefetch=1,
            grid=(NX,),
            in_specs=[
                pl.BlockSpec((group, 1, tokens, lanes), lambda i, s: (0, i, 0, 0)),
                pl.BlockSpec(scaled.shape, lambda i, s: (0, 0, 0)),
            ],
            out_specs=pl.BlockSpec((1, seqs_here, SEQ), lambda i, s: (i, 0, 0)),
        ),
        out_shape=jax.ShapeDtypeStruct((NX, seqs_here, SEQ), f32),
        compiler_params=pltpu.CompilerParams(vmem_limit_bytes=16 * MIB),
        cost_estimate=pl.CostEstimate(
            flops=2 * NX * tokens * group * lanes, bytes_accessed=2 * NX * tokens * group * lanes, transcendentals=0
        ),
    )(plan, strips, scaled)


ORDERS = ((0, 1, 2, 3), (2, 0, 3, 1), (1, 3, 0, 2), (3, 2, 1, 0))


def group_grad_kernel(plan_ref, layer_ref, scaled_ref, *refs):
    *part_refs, low_ref, coef_ref, factor_ref = refs
    group, _, tokens, lanes = layer_ref.shape
    seqs_here = tokens // SEQ
    here = pl.program_id(0)
    first, me = plan_ref[here], plan_ref[4]

    @pl.when(here == 0)
    def _():
        for i in range(NX):
            inverse = part_refs[i][NX]
            along = part_refs[0][i]
            for ref, order in zip(part_refs[1:], ORDERS[1:]):
                along += ref[order[i]]
            coef = inverse * inverse * inverse * along / (NX * group * lanes)
            factor_ref[i, :seqs_here] = inverse
            factor_ref[i, seqs_here:] = coef
            if i == 0:
                coef_ref[...] = coef

    for s in range(seqs_here):
        rows = slice(s * SEQ, (s + 1) * SEQ)
        inverse = row_to_column(factor_ref[here, s : s + 1, :])
        coef = row_to_column(factor_ref[here, seqs_here + s : seqs_here + s + 1, :])
        for p in range(group):
            scaled = scaled_ref[p, pl.ds(first + s, 1), :]
            low = inverse * scaled - layer_ref[p, 0, rows, :].astype(f32) * coef
            side = p % 2 * lanes
            low_ref[(p // 2) ^ me, rows, side : side + lanes] = low.astype(bf16)


def group_grad(strips, scaled, parts, plan):
    group, _, tokens, lanes = strips.shape
    quarter = group * lanes // 4
    seqs_here = tokens // SEQ
    return pl.pallas_call(
        group_grad_kernel,
        grid_spec=pltpu.PrefetchScalarGridSpec(
            num_scalar_prefetch=1,
            grid=(NX,),
            in_specs=[
                pl.BlockSpec((group, 1, tokens, lanes), lambda i, s: (0, i, 0, 0)),
                pl.BlockSpec(scaled.shape, lambda i, s: (0, 0, 0)),
            ]
            + [pl.BlockSpec(parts[0].shape, lambda i, s: (0, 0, 0))] * NX,
            out_specs=[
                pl.BlockSpec((4, tokens, quarter), lambda i, s: (0, i, 0)),
                pl.BlockSpec((seqs_here, SEQ), lambda i, s: (0, 0)),
            ],
            scratch_shapes=[pltpu.VMEM((NX, 2 * seqs_here, SEQ), f32)],
        ),
        out_shape=(
            jax.ShapeDtypeStruct((4, NX * tokens, quarter), bf16),
            jax.ShapeDtypeStruct((seqs_here, SEQ), f32),
        ),
        compiler_params=pltpu.CompilerParams(vmem_limit_bytes=24 * MIB),
        cost_estimate=pl.CostEstimate(
            flops=3 * NX * tokens * group * lanes, bytes_accessed=4 * NX * tokens * group * lanes, transcendentals=0
        ),
    )(plan, strips, scaled, *parts)


def hidden_grad_kernel(low_ref, weight_ref, out_ref, total_ref):
    step = pl.program_id(0)
    low = jnp.concatenate([low_ref[j, 0] for j in range(low_ref.shape[0])], axis=1)
    part = lax.dot_general(
        low, weight_ref[...], (((1,), (1,)), ((), ())), preferred_element_type=f32
    )

    @pl.when(step == 0)
    def _():
        total_ref[...] = part

    @pl.when(step > 0)
    def _():
        total_ref[...] += part

    @pl.when(step == pl.num_programs(0) - 1)
    def _():
        out_ref[...] = total_ref[...].astype(out_ref.dtype)


def hidden_grad(low, weight):
    group, blocks, tokens, lanes = low.shape
    units = weight.shape[0]
    model_width = group * blocks * lanes
    steps = 2 * blocks
    return pl.pallas_call(
        hidden_grad_kernel,
        grid=(steps,),
        in_specs=[
            pl.BlockSpec((group // 2, 1, tokens, lanes), lambda i: (i % 2, i // 2, 0, 0)),
            pl.BlockSpec((units, model_width // steps), lambda i: (0, i)),
        ],
        out_specs=pl.BlockSpec((tokens, units), lambda i: (0, 0)),
        out_shape=jax.ShapeDtypeStruct((tokens, units), bf16),
        scratch_shapes=[pltpu.VMEM((tokens, units), f32)],
        compiler_params=pltpu.CompilerParams(vmem_limit_bytes=56 * MIB),
        cost_estimate=pl.CostEstimate(
            flops=2 * tokens * units * model_width,
            bytes_accessed=2 * (tokens * model_width + units * model_width + tokens * units),
            transcendentals=0,
        ),
    )(low, weight)


def tie(*values):
    return lax.optimization_barrier(values)


def gather_start(value):
    return {
        (0, 0): value,
        (1, 0): over_zl(value),
        (0, 1): over_y(value, -1),
        (0, 3): over_y(value, 1),
    }


def gather_next(got):
    got = dict(got)
    got[1, 1] = over_y(got[1, 0], -1)
    got[1, 3] = over_y(got[1, 0], 1)
    got[0, 2] = over_y(got[0, 3], 1)
    return got


def gather_end(got, zl, y):
    got = dict(got)
    got[1, 2] = over_y(got[1, 1], -1)
    shape = got[0, 0].shape
    out = jnp.zeros((NZL * NY,) + shape, got[0, 0].dtype)
    for (part, step), value in got.items():
        place = ((y + step) % NY) * NZL + (zl + part) % NZL
        out = lax.dynamic_update_slice(out, value[None], (place,) + (0,) * len(shape))
    return out


def per_device(resid, hidden, down_weight, gain, domain_ids):
    tokens, units = hidden.shape
    model_width = down_weight.shape[1]
    group = lax.axis_size("tensor")
    shards = lax.axis_size("dp")
    width = model_width // group
    lanes = width // NX
    seqs_here = tokens // SEQ
    seqs = seqs_here * shards
    rank = lax.axis_index("tensor")
    zl, y = rank // NY, rank % NY
    place = y * NZL + zl
    shard = lax.axis_index("dp")
    x, zh, core = shard // (NZH * NCORE), (shard // NCORE) % NZH, shard % NCORE

    with jax.named_scope("tables"):
        owner = jnp.repeat(domain_ids, seqs_here)
        same = (owner[:, None] == owner[None, :]).astype(f32)
        gain_blocks = gain.reshape(NX, group, lanes)
        gain_own = lax.dynamic_slice_in_dim(gain_blocks, place, 1, 1).reshape(1, width)
        peers = [((x + step) % NX) * (NZH * NCORE) + zh * NCORE + core for step in (0, -1, 1, 2)]
        plan = [p * seqs_here for p in peers] + [zh * NCORE + core]
        plan = jnp.stack([jnp.asarray(v, jnp.int32) for v in plan])

    with jax.named_scope("hidden_exchange"):
        hidden_left = over_x(hidden, 1)
        hidden_right = over_x(hidden, -1)

    with jax.named_scope("resid_exchange"):
        block = rank // 2
        pieces = []
        for step in range(NY):
            first = ((block + step) % NY) * lanes
            piece = lax.dynamic_slice_in_dim(resid, first, lanes, 1)
            pieces.append(lax.ppermute(piece, "tensor", resid_route(step)))

    with jax.named_scope("layer_sum"):
        def dot_for(step, dtype):
            return pair_dot(hidden, down_weight, (y + step) % NY, zl, group, dtype)

        far = dot_for(2, bf16)
        from_left = over_y(far[0], 1)
        from_right = over_y(far[1], -1)
        right = dot_for(1, bf16)
        left = dot_for(3, bf16)
        got_right1 = over_y(right[1], 1)
        got_left0 = over_y(left[0], -1)
        from_left, from_right, *pieces = tie(from_left, from_right, *pieces)
        right0 = (right[0].astype(f32) + from_left.astype(f32)).astype(bf16)
        left1 = (left[1].astype(f32) + from_right.astype(f32)).astype(bf16)
        got_right0 = over_y(right0, 1)
        got_left1 = over_y(left1, -1)
        own = dot_for(0, f32)
        got_right1, got_left0, hidden_left, hidden_right = tie(
            got_right1, got_left0, hidden_left, hidden_right
        )
        other_sum = own[1] + got_right1.astype(f32) + got_left1.astype(f32)
        from_zl = over_zl(other_sum.astype(bf16))
        at = (y % 2) * NZL + zl
        pieces = jnp.stack(pieces)
        resid_strips = jnp.concatenate(
            [lax.dynamic_slice_in_dim(pieces, (at - b) % NY, 1, 0) for b in range(NX)], axis=0
        )
        layer = (
            own[0]
            + resid_strips.astype(f32)
            + got_right0.astype(f32)
            + got_left0.astype(f32)
            + from_zl.astype(f32)
        )

    with jax.named_scope("hidden_exchange"):
        hidden_far = (
            over_x(hidden_left[: tokens // 2], 1),
            over_x(hidden_right[tokens // 2 :], -1),
        )
        hidden_rows = jnp.concatenate((hidden, hidden_left, hidden_right) + hidden_far, axis=0)

    with jax.named_scope("strip_exchange"):
        low_layer = layer.astype(bf16)
        strips_x = [lax.dynamic_slice_in_dim(low_layer, x, 1, 0)]
        for step in (1, -1, 2):
            strip = lax.dynamic_slice_in_dim(low_layer, (x + step) % NX, 1, 0)
            strips_x.append(over_x(strip, step))
        got = gather_start(jnp.concatenate(strips_x, axis=0))

    with jax.named_scope("norm"):
        squares = jnp.sum(layer * layer, axis=(0, 2)).reshape(seqs_here, SEQ)
        squares = jnp.sum(gather_small(squares, "tensor"), axis=0)
        inverse = lax.rsqrt(squares / model_width + eps_norm)
        weighted = layer.reshape(NX, seqs_here, SEQ, lanes) * inverse[None, :, :, None]
        means = jnp.mean(weighted, axis=2).transpose(1, 0, 2).reshape(seqs_here, width)

    with jax.named_scope("contrast"):
        means_all = gather_small(means, "dp")
        keys = list(got)
        means_all, hidden_rows, *values = tie(means_all, hidden_rows, *got.values())
        got = gather_next(dict(zip(keys, values)))
        means_all = means_all.reshape(seqs, width)
        parts = gather_small(gram_part(means_all, gain_own, x), "tensor")
        keys = list(got)
        parts, *values = tie(parts, *got.values())
        strips = gather_end(dict(zip(keys, values)), zl, y)
        scaled, scaled_own, gain_grad = contrast(parts, same, gain_blocks, means_all, gain_own, x)

    with jax.named_scope("along"):
        part = jnp.concatenate([along_part(strips, scaled, plan), inverse[None]], axis=0)
        parts_x = [part] + [over_x(part, step) for step in (1, -1, 2)]

    with jax.named_scope("down_grad"):
        low_x, coef = group_grad(strips, scaled, parts_x, plan)

        def down(low):
            return lax.dot_general(
                hidden_rows, low, (((0,), (0,)), ((), ())), preferred_element_type=f32
            )

        from_core = over_core(down(low_x[3]))
        summed = (down(low_x[2]) + from_core).astype(bf16)

    with jax.named_scope("layer_grad"):
        own_rows = lax.dynamic_slice_in_dim(scaled_own, shard * seqs_here, seqs_here, 0)
        own_rows = own_rows.reshape(seqs_here, NX, lanes).transpose(1, 0, 2)
        low_own = (
            inverse[None, :, :, None] * own_rows[:, :, None, :]
            - layer.reshape(NX, seqs_here, SEQ, lanes) * coef[None, :, :, None]
        ).astype(bf16)
        got = gather_start(low_own.reshape(NX, tokens, lanes))
        keys = list(got)
        summed, low0, low1, *values = tie(summed, low_x[0], low_x[1], *got.values())
        low_rows = gather_end(gather_next(dict(zip(keys, values))), zl, y)
        grad_resid = lax.dynamic_slice(
            low_rows, ((rank % 2) * 4, rank // 2, 0, 0), (4, 1, tokens, lanes)
        )
        grad_resid = grad_resid[:, 0].transpose(1, 0, 2).reshape(tokens, width)
        places = [(p % NZL) * NY + p // NZL for p in range(group)]
        gain_grad = gather_small(gain_grad.reshape(NX, lanes), "tensor")
        gain_grad = jnp.stack([gain_grad[p] for p in places])
        grad_gain = lax.dynamic_slice(
            gain_grad, ((rank % 2) * 4, rank // 2, 0), (4, 1, lanes)
        ).reshape(width)

    with jax.named_scope("down_grad"):
        across = over_zh(summed)
        near = down(low0) + over_core(down(low1))
        near, across = tie(near, across)
        grad_down = near + across.astype(f32)

    with jax.named_scope("hidden_grad"):
        grad_hidden = hidden_grad(low_rows, down_weight)

    return (grad_hidden, grad_resid, grad_down, grad_gain)


def solution(mesh):
    return jax.shard_map(
        per_device,
        mesh=mesh,
        in_specs=(P("dp", "tensor"), P("dp", "tensor"), P("tensor", None), P(), P()),
        out_specs=(P("dp", "tensor"), P("dp", "tensor"), P("tensor", "dp"), P("tensor")),
        check_vma=False,
    )
```

```python
import functools
import jax
import jax.numpy as jnp
from jax import lax
from jax.experimental import pallas as pl
from jax.experimental.pallas import tpu as pltpu
from jax.sharding import PartitionSpec as P

SEQ = 128
NX, NZH, NCORE, NZL, NY = 4, 2, 2, 2, 4
GRAD_STEPS = 7
KEYS = ((0, 0), (1, 0), (0, 1), (0, 3), (0, 2), (1, 1), (1, 3), (1, 2))

score_scale = 20.0
loss_scale = 8192.0
eps_norm = 1e-05
eps_embed = 1e-06
highest = lax.Precision.HIGHEST
f32 = jnp.float32
bf16 = jnp.bfloat16
MIB = 1024 * 1024
QUICK = pl.CostEstimate(flops=1024, bytes_accessed=1024, transcendentals=0)


def dp_route(dx, dz, dc):
    pairs = []
    for x in range(NX):
        for z in range(NZH):
            for c in range(NCORE):
                to = (((x + dx) % NX) * NZH + (z + dz) % NZH) * NCORE + (c + dc) % NCORE
                pairs.append(((x * NZH + z) * NCORE + c, to))
    return pairs


def tensor_route(dz, dy):
    pairs = []
    for z in range(NZL):
        for y in range(NY):
            pairs.append((z * NY + y, ((z + dz) % NZL) * NY + (y + dy) % NY))
    return pairs


def swap_route(bit):
    size = NZH * NCORE
    return [(d, (d // size ^ bit) * size + d % size) for d in range(NX * size)]


def over_x(value, step):
    return lax.ppermute(value, "dp", dp_route(step, 0, 0))


def over_zh(value):
    return lax.ppermute(value, "dp", dp_route(0, 1, 0))


def over_core(value):
    return lax.ppermute(value, "dp", dp_route(0, 0, 1))


def over_y(value, step):
    return lax.ppermute(value, "tensor", tensor_route(0, step))


def over_zl(value):
    return lax.ppermute(value, "tensor", tensor_route(1, 0))


def gather_small(value, axis):
    n = lax.axis_size(axis)
    copies = jnp.broadcast_to(value[None], (n,) + value.shape)
    return lax.all_to_all(copies, axis, 0, 0)


def layer_dot_kernel(plan_ref, hidden_ref, weight_ref, *refs):
    *out_refs, total_ref = refs
    tile = 512

    @pl.when(pl.program_id(0) == 0)
    def _():
        for n in range(0, total_ref.shape[1], tile):
            total_ref[:, n : n + tile] = jnp.dot(
                hidden_ref[...], weight_ref[:, n : n + tile], preferred_element_type=f32
            )

    @pl.when(pl.program_id(0) == 1)
    def _():
        lanes = out_refs[0].shape[-1]
        flip = plan_ref[0] == 1
        for c, ref in enumerate(out_refs):
            for b in range(NX):
                start = pl.multiple_of((b * NY + plan_ref[1 + c]) * 2 * lanes, 2 * lanes)
                columns = pl.ds(start, 2 * lanes)
                pair = total_ref[:, columns] + jnp.dot(
                    hidden_ref[...], weight_ref[:, columns], preferred_element_type=f32
                )
                first, second = pair[:, :lanes], pair[:, lanes:]
                ref[0, b] = jnp.where(flip, second, first).astype(ref.dtype)
                ref[1, b] = jnp.where(flip, first, second).astype(ref.dtype)


def layer_dot(hidden, weight, columns, zl, group, dtypes):
    tokens, units = hidden.shape
    model_width = weight.shape[1]
    lanes = model_width // (NX * group)
    depth = units // 2
    out = pl.BlockSpec((2, NX, tokens, lanes), lambda k, s: (0, 0, 0, 0))
    return pl.pallas_call(
        layer_dot_kernel,
        grid_spec=pltpu.PrefetchScalarGridSpec(
            num_scalar_prefetch=1,
            grid=(2,),
            in_specs=[
                pl.BlockSpec((tokens, depth), lambda k, s: (0, k)),
                pl.BlockSpec((depth, model_width), lambda k, s: (k, 0)),
            ],
            out_specs=[out] * len(columns),
            scratch_shapes=[pltpu.VMEM((tokens, model_width), f32)],
        ),
        out_shape=[jax.ShapeDtypeStruct((2, NX, tokens, lanes), dtype) for dtype in dtypes],
        compiler_params=pltpu.CompilerParams(vmem_limit_bytes=56 * MIB),
        cost_estimate=pl.CostEstimate(
            flops=2 * tokens * units * model_width,
            bytes_accessed=2 * (tokens * units + units * model_width + tokens * model_width),
            transcendentals=0,
        ),
    )(jnp.stack([zl] + columns).astype(jnp.int32), hidden, weight)


def gram_kernel(plan_ref, mean_ref, gain_ref, strip_ref, out_ref):
    pooled = mean_ref[...] * gain_ref[...]
    gram = lax.dot_general(
        pooled, pooled, (((1,), (1,)), ((), ())), precision=highest, preferred_element_type=f32
    )
    out_ref[0] = jnp.concatenate([gram, jnp.zeros_like(gram)], axis=1)
    out_ref[1] = strip_ref[...]


def gram_part(means, gain, x):
    seqs, width = means.shape
    lanes = 2 * seqs
    return pl.pallas_call(
        gram_kernel,
        grid_spec=pltpu.PrefetchScalarGridSpec(
            num_scalar_prefetch=1,
            grid=(1,),
            in_specs=[
                pl.BlockSpec((seqs, width), lambda i, s: (0, 0)),
                pl.BlockSpec((1, width), lambda i, s: (0, 0)),
                pl.BlockSpec((seqs, lanes), lambda i, s: (0, s[0])),
            ],
            out_specs=pl.BlockSpec((2, seqs, lanes), lambda i, s: (0, 0, 0)),
        ),
        out_shape=jax.ShapeDtypeStruct((2, seqs, lanes), f32),
        compiler_params=pltpu.CompilerParams(vmem_limit_bytes=16 * MIB),
        cost_estimate=QUICK,
    )(x.astype(jnp.int32).reshape(1), means, gain, means)


def contrast_kernel(
    plan_ref, part_ref, same_ref, gain_block_ref, mean_ref, gain_ref, block_ref, block_gain_ref, own_ref, gain_grad_ref
):
    group = part_ref.shape[0]
    seqs = mean_ref.shape[0]
    rows = lax.broadcasted_iota(jnp.int32, (seqs, seqs), 0)
    cols = lax.broadcasted_iota(jnp.int32, (seqs, seqs), 1)
    gram = part_ref[0, 0]
    for r in range(1, group):
        gram += part_ref[r, 0]
    gram = gram[:, :seqs]
    diagonal = jnp.where(rows == cols, gram, 0.0)
    norm_col = jnp.sqrt(jnp.sum(diagonal, axis=1, keepdims=True) + eps_embed)
    norm_row = jnp.sqrt(jnp.sum(diagonal, axis=0, keepdims=True) + eps_embed)
    norms = norm_col * norm_row
    scores = score_scale * gram / norms
    query = rows % 2 == 0
    valid = query & (cols % 2 == 1) & (same_ref[...] > 0.5)
    weights = jnp.where(valid, jnp.exp(scores), 0.0)
    totals = jnp.sum(weights, axis=1, keepdims=True)
    soft = weights / jnp.where(totals > 0.0, totals, 1.0)
    target = jnp.where(query & (cols == rows + 1), 1.0, 0.0)
    d_score = loss_scale * (soft - target)
    both = d_score + d_score.T
    coef = jnp.sum(both * scores, axis=1, keepdims=True)
    mix = score_scale * both / norms - jnp.where(rows == cols, coef / (norm_col * norm_col), 0.0)
    mean, gain = mean_ref[...], gain_ref[...]
    d_pooled = jnp.dot(mix, mean * gain, precision=highest, preferred_element_type=f32)
    gain_grad_ref[...] = jnp.sum(d_pooled * mean, axis=0, keepdims=True)
    own_ref[...] = d_pooled * gain * (1.0 / SEQ)
    for place in range(group):
        part = part_ref[(place % NZL) * NY + place // NZL, 1]
        gain = gain_block_ref[0, place : place + 1, :]
        d_pooled = jnp.dot(mix, part * gain, precision=highest, preferred_element_type=f32)
        block_ref[place] = d_pooled * gain * (1.0 / SEQ)
        block_gain_ref[place : place + 1, :] = jnp.sum(d_pooled * part, axis=0, keepdims=True)


def contrast(parts, same, gain_blocks, means, gain, x):
    group, _, seqs, lanes = parts.shape
    width = means.shape[1]
    whole = lambda shape: pl.BlockSpec(shape, lambda i, s: (0,) * len(shape))
    return pl.pallas_call(
        contrast_kernel,
        grid_spec=pltpu.PrefetchScalarGridSpec(
            num_scalar_prefetch=1,
            grid=(1,),
            in_specs=[
                whole(parts.shape),
                whole(same.shape),
                pl.BlockSpec((1, group, lanes), lambda i, s: (s[0], 0, 0)),
                whole(means.shape),
                whole(gain.shape),
            ],
            out_specs=[whole((group, seqs, lanes)), whole((group, lanes)), whole((seqs, width)), whole((1, width))],
        ),
        out_shape=(
            jax.ShapeDtypeStruct((group, seqs, lanes), f32),
            jax.ShapeDtypeStruct((group, lanes), f32),
            jax.ShapeDtypeStruct((seqs, width), f32),
            jax.ShapeDtypeStruct((1, width), f32),
        ),
        compiler_params=pltpu.CompilerParams(vmem_limit_bytes=16 * MIB),
        cost_estimate=QUICK,
    )(x.astype(jnp.int32).reshape(1), parts, same, gain_blocks, means, gain)


def row_to_column(row):
    n = row.shape[1]
    eye = lax.broadcasted_iota(jnp.int32, (n, n), 0) == lax.broadcasted_iota(jnp.int32, (n, n), 1)
    return jnp.sum(jnp.where(eye, jnp.broadcast_to(row, (n, n)), 0.0), axis=1, keepdims=True)


def column_to_row(column):
    n = column.shape[0]
    eye = lax.broadcasted_iota(jnp.int32, (n, n), 0) == lax.broadcasted_iota(jnp.int32, (n, n), 1)
    return jnp.sum(jnp.where(eye, jnp.broadcast_to(column, (n, n)), 0.0), axis=0, keepdims=True)


def along_kernel(plan_ref, *refs):
    *layer_refs, scaled_ref, out_ref = refs
    tokens = layer_refs[0].shape[1]
    first = plan_ref[pl.program_id(0)]
    for s in range(tokens // SEQ):
        rows = slice(s * SEQ, (s + 1) * SEQ)
        along = None
        for i, ref in enumerate(layer_refs):
            scaled = scaled_ref[plan_ref[NX + i], pl.ds(first + s, 1), :]
            term = ref[0, rows, :].astype(f32) * scaled
            along = term if along is None else along + term
        out_ref[0, s : s + 1, :] = column_to_row(jnp.sum(along, axis=1, keepdims=True))


def along_part(strips, scaled, plan):
    _, tokens, lanes = strips[0].shape
    group = len(strips)
    seqs_here = tokens // SEQ
    return pl.pallas_call(
        along_kernel,
        grid_spec=pltpu.PrefetchScalarGridSpec(
            num_scalar_prefetch=1,
            grid=(NX,),
            in_specs=[pl.BlockSpec((1, tokens, lanes), lambda i, s: (i, 0, 0))] * group
            + [pl.BlockSpec(scaled.shape, lambda i, s: (0, 0, 0))],
            out_specs=pl.BlockSpec((1, seqs_here, SEQ), lambda i, s: (s[NX + 3 * group + i], 0, 0)),
        ),
        out_shape=jax.ShapeDtypeStruct((NX, seqs_here, SEQ), f32),
        compiler_params=pltpu.CompilerParams(vmem_limit_bytes=16 * MIB),
        cost_estimate=QUICK,
    )(plan, *strips, scaled)


def group_grad_kernel(plan_ref, *refs):
    *layer_refs, scaled_ref, sum_ref, low_ref, coef_ref, factor_ref = refs
    _, tokens, lanes = layer_refs[0].shape
    group = len(layer_refs)
    seqs_here = tokens // SEQ
    here = pl.program_id(0)
    first = plan_ref[here]

    @pl.when(here == 0)
    def _():
        for i in range(NX):
            position = plan_ref[NX + 3 * group + i]
            along, inverse = sum_ref[position], sum_ref[NX + position]
            coef = inverse * inverse * inverse * along / (NX * group * lanes)
            factor_ref[i, :seqs_here] = inverse
            factor_ref[i, seqs_here:] = coef
            if i == 0:
                coef_ref[...] = coef

    for s in range(seqs_here):
        rows = slice(s * SEQ, (s + 1) * SEQ)
        inverse = row_to_column(factor_ref[here, s : s + 1, :])
        coef = row_to_column(factor_ref[here, seqs_here + s : seqs_here + s + 1, :])
        for i, ref in enumerate(layer_refs):
            scaled = scaled_ref[plan_ref[NX + i], pl.ds(first + s, 1), :]
            low = inverse * scaled - ref[0, rows, :].astype(f32) * coef
            side = pl.ds(pl.multiple_of(plan_ref[NX + 2 * group + i], lanes), lanes)
            low_ref[plan_ref[NX + group + i], rows, side] = low.astype(bf16)


def group_grad(strips, scaled, sums, plan):
    _, tokens, lanes = strips[0].shape
    group = len(strips)
    quarter = group * lanes // 4
    seqs_here = tokens // SEQ
    return pl.pallas_call(
        group_grad_kernel,
        grid_spec=pltpu.PrefetchScalarGridSpec(
            num_scalar_prefetch=1,
            grid=(NX,),
            in_specs=[pl.BlockSpec((1, tokens, lanes), lambda i, s: (i, 0, 0))] * group
            + [pl.BlockSpec(scaled.shape, lambda i, s: (0, 0, 0))]
            + [pl.BlockSpec(sums.shape, lambda i, s: (0, 0, 0))],
            out_specs=[
                pl.BlockSpec((4, tokens, quarter), lambda i, s: (0, i, 0)),
                pl.BlockSpec((seqs_here, SEQ), lambda i, s: (0, 0)),
            ],
            scratch_shapes=[pltpu.VMEM((NX, 2 * seqs_here, SEQ), f32)],
        ),
        out_shape=(
            jax.ShapeDtypeStruct((4, NX * tokens, quarter), bf16),
            jax.ShapeDtypeStruct((seqs_here, SEQ), f32),
        ),
        compiler_params=pltpu.CompilerParams(vmem_limit_bytes=24 * MIB),
        cost_estimate=QUICK,
    )(plan, *strips, scaled, sums)


def hidden_grad_kernel(plan_ref, *refs):
    *refs, scaled_ref, block_gain_ref, inverse_ref, coef_ref, weight_ref, out_ref, resid_ref, gain_ref, low_ref = refs
    tokens = out_ref.shape[0]
    seqs_here = tokens // SEQ
    group = len(refs) // 2
    others, _, lanes = refs[0].shape
    width = resid_ref.shape[1]
    x, first = plan_ref[1], plan_ref[2]

    @pl.when(pl.program_id(0) == 0)
    def _():
        factors = [
            [jnp.broadcast_to(row_to_column(ref[s : s + 1, :]), (SEQ, lanes)) for ref in (inverse_ref, coef_ref)]
            for s in range(seqs_here)
        ]
        for i in range(group):
            place = plan_ref[3 + i]
            row_ref, strip_ref = refs[i], refs[group + i]
            for j in range(others + 1):
                block = lax.rem(x + j, others + 1)
                column = pl.ds(pl.multiple_of((block * group + place) * lanes, lanes), lanes)
                if j:
                    tail = row_ref[j - 1, tokens:, :].astype(f32)
                    tail = tail[:8] + tail[8:]
                    gain_ref[place, pl.ds(block, 1), :] = tail[seqs_here : seqs_here + 1]
                else:
                    gain_ref[place, pl.ds(block, 1), :] = block_gain_ref[pl.ds(place, 1), :]
                for s in range(seqs_here):
                    rows = slice(s * SEQ, (s + 1) * SEQ)
                    if j:
                        layer, scaled = row_ref[j - 1, rows, :], tail[s : s + 1]
                    else:
                        layer, scaled = strip_ref[0, rows, :], scaled_ref[place, pl.ds(first + s, 1), :]
                    inverse, coef = factors[s]
                    low_ref[rows, column] = (inverse * scaled - layer.astype(f32) * coef).astype(bf16)
        resid_ref[...] = low_ref[:, pl.ds(pl.multiple_of(plan_ref[0] * width, width), width)]

    out_ref[...] = lax.dot_general(
        low_ref[...], weight_ref[...], (((1,), (1,)), ((), ())), preferred_element_type=f32
    ).astype(out_ref.dtype)


def hidden_grad(rows, strips, scaled, block_gain, inverse, coef, weight, plan):
    others, height, lanes = rows[0].shape
    group = len(rows)
    seqs_here = inverse.shape[0]
    tokens = seqs_here * SEQ
    units, model_width = weight.shape
    chunk = units // GRAD_STEPS
    width = model_width // group
    whole = lambda shape: pl.BlockSpec(shape, lambda i, s: (0,) * len(shape))
    return pl.pallas_call(
        hidden_grad_kernel,
        grid_spec=pltpu.PrefetchScalarGridSpec(
            num_scalar_prefetch=1,
            grid=(GRAD_STEPS,),
            in_specs=[whole(rows[0].shape)] * group
            + [whole((1, tokens, lanes))] * group
            + [whole(v.shape) for v in (scaled, block_gain, inverse, coef)]
            + [pl.BlockSpec((chunk, model_width), lambda i, s: (i, 0))],
            out_specs=[
                pl.BlockSpec((tokens, chunk), lambda i, s: (0, i)),
                whole((tokens, width)),
                whole((group, others + 1, lanes)),
            ],
            scratch_shapes=[pltpu.VMEM((tokens, model_width), bf16)],
        ),
        out_shape=(
            jax.ShapeDtypeStruct((tokens, units), bf16),
            jax.ShapeDtypeStruct((tokens, width), bf16),
            jax.ShapeDtypeStruct((group, others + 1, lanes), f32),
        ),
        compiler_params=pltpu.CompilerParams(vmem_limit_bytes=56 * MIB),
        cost_estimate=QUICK,
    )(jnp.stack(plan).astype(jnp.int32), *rows, *strips, scaled, block_gain, inverse, coef, weight)


def tie(*values):
    return lax.optimization_barrier(values)


def gather_start(value):
    return {
        (0, 0): value,
        (1, 0): over_zl(value),
        (0, 1): over_y(value, -1),
        (0, 3): over_y(value, 1),
    }


def gather_next(got):
    got = dict(got)
    got[1, 1] = over_y(got[1, 0], -1)
    got[1, 3] = over_zl(got[0, 3])
    got[0, 2] = over_y(got[0, 3], 1)
    return got


def gather_last(got):
    got = dict(got)
    got[1, 2] = over_y(got[1, 1], -1)
    return got


def tie_gather(got, *values):
    keys = list(got)
    tied = tie(*got.values(), *values)
    return (dict(zip(keys, tied)),) + tuple(tied[len(keys) :])


def per_device(resid, hidden, down_weight, gain, domain_ids):
    tokens, units = hidden.shape
    model_width = down_weight.shape[1]
    group = lax.axis_size("tensor")
    shards = lax.axis_size("dp")
    width = model_width // group
    lanes = width // NX
    seqs_here = tokens // SEQ
    seqs = seqs_here * shards
    rank = lax.axis_index("tensor")
    zl, y = rank // NY, rank % NY
    place = y * NZL + zl
    shard = lax.axis_index("dp")
    x, zh, core = shard // (NZH * NCORE), (shard // NCORE) % NZH, shard % NCORE

    def place_of(part, step):
        return ((y + step) % NY) * NZL + (zl + part) % NZL

    with jax.named_scope("tables"):
        owner = jnp.repeat(domain_ids, seqs_here)
        same = (owner[:, None] == owner[None, :]).astype(f32)
        gain_blocks = gain.reshape(NX, group, lanes)
        gain_own = lax.dynamic_slice_in_dim(gain_blocks, place, 1, 1).reshape(1, width)
        peers = [((x + step) % NX) * (NZH * NCORE) + zh * NCORE + core for step in (0, -1, 1, 2)]
        places = [place_of(*key) for key in KEYS]
        plan = [p * seqs_here for p in peers] + places
        plan += [(p // 2) ^ (zh * NCORE + core) for p in places] + [p % 2 * lanes for p in places]
        plan += [(x + step) % NX for step in (0, -1, 1, 2)]
        plan = jnp.stack([jnp.asarray(v, jnp.int32) for v in plan])

    with jax.named_scope("hidden_exchange"):
        hidden_left = over_x(hidden, 1)
        hidden_right = over_x(hidden, -1)

    with jax.named_scope("resid_exchange"):
        pieces = resid.reshape(tokens, 2, NZL, lanes).transpose(2, 1, 0, 3)[:, None]
        pieces = jnp.broadcast_to(pieces, (NZL, NY // 2, 2, tokens, lanes))
        pieces = lax.all_to_all(pieces.reshape(group, tokens, lanes), "tensor", 0, 0)
        pieces = pieces.reshape(NX, 2, tokens, lanes)

    with jax.named_scope("layer_sum"):
        columns = [(y + step) % NY for step in (2, 1, 3, 0)]
        sums = layer_dot(hidden, down_weight, columns, zl, group, (bf16, bf16, bf16, f32))
        far, right, left, own, pieces = tie(*sums, pieces)
        from_left = over_y(far[0], 1)
        from_right = over_y(far[1], -1)
        from_left, from_right = tie(from_left, from_right)
        right0 = (right[0].astype(f32) + from_left.astype(f32)).astype(bf16)
        left1 = (left[1].astype(f32) + from_right.astype(f32)).astype(bf16)
        got_right = over_y(lax.dynamic_update_slice(right, right0[None], (0, 0, 0, 0)), 1)
        got_left = over_y(lax.dynamic_update_slice(left, left1[None], (1, 0, 0, 0)), -1)

    with jax.named_scope("hidden_exchange"):
        hidden_left, hidden_right, right0 = tie(hidden_left, hidden_right, right0)
        hidden_far = (
            over_x(hidden_left[: tokens // 2], 1),
            over_x(hidden_right[tokens // 2 :], -1),
        )
        got_right, got_left, *hidden_far = tie(got_right, got_left, *hidden_far)
        hidden_rows = jnp.concatenate([hidden, hidden_left, hidden_right] + hidden_far, axis=0)

    with jax.named_scope("layer_sum"):
        other_sum = own[1] + got_right[1].astype(f32) + got_left[1].astype(f32)
        from_zl = over_zl(other_sum.astype(bf16))
        from_zl, hidden_rows = tie(from_zl, hidden_rows)
        resid_strips = lax.dynamic_slice_in_dim(pieces, y // 2, 1, 1)[:, 0]
        layer = (
            own[0]
            + resid_strips.astype(f32)
            + got_right[0].astype(f32)
            + got_left[0].astype(f32)
            + from_zl.astype(f32)
        )

    with jax.named_scope("strip_exchange"):
        low_layer = layer.astype(bf16)
        strips_x = [lax.dynamic_slice_in_dim(low_layer, x, 1, 0)]
        for step in (1, -1, 2):
            strip = lax.dynamic_slice_in_dim(low_layer, (x + step) % NX, 1, 0)
            strips_x.append(over_x(strip, step))
        message = jnp.concatenate(strips_x, axis=0)

    with jax.named_scope("norm"):
        squares = jnp.sum(layer * layer, axis=(0, 2)).reshape(seqs_here, SEQ)
        squares = jnp.sum(gather_small(squares, "tensor"), axis=0)
        message, squares = tie(message, squares)
        got = gather_start(message)
        inverse = lax.rsqrt(squares / model_width + eps_norm)
        weighted = layer.reshape(NX, seqs_here, SEQ, lanes) * inverse[None, :, :, None]
        means = jnp.mean(weighted, axis=2).transpose(1, 0, 2).reshape(seqs_here, width)

    with jax.named_scope("contrast"):
        means_all = gather_small(means, "dp")
        got, means_all = tie_gather(got, means_all)
        got = gather_next(got)
        means_all = means_all.reshape(seqs, width)
        parts = gather_small(gram_part(means_all, gain_own, x), "tensor")
        got, parts, low_layer = tie_gather(got, parts, low_layer)
        got = gather_last(got)
        strips = [got[key] for key in KEYS]
        scaled, gain_grad_x, scaled_own, gain_grad = contrast(
            parts, same, gain_blocks, means_all, gain_own, x
        )

    with jax.named_scope("row_gather"):
        own_rows = lax.dynamic_slice_in_dim(scaled_own, shard * seqs_here, seqs_here, 0)
        own_rows = jnp.pad(jnp.concatenate([own_rows, gain_grad], axis=0), ((0, 8 - seqs_here - 1), (0, 0)))
        high = own_rows.astype(bf16)
        tail = jnp.concatenate([high, (own_rows - high.astype(f32)).astype(bf16)], axis=0)
        tail = tail.reshape(16, NX, lanes).transpose(1, 0, 2)
        blocks = jnp.concatenate([low_layer, tail], axis=1)
        blocks = jnp.concatenate([blocks, blocks], axis=0)
        rows = gather_start(lax.dynamic_slice_in_dim(blocks, x + 1, NX - 1, 0))

    with jax.named_scope("along"):
        own_inverse = jnp.where(jnp.arange(NX)[:, None, None] == x, inverse[None], 0.0)
        sums = jnp.concatenate([along_part(strips, scaled, plan), own_inverse], axis=0)
        sums = sums + lax.ppermute(sums, "dp", swap_route(1))
        sums = sums + lax.ppermute(sums, "dp", swap_route(2))
        rows, sums = tie_gather(rows, sums)
        rows = gather_next(rows)

    with jax.named_scope("down_grad"):
        low_x, coef = group_grad(strips, scaled, sums, plan)

        def down(low):
            return lax.dot_general(
                hidden_rows, low, (((0,), (0,)), ((), ())), preferred_element_type=f32
            )

        from_core = over_core(down(low_x[3]))
        summed = (down(low_x[2]) + from_core).astype(bf16)
        rows, summed, low0, low1 = tie_gather(rows, summed, low_x[0], low_x[1])
        rows = gather_last(rows)
        across = over_zh(summed)
        near = down(low0) + over_core(down(low1))

    with jax.named_scope("hidden_grad"):
        rows, near = tie_gather(rows, near)
        rows = [rows[key] for key in KEYS]
        grad_hidden, grad_resid, gain_grad = hidden_grad(
            rows, strips, scaled, gain_grad_x, inverse, coef, down_weight, [rank, x, shard * seqs_here] + places
        )
        grad_gain = lax.dynamic_slice(
            gain_grad, ((rank % 2) * 4, rank // 2, 0), (4, 1, lanes)
        ).reshape(width)

    with jax.named_scope("down_grad"):
        grad_down = near + across.astype(f32)

    return (grad_hidden, grad_resid, grad_down, grad_gain)


def solution(mesh):
    return jax.shard_map(
        per_device,
        mesh=mesh,
        in_specs=(P("dp", "tensor"), P("dp", "tensor"), P("tensor", None), P(), P()),
        out_specs=(P("dp", "tensor"), P("dp", "tensor"), P("tensor", "dp"), P("tensor")),
        check_vma=False,
    )
```

```python
import functools
import jax
import jax.numpy as jnp
from jax import lax
from jax.experimental import pallas as pl
from jax.experimental.pallas import tpu as pltpu
from jax.sharding import PartitionSpec as P

SEQ = 128
NX, NZH, NCORE, NZL, NY = 4, 2, 2, 2, 4
GRAD_STEPS = 7
KEYS = ((0, 0), (1, 0), (0, 1), (0, 3), (0, 2), (1, 1), (1, 3), (1, 2))

score_scale = 20.0
loss_scale = 8192.0
eps_norm = 1e-05
eps_embed = 1e-06
highest = lax.Precision.HIGHEST
f32 = jnp.float32
bf16 = jnp.bfloat16
MIB = 1024 * 1024
QUICK = pl.CostEstimate(flops=1024, bytes_accessed=1024, transcendentals=0)


def dp_route(dx, dz, dc):
    pairs = []
    for x in range(NX):
        for z in range(NZH):
            for c in range(NCORE):
                to = (((x + dx) % NX) * NZH + (z + dz) % NZH) * NCORE + (c + dc) % NCORE
                pairs.append(((x * NZH + z) * NCORE + c, to))
    return pairs


def tensor_route(dz, dy):
    pairs = []
    for z in range(NZL):
        for y in range(NY):
            pairs.append((z * NY + y, ((z + dz) % NZL) * NY + (y + dy) % NY))
    return pairs


def swap_route(bit):
    size = NZH * NCORE
    return [(d, (d // size ^ bit) * size + d % size) for d in range(NX * size)]


def over_x(value, step):
    return lax.ppermute(value, "dp", dp_route(step, 0, 0))


def over_zh(value):
    return lax.ppermute(value, "dp", dp_route(0, 1, 0))


def over_core(value):
    return lax.ppermute(value, "dp", dp_route(0, 0, 1))


def over_y(value, step):
    return lax.ppermute(value, "tensor", tensor_route(0, step))


def over_zl(value):
    return lax.ppermute(value, "tensor", tensor_route(1, 0))


def gather_small(value, axis):
    n = lax.axis_size(axis)
    copies = jnp.broadcast_to(value[None], (n,) + value.shape)
    return lax.all_to_all(copies, axis, 0, 0)


def layer_dot_kernel(plan_ref, hidden_ref, weight_ref, *refs):
    *out_refs, total_ref = refs
    lanes = out_refs[0].shape[-1]
    flip = plan_ref[0] == 1
    total_ref[...] = jnp.dot(hidden_ref[...], weight_ref[...], preferred_element_type=f32)
    for c in range(len(out_refs) // 2):
        same_ref, other_ref = out_refs[2 * c : 2 * c + 2]
        start = pl.multiple_of(plan_ref[1 + c] * 2 * lanes, 2 * lanes)
        pair = total_ref[:, pl.ds(start, 2 * lanes)]
        first, second = pair[:, :lanes], pair[:, lanes:]
        same_ref[0] = jnp.where(flip, second, first).astype(same_ref.dtype)
        other_ref[0] = jnp.where(flip, first, second).astype(other_ref.dtype)


def layer_dot(hidden, weight, columns, zl, group, dtypes):
    tokens, units = hidden.shape
    model_width = weight.shape[1]
    lanes = model_width // (NX * group)
    out = pl.BlockSpec((1, tokens, lanes), lambda b, s: (b, 0, 0))
    return pl.pallas_call(
        layer_dot_kernel,
        grid_spec=pltpu.PrefetchScalarGridSpec(
            num_scalar_prefetch=1,
            grid=(NX,),
            in_specs=[
                pl.BlockSpec((tokens, units), lambda b, s: (0, 0)),
                pl.BlockSpec((units, group * lanes), lambda b, s: (0, b)),
            ],
            out_specs=[out] * (2 * len(columns)),
            scratch_shapes=[pltpu.VMEM((tokens, group * lanes), f32)],
        ),
        out_shape=[
            jax.ShapeDtypeStruct((NX, tokens, lanes), dtype) for dtype in dtypes for _ in range(2)
        ],
        compiler_params=pltpu.CompilerParams(vmem_limit_bytes=56 * MIB),
        cost_estimate=pl.CostEstimate(
            flops=2 * tokens * units * model_width,
            bytes_accessed=2 * (tokens * units + units * model_width + tokens * model_width),
            transcendentals=0,
        ),
    )(jnp.stack([zl] + columns).astype(jnp.int32), hidden, weight)


def gram_kernel(plan_ref, mean_ref, gain_ref, strip_ref, out_ref):
    pooled = mean_ref[...] * gain_ref[...]
    gram = lax.dot_general(
        pooled, pooled, (((1,), (1,)), ((), ())), precision=highest, preferred_element_type=f32
    )
    out_ref[0] = jnp.concatenate([gram, jnp.zeros_like(gram)], axis=1)
    out_ref[1] = strip_ref[...]


def gram_part(means, gain, x):
    seqs, width = means.shape
    lanes = 2 * seqs
    return pl.pallas_call(
        gram_kernel,
        grid_spec=pltpu.PrefetchScalarGridSpec(
            num_scalar_prefetch=1,
            grid=(1,),
            in_specs=[
                pl.BlockSpec((seqs, width), lambda i, s: (0, 0)),
                pl.BlockSpec((1, width), lambda i, s: (0, 0)),
                pl.BlockSpec((seqs, lanes), lambda i, s: (0, s[0])),
            ],
            out_specs=pl.BlockSpec((2, seqs, lanes), lambda i, s: (0, 0, 0)),
        ),
        out_shape=jax.ShapeDtypeStruct((2, seqs, lanes), f32),
        compiler_params=pltpu.CompilerParams(vmem_limit_bytes=16 * MIB),
        cost_estimate=QUICK,
    )(x.astype(jnp.int32).reshape(1), means, gain, means)


def contrast_kernel(
    plan_ref, part_ref, same_ref, gain_block_ref, mean_ref, gain_ref, block_ref, block_gain_ref, own_ref, gain_grad_ref
):
    group = part_ref.shape[0]
    seqs = mean_ref.shape[0]
    rows = lax.broadcasted_iota(jnp.int32, (seqs, seqs), 0)
    cols = lax.broadcasted_iota(jnp.int32, (seqs, seqs), 1)
    gram = part_ref[0, 0]
    for r in range(1, group):
        gram += part_ref[r, 0]
    gram = gram[:, :seqs]
    diagonal = jnp.where(rows == cols, gram, 0.0)
    norm_col = jnp.sqrt(jnp.sum(diagonal, axis=1, keepdims=True) + eps_embed)
    norm_row = jnp.sqrt(jnp.sum(diagonal, axis=0, keepdims=True) + eps_embed)
    norms = norm_col * norm_row
    scores = score_scale * gram / norms
    query = rows % 2 == 0
    valid = query & (cols % 2 == 1) & (same_ref[...] > 0.5)
    weights = jnp.where(valid, jnp.exp(scores), 0.0)
    totals = jnp.sum(weights, axis=1, keepdims=True)
    soft = weights / jnp.where(totals > 0.0, totals, 1.0)
    target = jnp.where(query & (cols == rows + 1), 1.0, 0.0)
    d_score = loss_scale * (soft - target)
    both = d_score + d_score.T
    coef = jnp.sum(both * scores, axis=1, keepdims=True)
    mix = score_scale * both / norms - jnp.where(rows == cols, coef / (norm_col * norm_col), 0.0)
    mean, gain = mean_ref[...], gain_ref[...]
    d_pooled = jnp.dot(mix, mean * gain, precision=highest, preferred_element_type=f32)
    gain_grad_ref[...] = jnp.sum(d_pooled * mean, axis=0, keepdims=True)
    own_ref[...] = d_pooled * gain * (1.0 / SEQ)
    for place in range(group):
        part = part_ref[(place % NZL) * NY + place // NZL, 1]
        gain = gain_block_ref[0, place : place + 1, :]
        d_pooled = jnp.dot(mix, part * gain, precision=highest, preferred_element_type=f32)
        block_ref[place] = d_pooled * gain * (1.0 / SEQ)
        block_gain_ref[place : place + 1, :] = jnp.sum(d_pooled * part, axis=0, keepdims=True)


def contrast(parts, same, gain_blocks, means, gain, x):
    group, _, seqs, lanes = parts.shape
    width = means.shape[1]
    whole = lambda shape: pl.BlockSpec(shape, lambda i, s: (0,) * len(shape))
    return pl.pallas_call(
        contrast_kernel,
        grid_spec=pltpu.PrefetchScalarGridSpec(
            num_scalar_prefetch=1,
            grid=(1,),
            in_specs=[
                whole(parts.shape),
                whole(same.shape),
                pl.BlockSpec((1, group, lanes), lambda i, s: (s[0], 0, 0)),
                whole(means.shape),
                whole(gain.shape),
            ],
            out_specs=[whole((group, seqs, lanes)), whole((group, lanes)), whole((seqs, width)), whole((1, width))],
        ),
        out_shape=(
            jax.ShapeDtypeStruct((group, seqs, lanes), f32),
            jax.ShapeDtypeStruct((group, lanes), f32),
            jax.ShapeDtypeStruct((seqs, width), f32),
            jax.ShapeDtypeStruct((1, width), f32),
        ),
        compiler_params=pltpu.CompilerParams(vmem_limit_bytes=16 * MIB),
        cost_estimate=QUICK,
    )(x.astype(jnp.int32).reshape(1), parts, same, gain_blocks, means, gain)


def row_to_column(row):
    n = row.shape[1]
    eye = lax.broadcasted_iota(jnp.int32, (n, n), 0) == lax.broadcasted_iota(jnp.int32, (n, n), 1)
    return jnp.sum(jnp.where(eye, jnp.broadcast_to(row, (n, n)), 0.0), axis=1, keepdims=True)


def column_to_row(column):
    n = column.shape[0]
    eye = lax.broadcasted_iota(jnp.int32, (n, n), 0) == lax.broadcasted_iota(jnp.int32, (n, n), 1)
    return jnp.sum(jnp.where(eye, jnp.broadcast_to(column, (n, n)), 0.0), axis=0, keepdims=True)


def along_kernel(plan_ref, *refs):
    *layer_refs, scaled_ref, out_ref = refs
    tokens = layer_refs[0].shape[1]
    first = plan_ref[pl.program_id(0)]
    for s in range(tokens // SEQ):
        rows = slice(s * SEQ, (s + 1) * SEQ)
        along = None
        for i, ref in enumerate(layer_refs):
            scaled = scaled_ref[plan_ref[NX + i], pl.ds(first + s, 1), :]
            term = ref[0, rows, :].astype(f32) * scaled
            along = term if along is None else along + term
        out_ref[0, s : s + 1, :] = column_to_row(jnp.sum(along, axis=1, keepdims=True))


def along_part(strips, scaled, plan):
    _, tokens, lanes = strips[0].shape
    group = len(strips)
    seqs_here = tokens // SEQ
    return pl.pallas_call(
        along_kernel,
        grid_spec=pltpu.PrefetchScalarGridSpec(
            num_scalar_prefetch=1,
            grid=(NX,),
            in_specs=[pl.BlockSpec((1, tokens, lanes), lambda i, s: (i, 0, 0))] * group
            + [pl.BlockSpec(scaled.shape, lambda i, s: (0, 0, 0))],
            out_specs=pl.BlockSpec((1, seqs_here, SEQ), lambda i, s: (s[NX + 3 * group + i], 0, 0)),
        ),
        out_shape=jax.ShapeDtypeStruct((NX, seqs_here, SEQ), f32),
        compiler_params=pltpu.CompilerParams(vmem_limit_bytes=16 * MIB),
        cost_estimate=QUICK,
    )(plan, *strips, scaled)


def group_grad_kernel(plan_ref, *refs):
    *layer_refs, scaled_ref, sum_ref, low_ref, coef_ref, factor_ref = refs
    _, tokens, lanes = layer_refs[0].shape
    group = len(layer_refs)
    seqs_here = tokens // SEQ
    here = pl.program_id(0)
    first = plan_ref[here]

    @pl.when(here == 0)
    def _():
        for i in range(NX):
            position = plan_ref[NX + 3 * group + i]
            along, inverse = sum_ref[position], sum_ref[NX + position]
            coef = inverse * inverse * inverse * along / (NX * group * lanes)
            factor_ref[i, :seqs_here] = inverse
            factor_ref[i, seqs_here:] = coef
            if i == 0:
                coef_ref[...] = coef

    for s in range(seqs_here):
        rows = slice(s * SEQ, (s + 1) * SEQ)
        inverse = row_to_column(factor_ref[here, s : s + 1, :])
        coef = row_to_column(factor_ref[here, seqs_here + s : seqs_here + s + 1, :])
        for i, ref in enumerate(layer_refs):
            scaled = scaled_ref[plan_ref[NX + i], pl.ds(first + s, 1), :]
            low = inverse * scaled - ref[0, rows, :].astype(f32) * coef
            side = pl.ds(pl.multiple_of(plan_ref[NX + 2 * group + i], lanes), lanes)
            low_ref[plan_ref[NX + group + i], rows, side] = low.astype(bf16)


def group_grad(strips, scaled, sums, plan):
    _, tokens, lanes = strips[0].shape
    group = len(strips)
    quarter = group * lanes // 4
    seqs_here = tokens // SEQ
    return pl.pallas_call(
        group_grad_kernel,
        grid_spec=pltpu.PrefetchScalarGridSpec(
            num_scalar_prefetch=1,
            grid=(NX,),
            in_specs=[pl.BlockSpec((1, tokens, lanes), lambda i, s: (i, 0, 0))] * group
            + [pl.BlockSpec(scaled.shape, lambda i, s: (0, 0, 0))]
            + [pl.BlockSpec(sums.shape, lambda i, s: (0, 0, 0))],
            out_specs=[
                pl.BlockSpec((4, tokens, quarter), lambda i, s: (0, i, 0)),
                pl.BlockSpec((seqs_here, SEQ), lambda i, s: (0, 0)),
            ],
            scratch_shapes=[pltpu.VMEM((NX, 2 * seqs_here, SEQ), f32)],
        ),
        out_shape=(
            jax.ShapeDtypeStruct((4, NX * tokens, quarter), bf16),
            jax.ShapeDtypeStruct((seqs_here, SEQ), f32),
        ),
        compiler_params=pltpu.CompilerParams(vmem_limit_bytes=24 * MIB),
        cost_estimate=QUICK,
    )(plan, *strips, scaled, sums)


def hidden_grad_kernel(plan_ref, *refs):
    refs, outs = refs[:-5], refs[-5:]
    out_ref, resid_ref, gain_ref, low_ref, gains_ref = outs
    *refs, scaled_ref, block_gain_ref, inverse_ref, coef_ref, weight_ref = refs
    tokens = out_ref.shape[0]
    seqs_here = tokens // SEQ
    group = len(refs) // 2
    others, _, lanes = refs[0].shape
    width = resid_ref.shape[1]
    x, first = plan_ref[1], plan_ref[2]

    @pl.when(pl.program_id(0) == 0)
    def _():
        factors = [
            [jnp.broadcast_to(row_to_column(ref[s : s + 1, :]), (SEQ, lanes)) for ref in (inverse_ref, coef_ref)]
            for s in range(seqs_here)
        ]
        for i in range(group):
            place = plan_ref[3 + i]
            row_ref, strip_ref = refs[i], refs[group + i]
            for j in range(others + 1):
                block = lax.rem(x + j, others + 1)
                column = pl.ds(pl.multiple_of((block * group + place) * lanes, lanes), lanes)
                if j:
                    tail = row_ref[j - 1, tokens:, :].astype(f32)
                    tail = tail[:8] + tail[8:]
                    gains_ref[place, pl.ds(block, 1), :] = tail[seqs_here : seqs_here + 1]
                else:
                    gains_ref[place, pl.ds(block, 1), :] = block_gain_ref[pl.ds(place, 1), :]
                for s in range(seqs_here):
                    rows = slice(s * SEQ, (s + 1) * SEQ)
                    if j:
                        layer, scaled = row_ref[j - 1, rows, :], tail[s : s + 1]
                    else:
                        layer, scaled = strip_ref[0, rows, :], scaled_ref[place, pl.ds(first + s, 1), :]
                    inverse, coef = factors[s]
                    low_ref[rows, column] = (inverse * scaled - layer.astype(f32) * coef).astype(bf16)
        first_place = plan_ref[0] % 2 * (group // 2)
        for j in range(group // 2):
            gain_ref[j : j + 1, :] = gains_ref[first_place + j, pl.ds(plan_ref[0] // 2, 1), :]
        resid_ref[...] = low_ref[:, pl.ds(pl.multiple_of(plan_ref[0] * width, width), width)]

    out_ref[...] = lax.dot_general(
        low_ref[...], weight_ref[...], (((1,), (1,)), ((), ())), preferred_element_type=f32
    ).astype(out_ref.dtype)


def hidden_grad(rows, strips, scaled, block_gain, inverse, coef, weight, plan):
    others, height, lanes = rows[0].shape
    group = len(rows)
    seqs_here = inverse.shape[0]
    tokens = seqs_here * SEQ
    units, model_width = weight.shape
    chunk = units // GRAD_STEPS
    width = model_width // group
    whole = lambda shape: pl.BlockSpec(shape, lambda i, s: (0,) * len(shape))
    return pl.pallas_call(
        hidden_grad_kernel,
        grid_spec=pltpu.PrefetchScalarGridSpec(
            num_scalar_prefetch=1,
            grid=(GRAD_STEPS,),
            in_specs=[whole(rows[0].shape)] * group
            + [whole((1, tokens, lanes))] * group
            + [whole(v.shape) for v in (scaled, block_gain, inverse, coef)]
            + [pl.BlockSpec((chunk, model_width), lambda i, s: (i, 0))],
            out_specs=[
                pl.BlockSpec((tokens, chunk), lambda i, s: (0, i)),
                whole((tokens, width)),
                whole((group // 2, lanes)),
            ],
            scratch_shapes=[
                pltpu.VMEM((tokens, model_width), bf16),
                pltpu.VMEM((group, others + 1, lanes), f32),
            ],
        ),
        out_shape=(
            jax.ShapeDtypeStruct((tokens, units), bf16),
            jax.ShapeDtypeStruct((tokens, width), bf16),
            jax.ShapeDtypeStruct((group // 2, lanes), f32),
        ),
        compiler_params=pltpu.CompilerParams(vmem_limit_bytes=56 * MIB),
        cost_estimate=QUICK,
    )(jnp.stack(plan).astype(jnp.int32), *rows, *strips, scaled, block_gain, inverse, coef, weight)


def tie(*values):
    return lax.optimization_barrier(values)


def gather_start(value):
    return {
        (0, 0): value,
        (1, 0): over_zl(value),
        (0, 1): over_y(value, -1),
        (0, 3): over_y(value, 1),
    }


def gather_next(got):
    got = dict(got)
    got[1, 1] = over_y(got[1, 0], -1)
    got[1, 3] = over_zl(got[0, 3])
    got[0, 2] = over_y(got[0, 3], 1)
    return got


def gather_last(got):
    got = dict(got)
    got[1, 2] = over_y(got[1, 1], -1)
    return got


def tie_gather(got, *values):
    keys = list(got)
    tied = tie(*got.values(), *values)
    return (dict(zip(keys, tied)),) + tuple(tied[len(keys) :])


def per_device(resid, hidden, down_weight, gain, domain_ids):
    tokens, units = hidden.shape
    model_width = down_weight.shape[1]
    group = lax.axis_size("tensor")
    shards = lax.axis_size("dp")
    width = model_width // group
    lanes = width // NX
    seqs_here = tokens // SEQ
    seqs = seqs_here * shards
    rank = lax.axis_index("tensor")
    zl, y = rank // NY, rank % NY
    place = y * NZL + zl
    shard = lax.axis_index("dp")
    x, zh, core = shard // (NZH * NCORE), (shard // NCORE) % NZH, shard % NCORE

    def place_of(part, step):
        return ((y + step) % NY) * NZL + (zl + part) % NZL

    with jax.named_scope("tables"):
        owner = jnp.repeat(domain_ids, seqs_here)
        same = (owner[:, None] == owner[None, :]).astype(f32)
        gain_blocks = gain.reshape(NX, group, lanes)
        gain_own = lax.dynamic_slice_in_dim(gain_blocks, place, 1, 1).reshape(1, width)
        peers = [((x + step) % NX) * (NZH * NCORE) + zh * NCORE + core for step in (0, -1, 1, 2)]
        places = [place_of(*key) for key in KEYS]
        plan = [p * seqs_here for p in peers] + places
        plan += [(p // 2) ^ (zh * NCORE + core) for p in places] + [p % 2 * lanes for p in places]
        plan += [(x + step) % NX for step in (0, -1, 1, 2)]
        plan = jnp.stack([jnp.asarray(v, jnp.int32) for v in plan])

    with jax.named_scope("hidden_exchange"):
        hidden_left = over_x(hidden, 1)
        hidden_right = over_x(hidden, -1)

    with jax.named_scope("resid_exchange"):
        pieces = resid.reshape(tokens, 2, NZL, lanes).transpose(2, 1, 0, 3)[:, None]
        pieces = jnp.broadcast_to(pieces, (NZL, NY // 2, 2, tokens, lanes))
        pieces = lax.all_to_all(pieces.reshape(group, tokens, lanes), "tensor", 0, 0)
        pieces = pieces.reshape(NX, 2, tokens, lanes)

    with jax.named_scope("layer_sum"):
        def dot_for(steps, dtypes):
            columns = [(y + step) % NY for step in steps]
            return layer_dot(hidden, down_weight, columns, zl, group, dtypes)

        *sums, pieces = tie(*dot_for((2, 1, 3, 0), (bf16, bf16, bf16, f32)), pieces)
        term = dict(zip([(part, step) for step in (2, 1, 3, 0) for part in (0, 1)], sums))

        def add(*values):
            return sum(value.astype(f32) for value in values)

        from_12 = over_y(term[1, 2], -1)
        from_11 = over_y(term[1, 1], 1)
        from_12, from_11, hidden_left, hidden_right = tie(from_12, from_11, hidden_left, hidden_right)
        hidden_far = (
            over_x(hidden_left[: tokens // 2], 1),
            over_x(hidden_right[tokens // 2 :], -1),
        )
        from_13 = over_zl(add(term[1, 3], from_12).astype(bf16))
        from_02 = over_y(term[0, 2], -1)
        from_01 = over_y(term[0, 1], 1)
        own_other = add(term[1, 0], from_11).astype(bf16)
        from_13, from_02 = tie(from_13, from_02)
        from_03 = over_y(add(term[0, 3], from_13, from_02).astype(bf16), -1)
        from_10 = over_zl(own_other)
        from_03, from_10, from_01, *hidden_far = tie(from_03, from_10, from_01, *hidden_far)
        resid_strips = lax.dynamic_slice_in_dim(pieces, y // 2, 1, 1)[:, 0]
        layer = add(term[0, 0], resid_strips, from_01, from_03, from_10)

    with jax.named_scope("strip_exchange"):
        low_layer = layer.astype(bf16)
        strips_x = [lax.dynamic_slice_in_dim(low_layer, x, 1, 0)]
        for step in (1, -1, 2):
            strip = lax.dynamic_slice_in_dim(low_layer, (x + step) % NX, 1, 0)
            strips_x.append(over_x(strip, step))
        message = jnp.concatenate(strips_x, axis=0)

    with jax.named_scope("norm"):
        squares = jnp.sum(layer * layer, axis=(0, 2)).reshape(seqs_here, SEQ)
        squares = jnp.sum(gather_small(squares, "tensor"), axis=0)
        message, squares = tie(message, squares)
        hidden_rows = jnp.concatenate([hidden, hidden_left, hidden_right] + hidden_far, axis=0)
        got = gather_start(message)
        inverse = lax.rsqrt(squares / model_width + eps_norm)
        weighted = layer.reshape(NX, seqs_here, SEQ, lanes) * inverse[None, :, :, None]
        means = jnp.mean(weighted, axis=2).transpose(1, 0, 2).reshape(seqs_here, width)

    with jax.named_scope("contrast"):
        means_all = gather_small(means, "dp")
        got, means_all = tie_gather(got, means_all)
        got = gather_next(got)
        means_all = means_all.reshape(seqs, width)
        parts = gather_small(gram_part(means_all, gain_own, x), "tensor")
        got, parts, low_layer, hidden_rows = tie_gather(got, parts, low_layer, hidden_rows)
        got = gather_last(got)
        strips = [got[key] for key in KEYS]
        scaled, gain_grad_x, scaled_own, gain_grad = contrast(
            parts, same, gain_blocks, means_all, gain_own, x
        )

    with jax.named_scope("row_gather"):
        own_rows = lax.dynamic_slice_in_dim(scaled_own, shard * seqs_here, seqs_here, 0)
        own_rows = jnp.pad(jnp.concatenate([own_rows, gain_grad], axis=0), ((0, 8 - seqs_here - 1), (0, 0)))
        high = lax.reduce_precision(own_rows, exponent_bits=8, mantissa_bits=7)
        tail = jnp.concatenate([high, own_rows - high], axis=0).astype(bf16)
        tail = tail.reshape(16, NX, lanes).transpose(1, 0, 2)
        blocks = jnp.concatenate([low_layer, tail], axis=1)
        blocks = jnp.concatenate([blocks, blocks], axis=0)
        rows = gather_start(lax.dynamic_slice_in_dim(blocks, x + 1, NX - 1, 0))

    with jax.named_scope("along"):
        own_inverse = jnp.where(jnp.arange(NX)[:, None, None] == x, inverse[None], 0.0)
        sums = jnp.concatenate([along_part(strips, scaled, plan), own_inverse], axis=0)
        sums = sums + lax.ppermute(sums, "dp", swap_route(1))
        rows, sums = tie_gather(rows, sums)
        rows = gather_next(rows)
        sums = sums + lax.ppermute(sums, "dp", swap_route(2))

    with jax.named_scope("down_grad"):
        low_x, coef = group_grad(strips, scaled, sums, plan)
        rows, low_x = tie_gather(rows, low_x)
        rows = gather_last(rows)

        def down(low):
            return lax.dot_general(
                hidden_rows, low, (((0,), (0,)), ((), ())), preferred_element_type=f32
            )

        from_core = over_core(down(low_x[3]))
        summed = (down(low_x[2]) + from_core).astype(bf16)
        summed, low0, low1 = tie(summed, low_x[0], low_x[1])
        across = over_zh(summed)
        near1 = down(low1)
        near = down(low0) + over_core(near1)

    with jax.named_scope("hidden_grad"):
        rows, near = tie_gather(rows, near)
        rows = [rows[key] for key in KEYS]
        grad_hidden, grad_resid, gain_grad = hidden_grad(
            rows, strips, scaled, gain_grad_x, inverse, coef, down_weight, [rank, x, shard * seqs_here] + places
        )
        grad_gain = gain_grad.reshape(width)

    with jax.named_scope("down_grad"):
        across, grad_hidden = tie(across, grad_hidden)
        grad_down = near + across.astype(f32)

    return (grad_hidden, grad_resid, grad_down, grad_gain)


def solution(mesh):
    return jax.shard_map(
        per_device,
        mesh=mesh,
        in_specs=(P("dp", "tensor"), P("dp", "tensor"), P("tensor", None), P(), P()),
        out_specs=(P("dp", "tensor"), P("dp", "tensor"), P("tensor", "dp"), P("tensor")),
        check_vma=False,
    )
```

```python
import functools
import jax
import jax.numpy as jnp
from jax import lax
from jax.experimental import pallas as pl
from jax.experimental.pallas import tpu as pltpu
from jax.sharding import PartitionSpec as P

SEQ = 128
NX, NZH, NCORE, NZL, NY = 4, 2, 2, 2, 4
GRAD_STEPS = 7
KEYS = ((0, 0), (1, 0), (0, 1), (0, 3), (0, 2), (1, 1), (1, 3), (1, 2))

score_scale = 20.0
loss_scale = 8192.0
eps_norm = 1e-05
eps_embed = 1e-06
highest = lax.Precision.HIGHEST
f32 = jnp.float32
bf16 = jnp.bfloat16
MIB = 1024 * 1024
QUICK = pl.CostEstimate(flops=1024, bytes_accessed=1024, transcendentals=0)


def dp_route(dx, dz, dc):
    pairs = []
    for x in range(NX):
        for z in range(NZH):
            for c in range(NCORE):
                to = (((x + dx) % NX) * NZH + (z + dz) % NZH) * NCORE + (c + dc) % NCORE
                pairs.append(((x * NZH + z) * NCORE + c, to))
    return pairs


def tensor_route(dz, dy):
    pairs = []
    for z in range(NZL):
        for y in range(NY):
            pairs.append((z * NY + y, ((z + dz) % NZL) * NY + (y + dy) % NY))
    return pairs


def swap_route(bit):
    size = NZH * NCORE
    return [(d, (d // size ^ bit) * size + d % size) for d in range(NX * size)]


def over_x(value, step):
    return lax.ppermute(value, "dp", dp_route(step, 0, 0))


def over_zh(value):
    return lax.ppermute(value, "dp", dp_route(0, 1, 0))


def over_core(value):
    return lax.ppermute(value, "dp", dp_route(0, 0, 1))


def over_y(value, step):
    return lax.ppermute(value, "tensor", tensor_route(0, step))


def over_zl(value):
    return lax.ppermute(value, "tensor", tensor_route(1, 0))


def gather_small(value, axis):
    n = lax.axis_size(axis)
    copies = jnp.broadcast_to(value[None], (n,) + value.shape)
    return lax.all_to_all(copies, axis, 0, 0)


def layer_dot_kernel(plan_ref, hidden_ref, weight_ref, *refs):
    *out_refs, total_ref = refs
    lanes = out_refs[0].shape[-1]
    flip = plan_ref[0] == 1
    total_ref[...] = jnp.dot(hidden_ref[...], weight_ref[...], preferred_element_type=f32)
    for c in range(len(out_refs) // 2):
        same_ref, other_ref = out_refs[2 * c : 2 * c + 2]
        start = pl.multiple_of(plan_ref[1 + c] * 2 * lanes, 2 * lanes)
        pair = total_ref[:, pl.ds(start, 2 * lanes)]
        first, second = pair[:, :lanes], pair[:, lanes:]
        same_ref[0] = jnp.where(flip, second, first).astype(same_ref.dtype)
        other_ref[0] = jnp.where(flip, first, second).astype(other_ref.dtype)


def layer_dot(hidden, weight, columns, zl, group, dtypes):
    tokens, units = hidden.shape
    model_width = weight.shape[1]
    lanes = model_width // (NX * group)
    out = pl.BlockSpec((1, tokens, lanes), lambda b, s: (b, 0, 0))
    return pl.pallas_call(
        layer_dot_kernel,
        grid_spec=pltpu.PrefetchScalarGridSpec(
            num_scalar_prefetch=1,
            grid=(NX,),
            in_specs=[
                pl.BlockSpec((tokens, units), lambda b, s: (0, 0)),
                pl.BlockSpec((units, group * lanes), lambda b, s: (0, b)),
            ],
            out_specs=[out] * (2 * len(columns)),
            scratch_shapes=[pltpu.VMEM((tokens, group * lanes), f32)],
        ),
        out_shape=[
            jax.ShapeDtypeStruct((NX, tokens, lanes), dtype) for dtype in dtypes for _ in range(2)
        ],
        compiler_params=pltpu.CompilerParams(vmem_limit_bytes=56 * MIB),
        cost_estimate=pl.CostEstimate(
            flops=2 * tokens * units * model_width,
            bytes_accessed=2 * (tokens * units + units * model_width + tokens * model_width),
            transcendentals=0,
        ),
    )(jnp.stack([zl] + columns).astype(jnp.int32), hidden, weight)


def pair_picks(seqs):
    rows = lax.broadcasted_iota(jnp.int32, (seqs // 2, seqs), 0)
    cols = lax.broadcasted_iota(jnp.int32, (seqs // 2, seqs), 1)
    return (cols == 2 * rows).astype(f32), (cols == 2 * rows + 1).astype(f32)


def exact_dot(left, right, contract):
    return lax.dot_general(left, right, (contract, ((), ())), precision=highest, preferred_element_type=f32)


def gram_kernel(plan_ref, mean_ref, gain_ref, strip_ref, out_ref):
    seqs, width = mean_ref.shape
    pooled = mean_ref[...] * gain_ref[...]
    queries, passages = [exact_dot(pick, pooled, ((1,), (0,))) for pick in pair_picks(seqs)]
    dots = exact_dot(queries, passages, ((1,), (1,)))
    squares = exact_dot(jnp.ones((8, width), f32), pooled * pooled, ((1,), (1,)))
    out_ref[:seqs, :] = strip_ref[...]
    out_ref[seqs : seqs + 8, :] = jnp.concatenate([dots[8 * i : 8 * i + 8] for i in range(4)], axis=1)
    out_ref[seqs + 8 :, :] = jnp.concatenate([squares, jnp.zeros_like(squares)], axis=1)


def gram_part(means, gain, x):
    seqs, width = means.shape
    lanes = 2 * seqs
    return pl.pallas_call(
        gram_kernel,
        grid_spec=pltpu.PrefetchScalarGridSpec(
            num_scalar_prefetch=1,
            grid=(1,),
            in_specs=[
                pl.BlockSpec((seqs, width), lambda i, s: (0, 0)),
                pl.BlockSpec((1, width), lambda i, s: (0, 0)),
                pl.BlockSpec((seqs, lanes), lambda i, s: (0, s[0])),
            ],
            out_specs=pl.BlockSpec((seqs + 16, lanes), lambda i, s: (0, 0)),
        ),
        out_shape=jax.ShapeDtypeStruct((seqs + 16, lanes), f32),
        compiler_params=pltpu.CompilerParams(vmem_limit_bytes=16 * MIB),
        cost_estimate=QUICK,
    )(x.astype(jnp.int32).reshape(1), means, gain, means)


def contrast_kernel(
    plan_ref, part_ref, same_ref, gain_block_ref, mean_ref, gain_ref, block_ref, block_gain_ref, own_ref, gain_grad_ref
):
    group = part_ref.shape[0]
    seqs = mean_ref.shape[0]
    rows = lax.broadcasted_iota(jnp.int32, (seqs, seqs), 0)
    cols = lax.broadcasted_iota(jnp.int32, (seqs, seqs), 1)
    total = part_ref[0, seqs:, :]
    for r in range(1, group):
        total += part_ref[r, seqs:, :]
    half = seqs // 2
    dots = jnp.concatenate([total[:8, half * i : half * (i + 1)] for i in range(4)], axis=0)
    pick_query, pick_passage = pair_picks(seqs)
    gram = exact_dot(pick_query, exact_dot(dots, pick_passage, ((1,), (0,))), ((0,), (0,)))
    gram = gram + gram.T
    norm_row = jnp.sqrt(total[8:9, :seqs] + eps_embed)
    norm_col = row_to_column(norm_row)
    norms = norm_col * norm_row
    scores = score_scale * gram / norms
    query = rows % 2 == 0
    valid = query & (cols % 2 == 1) & (same_ref[...] > 0.5)
    weights = jnp.where(valid, jnp.exp(scores), 0.0)
    totals = jnp.sum(weights, axis=1, keepdims=True)
    soft = weights / jnp.where(totals > 0.0, totals, 1.0)
    target = jnp.where(query & (cols == rows + 1), 1.0, 0.0)
    d_score = loss_scale * (soft - target)
    both = d_score + d_score.T
    coef = jnp.sum(both * scores, axis=1, keepdims=True)
    mix = score_scale * both / norms - jnp.where(rows == cols, coef / (norm_col * norm_col), 0.0)
    mean, gain = mean_ref[...], gain_ref[...]
    d_pooled = jnp.dot(mix, mean * gain, precision=highest, preferred_element_type=f32)
    gain_grad_ref[...] = jnp.sum(d_pooled * mean, axis=0, keepdims=True)
    own_ref[...] = d_pooled * gain * (1.0 / SEQ)
    for place in range(group):
        part = part_ref[(place % NZL) * NY + place // NZL, :seqs, :]
        gain = gain_block_ref[0, place : place + 1, :]
        d_pooled = jnp.dot(mix, part * gain, precision=highest, preferred_element_type=f32)
        block_ref[place] = d_pooled * gain * (1.0 / SEQ)
        block_gain_ref[place : place + 1, :] = jnp.sum(d_pooled * part, axis=0, keepdims=True)


def contrast(parts, same, gain_blocks, means, gain, x):
    group, _, lanes = parts.shape
    seqs, width = means.shape
    whole = lambda shape: pl.BlockSpec(shape, lambda i, s: (0,) * len(shape))
    return pl.pallas_call(
        contrast_kernel,
        grid_spec=pltpu.PrefetchScalarGridSpec(
            num_scalar_prefetch=1,
            grid=(1,),
            in_specs=[
                whole(parts.shape),
                whole(same.shape),
                pl.BlockSpec((1, group, lanes), lambda i, s: (s[0], 0, 0)),
                whole(means.shape),
                whole(gain.shape),
            ],
            out_specs=[whole((group, seqs, lanes)), whole((group, lanes)), whole((seqs, width)), whole((1, width))],
        ),
        out_shape=(
            jax.ShapeDtypeStruct((group, seqs, lanes), f32),
            jax.ShapeDtypeStruct((group, lanes), f32),
            jax.ShapeDtypeStruct((seqs, width), f32),
            jax.ShapeDtypeStruct((1, width), f32),
        ),
        compiler_params=pltpu.CompilerParams(vmem_limit_bytes=16 * MIB),
        cost_estimate=QUICK,
    )(x.astype(jnp.int32).reshape(1), parts, same, gain_blocks, means, gain)


def row_to_column(row):
    n = row.shape[1]
    eye = lax.broadcasted_iota(jnp.int32, (n, n), 0) == lax.broadcasted_iota(jnp.int32, (n, n), 1)
    return jnp.sum(jnp.where(eye, jnp.broadcast_to(row, (n, n)), 0.0), axis=1, keepdims=True)


def column_to_row(column):
    n = column.shape[0]
    eye = lax.broadcasted_iota(jnp.int32, (n, n), 0) == lax.broadcasted_iota(jnp.int32, (n, n), 1)
    return jnp.sum(jnp.where(eye, jnp.broadcast_to(column, (n, n)), 0.0), axis=0, keepdims=True)


def strip_reader(refs):
    *refs, last = refs
    first_half = pl.program_id(0) < NX // 2

    def read(i, rows):
        value = refs[i][0, rows, :]
        if i == len(refs) - 1:
            value = jnp.where(first_half, value, last[0, rows, :])
        return value.astype(f32)

    return read


def strip_specs(strips):
    _, tokens, lanes = strips[0].shape
    half = NX // 2
    block = (1, tokens, lanes)
    return [pl.BlockSpec(block, lambda i, s: (i, 0, 0))] * (len(strips) - 2) + [
        pl.BlockSpec(block, lambda i, s: (jnp.minimum(i, half - 1), 0, 0)),
        pl.BlockSpec(block, lambda i, s: (jnp.maximum(i - half, 0), 0, 0)),
    ]


def along_kernel(plan_ref, *refs):
    *layer_refs, scaled_ref, out_ref = refs
    tokens = layer_refs[0].shape[1]
    group = len(layer_refs) - 1
    read = strip_reader(layer_refs)
    first = plan_ref[pl.program_id(0)]
    for s in range(tokens // SEQ):
        rows = slice(s * SEQ, (s + 1) * SEQ)
        along = None
        for i in range(group):
            scaled = scaled_ref[plan_ref[NX + i], pl.ds(first + s, 1), :]
            term = read(i, rows) * scaled
            along = term if along is None else along + term
        out_ref[0, s : s + 1, :] = column_to_row(jnp.sum(along, axis=1, keepdims=True))


def along_part(strips, scaled, plan):
    _, tokens, lanes = strips[0].shape
    group = len(strips) - 1
    seqs_here = tokens // SEQ
    return pl.pallas_call(
        along_kernel,
        grid_spec=pltpu.PrefetchScalarGridSpec(
            num_scalar_prefetch=1,
            grid=(NX,),
            in_specs=strip_specs(strips) + [pl.BlockSpec(scaled.shape, lambda i, s: (0, 0, 0))],
            out_specs=pl.BlockSpec((1, seqs_here, SEQ), lambda i, s: (s[NX + 3 * group + i], 0, 0)),
        ),
        out_shape=jax.ShapeDtypeStruct((NX, seqs_here, SEQ), f32),
        compiler_params=pltpu.CompilerParams(vmem_limit_bytes=16 * MIB),
        cost_estimate=QUICK,
    )(plan, *strips, scaled)


def group_grad_kernel(plan_ref, *refs):
    *layer_refs, scaled_ref, sum_ref, low_ref, coef_ref, factor_ref = refs
    _, tokens, lanes = layer_refs[0].shape
    group = len(layer_refs) - 1
    read = strip_reader(layer_refs)
    seqs_here = tokens // SEQ
    here = pl.program_id(0)
    first = plan_ref[here]

    @pl.when(here == 0)
    def _():
        for i in range(NX):
            position = plan_ref[NX + 3 * group + i]
            along, inverse = sum_ref[position], sum_ref[NX + position]
            coef = inverse * inverse * inverse * along / (NX * group * lanes)
            factor_ref[i, :seqs_here] = inverse
            factor_ref[i, seqs_here:] = coef
            if i == 0:
                coef_ref[...] = coef

    for s in range(seqs_here):
        rows = slice(s * SEQ, (s + 1) * SEQ)
        inverse = row_to_column(factor_ref[here, s : s + 1, :])
        coef = row_to_column(factor_ref[here, seqs_here + s : seqs_here + s + 1, :])
        for i in range(group):
            scaled = scaled_ref[plan_ref[NX + i], pl.ds(first + s, 1), :]
            low = inverse * scaled - read(i, rows) * coef
            side = pl.ds(pl.multiple_of(plan_ref[NX + 2 * group + i], lanes), lanes)
            low_ref[plan_ref[NX + group + i], rows, side] = low.astype(bf16)


def group_grad(strips, scaled, sums, plan):
    _, tokens, lanes = strips[0].shape
    group = len(strips) - 1
    quarter = group * lanes // 4
    seqs_here = tokens // SEQ
    return pl.pallas_call(
        group_grad_kernel,
        grid_spec=pltpu.PrefetchScalarGridSpec(
            num_scalar_prefetch=1,
            grid=(NX,),
            in_specs=strip_specs(strips)
            + [pl.BlockSpec(scaled.shape, lambda i, s: (0, 0, 0))]
            + [pl.BlockSpec(sums.shape, lambda i, s: (0, 0, 0))],
            out_specs=[
                pl.BlockSpec((4, tokens, quarter), lambda i, s: (0, i, 0)),
                pl.BlockSpec((seqs_here, SEQ), lambda i, s: (0, 0)),
            ],
            scratch_shapes=[pltpu.VMEM((NX, 2 * seqs_here, SEQ), f32)],
        ),
        out_shape=(
            jax.ShapeDtypeStruct((4, NX * tokens, quarter), bf16),
            jax.ShapeDtypeStruct((seqs_here, SEQ), f32),
        ),
        compiler_params=pltpu.CompilerParams(vmem_limit_bytes=24 * MIB),
        cost_estimate=QUICK,
    )(plan, *strips, scaled, sums)


def hidden_grad_kernel(plan_ref, *refs):
    refs, outs = refs[:-5], refs[-5:]
    out_ref, resid_ref, gain_ref, low_ref, gains_ref = outs
    *refs, scaled_ref, block_gain_ref, inverse_ref, coef_ref, weight_ref = refs
    tokens = out_ref.shape[0]
    seqs_here = tokens // SEQ
    group = len(refs) // 2
    row_refs, rest_ref, strip_refs = refs[:group], refs[group], refs[group + 1 :]
    others, _, lanes = refs[0].shape
    width = resid_ref.shape[1]
    x, first = plan_ref[1], plan_ref[2]

    @pl.when(pl.program_id(0) == 0)
    def _():
        factors = [
            [jnp.broadcast_to(row_to_column(ref[s : s + 1, :]), (SEQ, lanes)) for ref in (inverse_ref, coef_ref)]
            for s in range(seqs_here)
        ]
        for i in range(group):
            place = plan_ref[3 + i]
            row_ref, strip_ref = row_refs[i], strip_refs[i]
            last = i == group - 1
            tail_ref, tail_start = (rest_ref, tokens // 2) if last else (row_ref, tokens)
            for j in range(others + 1):
                block = lax.rem(x + j, others + 1)
                column = pl.ds(pl.multiple_of((block * group + place) * lanes, lanes), lanes)
                if j:
                    tail = tail_ref[j - 1, tail_start:, :].astype(f32)
                    tail = tail[:8] + tail[8:]
                    gains_ref[place, pl.ds(block, 1), :] = tail[seqs_here : seqs_here + 1]
                else:
                    gains_ref[place, pl.ds(block, 1), :] = block_gain_ref[pl.ds(place, 1), :]
                for s in range(seqs_here):
                    rows = slice(s * SEQ, (s + 1) * SEQ)
                    if j and last and 2 * s >= seqs_here:
                        rest = slice(rows.start - tokens // 2, rows.stop - tokens // 2)
                        layer, scaled = rest_ref[j - 1, rest, :], tail[s : s + 1]
                    elif j:
                        layer, scaled = row_ref[j - 1, rows, :], tail[s : s + 1]
                    else:
                        layer, scaled = strip_ref[0, rows, :], scaled_ref[place, pl.ds(first + s, 1), :]
                    inverse, coef = factors[s]
                    low_ref[rows, column] = (inverse * scaled - layer.astype(f32) * coef).astype(bf16)
        first_place = plan_ref[0] % 2 * (group // 2)
        for j in range(group // 2):
            gain_ref[j : j + 1, :] = gains_ref[first_place + j, pl.ds(plan_ref[0] // 2, 1), :]
        resid_ref[...] = low_ref[:, pl.ds(pl.multiple_of(plan_ref[0] * width, width), width)]

    out_ref[...] = lax.dot_general(
        low_ref[...], weight_ref[...], (((1,), (1,)), ((), ())), preferred_element_type=f32
    ).astype(out_ref.dtype)


def hidden_grad(rows, strips, scaled, block_gain, inverse, coef, weight, plan):
    others, height, lanes = rows[0].shape
    group = len(strips)
    seqs_here = inverse.shape[0]
    tokens = seqs_here * SEQ
    units, model_width = weight.shape
    chunk = units // GRAD_STEPS
    width = model_width // group
    whole = lambda shape: pl.BlockSpec(shape, lambda i, s: (0,) * len(shape))
    return pl.pallas_call(
        hidden_grad_kernel,
        grid_spec=pltpu.PrefetchScalarGridSpec(
            num_scalar_prefetch=1,
            grid=(GRAD_STEPS,),
            in_specs=[whole(row.shape) for row in rows]
            + [whole((1, tokens, lanes))] * group
            + [whole(v.shape) for v in (scaled, block_gain, inverse, coef)]
            + [pl.BlockSpec((chunk, model_width), lambda i, s: (i, 0))],
            out_specs=[
                pl.BlockSpec((tokens, chunk), lambda i, s: (0, i)),
                whole((tokens, width)),
                whole((group // 2, lanes)),
            ],
            scratch_shapes=[
                pltpu.VMEM((tokens, model_width), bf16),
                pltpu.VMEM((group, others + 1, lanes), f32),
            ],
        ),
        out_shape=(
            jax.ShapeDtypeStruct((tokens, units), bf16),
            jax.ShapeDtypeStruct((tokens, width), bf16),
            jax.ShapeDtypeStruct((group // 2, lanes), f32),
        ),
        compiler_params=pltpu.CompilerParams(vmem_limit_bytes=56 * MIB),
        cost_estimate=QUICK,
    )(jnp.stack(plan).astype(jnp.int32), *rows, *strips, scaled, block_gain, inverse, coef, weight)


def tie(*values):
    return lax.optimization_barrier(values)


def gather_start(value):
    return {
        (0, 0): value,
        (1, 0): over_zl(value),
        (0, 1): over_y(value, -1),
        (0, 3): over_y(value, 1),
    }


def gather_next(got):
    got = dict(got)
    got[1, 1] = over_y(got[1, 0], -1)
    got[1, 3] = over_zl(got[0, 3])
    got[0, 2] = over_y(got[0, 3], 1)
    return got


def gather_last(got, cut):
    got = dict(got)
    got[1, 2] = over_y(got[1, 1][:, :cut], -1)
    got["rest"] = over_y(got[1, 3][:, cut:], 1)
    return got


def tie_gather(got, *values):
    keys = list(got)
    tied = tie(*got.values(), *values)
    return (dict(zip(keys, tied)),) + tuple(tied[len(keys) :])


def per_device(resid, hidden, down_weight, gain, domain_ids):
    tokens, units = hidden.shape
    model_width = down_weight.shape[1]
    group = lax.axis_size("tensor")
    shards = lax.axis_size("dp")
    width = model_width // group
    lanes = width // NX
    seqs_here = tokens // SEQ
    seqs = seqs_here * shards
    rank = lax.axis_index("tensor")
    zl, y = rank // NY, rank % NY
    place = y * NZL + zl
    shard = lax.axis_index("dp")
    x, zh, core = shard // (NZH * NCORE), (shard // NCORE) % NZH, shard % NCORE

    def place_of(part, step):
        return ((y + step) % NY) * NZL + (zl + part) % NZL

    with jax.named_scope("tables"):
        owner = jnp.repeat(domain_ids, seqs_here)
        same = (owner[:, None] == owner[None, :]).astype(f32)
        gain_blocks = gain.reshape(NX, group, lanes)
        gain_own = lax.dynamic_slice_in_dim(gain_blocks, place, 1, 1).reshape(1, width)
        peers = [((x + step) % NX) * (NZH * NCORE) + zh * NCORE + core for step in (0, -1, 1, 2)]
        places = [place_of(*key) for key in KEYS]
        plan = [p * seqs_here for p in peers] + places
        plan += [(p // 2) ^ (zh * NCORE + core) for p in places] + [p % 2 * lanes for p in places]
        plan += [(x + step) % NX for step in (0, -1, 1, 2)]
        plan = jnp.stack([jnp.asarray(v, jnp.int32) for v in plan])

    with jax.named_scope("hidden_exchange"):
        hidden_left = over_x(hidden, 1)
        hidden_right = over_x(hidden, -1)
        hidden_far = over_x(hidden, 2)

    with jax.named_scope("resid_exchange"):
        pieces = resid.reshape(tokens, 2, NZL, lanes).transpose(2, 1, 0, 3)[:, None]
        pieces = jnp.broadcast_to(pieces, (NZL, NY // 2, 2, tokens, lanes))
        pieces = lax.all_to_all(pieces.reshape(group, tokens, lanes), "tensor", 0, 0)
        pieces = pieces.reshape(NX, 2, tokens, lanes)

    with jax.named_scope("layer_sum"):
        def dot_for(steps, dtypes):
            columns = [(y + step) % NY for step in steps]
            return layer_dot(hidden, down_weight, columns, zl, group, dtypes)

        *sums, pieces = tie(*dot_for((2, 1, 3, 0), (bf16, bf16, bf16, f32)), pieces)
        term = dict(zip([(part, step) for step in (2, 1, 3, 0) for part in (0, 1)], sums))

        def add(*values):
            return sum(value.astype(f32) for value in values)

        from_12 = over_y(term[1, 2], -1)
        from_11 = over_y(term[1, 1], 1)
        from_02 = over_y(term[0, 2], 1)
        from_12, from_11, hidden_left, hidden_right = tie(from_12, from_11, hidden_left, hidden_right)
        from_13 = over_zl(add(term[1, 3], from_12).astype(bf16))
        own_other = add(term[1, 0], from_11).astype(bf16)
        from_13, from_02 = tie(from_13, from_02)
        from_03 = over_y(add(term[0, 3], from_13).astype(bf16), -1)
        from_01 = over_y(add(term[0, 1], from_02).astype(bf16), 1)
        from_10 = over_zl(own_other)
        from_03, from_10, from_01 = tie(from_03, from_10, from_01)
        resid_strips = lax.dynamic_slice_in_dim(pieces, y // 2, 1, 1)[:, 0]
        layer = add(term[0, 0], resid_strips, from_01, from_03, from_10)

    with jax.named_scope("strip_exchange"):
        low_layer = layer.astype(bf16)
        strips_x = [lax.dynamic_slice_in_dim(low_layer, x, 1, 0)]
        for step in (1, -1, 2):
            strip = lax.dynamic_slice_in_dim(low_layer, (x + step) % NX, 1, 0)
            strips_x.append(over_x(strip, step))
        message = jnp.concatenate(strips_x, axis=0)

    with jax.named_scope("norm"):
        squares = jnp.sum(layer * layer, axis=(0, 2)).reshape(seqs_here, SEQ)
        squares = jnp.sum(gather_small(squares, "tensor"), axis=0)
        message, squares, hidden_far = tie(message, squares, hidden_far)
        hidden_rows = jnp.concatenate([hidden, hidden_left, hidden_right, hidden_far], axis=0)
        got = gather_start(message)
        inverse = lax.rsqrt(squares / model_width + eps_norm)
        weighted = layer.reshape(NX, seqs_here, SEQ, lanes) * inverse[None, :, :, None]
        means = jnp.mean(weighted, axis=2).transpose(1, 0, 2).reshape(seqs_here, width)

    with jax.named_scope("contrast"):
        means_all = gather_small(means, "dp")
        got, means_all = tie_gather(got, means_all)
        got = gather_next(got)
        means_all = means_all.reshape(seqs, width)
        parts = gather_small(gram_part(means_all, gain_own, x), "tensor")
        got, parts, low_layer, hidden_rows = tie_gather(got, parts, low_layer, hidden_rows)
        half = NX // 2
        got[1, 2] = over_y(got[1, 1][:half], -1)
        strips = [got[key] for key in KEYS] + [over_y(got[1, 3][half:], 1)]
        scaled, gain_grad_x, scaled_own, gain_grad = contrast(
            parts, same, gain_blocks, means_all, gain_own, x
        )

    with jax.named_scope("row_gather"):
        own_rows = lax.dynamic_slice_in_dim(scaled_own, shard * seqs_here, seqs_here, 0)
        own_rows = jnp.pad(jnp.concatenate([own_rows, gain_grad], axis=0), ((0, 8 - seqs_here - 1), (0, 0)))
        high = lax.reduce_precision(own_rows, exponent_bits=8, mantissa_bits=7)
        tail = jnp.concatenate([high, own_rows - high], axis=0).astype(bf16)
        tail = tail.reshape(16, NX, lanes).transpose(1, 0, 2)
        blocks = jnp.concatenate([low_layer, tail], axis=1)
        blocks = jnp.concatenate([blocks, blocks], axis=0)
        rows = gather_start(lax.dynamic_slice_in_dim(blocks, x + 1, NX - 1, 0))

    with jax.named_scope("along"):
        own_inverse = jnp.where(jnp.arange(NX)[:, None, None] == x, inverse[None], 0.0)
        sums = jnp.concatenate([along_part(strips, scaled, plan), own_inverse], axis=0)
        sums = sums + lax.ppermute(sums, "dp", swap_route(1))
        rows, sums = tie_gather(rows, sums)
        rows = gather_next(rows)
        sums = sums + lax.ppermute(sums, "dp", swap_route(2))

    with jax.named_scope("down_grad"):
        low_x, coef = group_grad(strips, scaled, sums, plan)
        rows, low_x = tie_gather(rows, low_x)
        rows = gather_last(rows, tokens // 2)

        def down(low):
            return lax.dot_general(
                hidden_rows, low, (((0,), (0,)), ((), ())), preferred_element_type=f32
            )

        part3, low_x = tie(down(low_x[3]), low_x)
        part1, low_x = tie(down(low_x[1]), low_x)
        from_core = over_core(part3), over_core(part1)
        summed = (down(low_x[2]) + from_core[0]).astype(bf16)
        summed, low0 = tie(summed, low_x[0])
        across = over_zh(summed)
        rows, low0 = tie_gather(rows, low0)
        near = down(low0) + from_core[1]

    with jax.named_scope("hidden_grad"):
        rows, near = tie_gather(rows, near)
        rows = [rows[key] for key in KEYS + ("rest",)]
        grad_hidden, grad_resid, gain_grad = hidden_grad(
            rows, strips[:group], scaled, gain_grad_x, inverse, coef, down_weight, [rank, x, shard * seqs_here] + places
        )
        grad_gain = gain_grad.reshape(width)

    with jax.named_scope("down_grad"):
        across, grad_hidden = tie(across, grad_hidden)
        grad_down = near + across.astype(f32)

    return (grad_hidden, grad_resid, grad_down, grad_gain)


def solution(mesh):
    return jax.shard_map(
        per_device,
        mesh=mesh,
        in_specs=(P("dp", "tensor"), P("dp", "tensor"), P("tensor", None), P(), P()),
        out_specs=(P("dp", "tensor"), P("dp", "tensor"), P("tensor", "dp"), P("tensor")),
        check_vma=False,
    )
```

```python
import functools
import jax
import jax.numpy as jnp
from jax import lax
from jax.experimental import pallas as pl
from jax.experimental.pallas import tpu as pltpu
from jax.sharding import PartitionSpec as P

SEQ = 128
NX, NZH, NCORE, NZL, NY = 4, 2, 2, 2, 4
GRAD_STEPS = 7
KEYS = ((0, 0), (1, 0), (0, 1), (0, 3), (0, 2), (1, 1), (1, 3), (1, 2))

score_scale = 20.0
loss_scale = 8192.0
eps_norm = 1e-05
eps_embed = 1e-06
highest = lax.Precision.HIGHEST
f32 = jnp.float32
bf16 = jnp.bfloat16
MIB = 1024 * 1024
QUICK = pl.CostEstimate(flops=1024, bytes_accessed=1024, transcendentals=0)


def dp_route(dx, dz, dc):
    pairs = []
    for x in range(NX):
        for z in range(NZH):
            for c in range(NCORE):
                to = (((x + dx) % NX) * NZH + (z + dz) % NZH) * NCORE + (c + dc) % NCORE
                pairs.append(((x * NZH + z) * NCORE + c, to))
    return pairs


def tensor_route(dz, dy):
    pairs = []
    for z in range(NZL):
        for y in range(NY):
            pairs.append((z * NY + y, ((z + dz) % NZL) * NY + (y + dy) % NY))
    return pairs


def swap_route(bit):
    size = NZH * NCORE
    return [(d, (d // size ^ bit) * size + d % size) for d in range(NX * size)]


def over_x(value, step):
    return lax.ppermute(value, "dp", dp_route(step, 0, 0))


def over_zh(value):
    return lax.ppermute(value, "dp", dp_route(0, 1, 0))


def over_core(value):
    return lax.ppermute(value, "dp", dp_route(0, 0, 1))


def over_y(value, step):
    return lax.ppermute(value, "tensor", tensor_route(0, step))


def over_zl(value):
    return lax.ppermute(value, "tensor", tensor_route(1, 0))


def gather_small(value, axis):
    n = lax.axis_size(axis)
    copies = jnp.broadcast_to(value[None], (n,) + value.shape)
    return lax.all_to_all(copies, axis, 0, 0)


def layer_dot_kernel(plan_ref, hidden_ref, weight_ref, *refs):
    *out_refs, total_ref = refs
    lanes = out_refs[0].shape[-1]
    flip = plan_ref[0] == 1
    total_ref[...] = jnp.dot(hidden_ref[...], weight_ref[...], preferred_element_type=f32)
    for c in range(len(out_refs) // 2):
        same_ref, other_ref = out_refs[2 * c : 2 * c + 2]
        start = pl.multiple_of(plan_ref[1 + c] * 2 * lanes, 2 * lanes)
        pair = total_ref[:, pl.ds(start, 2 * lanes)]
        first, second = pair[:, :lanes], pair[:, lanes:]
        same_ref[0] = jnp.where(flip, second, first).astype(same_ref.dtype)
        other_ref[0] = jnp.where(flip, first, second).astype(other_ref.dtype)


def layer_dot(hidden, weight, columns, zl, group, dtypes):
    tokens, units = hidden.shape
    model_width = weight.shape[1]
    lanes = model_width // (NX * group)
    out = pl.BlockSpec((1, tokens, lanes), lambda b, s: (b, 0, 0))
    return pl.pallas_call(
        layer_dot_kernel,
        grid_spec=pltpu.PrefetchScalarGridSpec(
            num_scalar_prefetch=1,
            grid=(NX,),
            in_specs=[
                pl.BlockSpec((tokens, units), lambda b, s: (0, 0)),
                pl.BlockSpec((units, group * lanes), lambda b, s: (0, b)),
            ],
            out_specs=[out] * (2 * len(columns)),
            scratch_shapes=[pltpu.VMEM((tokens, group * lanes), f32)],
        ),
        out_shape=[
            jax.ShapeDtypeStruct((NX, tokens, lanes), dtype) for dtype in dtypes for _ in range(2)
        ],
        compiler_params=pltpu.CompilerParams(vmem_limit_bytes=56 * MIB),
        cost_estimate=pl.CostEstimate(
            flops=2 * tokens * units * model_width,
            bytes_accessed=2 * (tokens * units + units * model_width + tokens * model_width),
            transcendentals=0,
        ),
    )(jnp.stack([zl] + columns).astype(jnp.int32), hidden, weight)


def pair_picks(seqs):
    rows = lax.broadcasted_iota(jnp.int32, (seqs // 2, seqs), 0)
    cols = lax.broadcasted_iota(jnp.int32, (seqs // 2, seqs), 1)
    return (cols == 2 * rows).astype(f32), (cols == 2 * rows + 1).astype(f32)


def exact_dot(left, right, contract):
    return lax.dot_general(left, right, (contract, ((), ())), precision=highest, preferred_element_type=f32)


def gram_kernel(plan_ref, mean_ref, gain_ref, strip_ref, out_ref):
    seqs, width = mean_ref.shape
    pooled = mean_ref[...] * gain_ref[...]
    queries, passages = [exact_dot(pick, pooled, ((1,), (0,))) for pick in pair_picks(seqs)]
    dots = exact_dot(queries, passages, ((1,), (1,)))
    squares = exact_dot(jnp.ones((8, width), f32), pooled * pooled, ((1,), (1,)))
    out_ref[:seqs, :] = strip_ref[...]
    out_ref[seqs : seqs + 8, :] = jnp.concatenate([dots[8 * i : 8 * i + 8] for i in range(4)], axis=1)
    out_ref[seqs + 8 :, :] = jnp.concatenate([squares, jnp.zeros_like(squares)], axis=1)


def gram_part(means, gain, x):
    seqs, width = means.shape
    lanes = 2 * seqs
    return pl.pallas_call(
        gram_kernel,
        grid_spec=pltpu.PrefetchScalarGridSpec(
            num_scalar_prefetch=1,
            grid=(1,),
            in_specs=[
                pl.BlockSpec((seqs, width), lambda i, s: (0, 0)),
                pl.BlockSpec((1, width), lambda i, s: (0, 0)),
                pl.BlockSpec((seqs, lanes), lambda i, s: (0, s[0])),
            ],
            out_specs=pl.BlockSpec((seqs + 16, lanes), lambda i, s: (0, 0)),
        ),
        out_shape=jax.ShapeDtypeStruct((seqs + 16, lanes), f32),
        compiler_params=pltpu.CompilerParams(vmem_limit_bytes=16 * MIB),
        cost_estimate=QUICK,
    )(x.astype(jnp.int32).reshape(1), means, gain, means)


def contrast_kernel(
    plan_ref, part_ref, same_ref, gain_block_ref, mean_ref, gain_ref, block_ref, block_gain_ref, own_ref, gain_grad_ref
):
    group = part_ref.shape[0]
    seqs = mean_ref.shape[0]
    rows = lax.broadcasted_iota(jnp.int32, (seqs, seqs), 0)
    cols = lax.broadcasted_iota(jnp.int32, (seqs, seqs), 1)
    total = part_ref[0, seqs:, :]
    for r in range(1, group):
        total += part_ref[r, seqs:, :]
    half = seqs // 2
    dots = jnp.concatenate([total[:8, half * i : half * (i + 1)] for i in range(4)], axis=0)
    pick_query, pick_passage = pair_picks(seqs)
    gram = exact_dot(pick_query, exact_dot(dots, pick_passage, ((1,), (0,))), ((0,), (0,)))
    gram = gram + gram.T
    norm_row = jnp.sqrt(total[8:9, :seqs] + eps_embed)
    norm_col = row_to_column(norm_row)
    norms = norm_col * norm_row
    scores = score_scale * gram / norms
    query = rows % 2 == 0
    valid = query & (cols % 2 == 1) & (same_ref[...] > 0.5)
    weights = jnp.where(valid, jnp.exp(scores), 0.0)
    totals = jnp.sum(weights, axis=1, keepdims=True)
    soft = weights / jnp.where(totals > 0.0, totals, 1.0)
    target = jnp.where(query & (cols == rows + 1), 1.0, 0.0)
    d_score = loss_scale * (soft - target)
    both = d_score + d_score.T
    coef = jnp.sum(both * scores, axis=1, keepdims=True)
    mix = score_scale * both / norms - jnp.where(rows == cols, coef / (norm_col * norm_col), 0.0)
    mean, gain = mean_ref[...], gain_ref[...]
    d_pooled = jnp.dot(mix, mean * gain, precision=highest, preferred_element_type=f32)
    gain_grad_ref[...] = jnp.sum(d_pooled * mean, axis=0, keepdims=True)
    own_ref[...] = d_pooled * gain * (1.0 / SEQ)
    for place in range(group):
        part = part_ref[(place % NZL) * NY + place // NZL, :seqs, :]
        gain = gain_block_ref[0, place : place + 1, :]
        d_pooled = jnp.dot(mix, part * gain, precision=highest, preferred_element_type=f32)
        block_ref[place] = d_pooled * gain * (1.0 / SEQ)
        block_gain_ref[place : place + 1, :] = jnp.sum(d_pooled * part, axis=0, keepdims=True)


def contrast(parts, same, gain_blocks, means, gain, x):
    group, _, lanes = parts.shape
    seqs, width = means.shape
    whole = lambda shape: pl.BlockSpec(shape, lambda i, s: (0,) * len(shape))
    return pl.pallas_call(
        contrast_kernel,
        grid_spec=pltpu.PrefetchScalarGridSpec(
            num_scalar_prefetch=1,
            grid=(1,),
            in_specs=[
                whole(parts.shape),
                whole(same.shape),
                pl.BlockSpec((1, group, lanes), lambda i, s: (s[0], 0, 0)),
                whole(means.shape),
                whole(gain.shape),
            ],
            out_specs=[whole((group, seqs, lanes)), whole((group, lanes)), whole((seqs, width)), whole((1, width))],
        ),
        out_shape=(
            jax.ShapeDtypeStruct((group, seqs, lanes), f32),
            jax.ShapeDtypeStruct((group, lanes), f32),
            jax.ShapeDtypeStruct((seqs, width), f32),
            jax.ShapeDtypeStruct((1, width), f32),
        ),
        compiler_params=pltpu.CompilerParams(vmem_limit_bytes=16 * MIB),
        cost_estimate=QUICK,
    )(x.astype(jnp.int32).reshape(1), parts, same, gain_blocks, means, gain)


def row_to_column(row):
    n = row.shape[1]
    eye = lax.broadcasted_iota(jnp.int32, (n, n), 0) == lax.broadcasted_iota(jnp.int32, (n, n), 1)
    return jnp.sum(jnp.where(eye, jnp.broadcast_to(row, (n, n)), 0.0), axis=1, keepdims=True)


def column_to_row(column):
    n = column.shape[0]
    eye = lax.broadcasted_iota(jnp.int32, (n, n), 0) == lax.broadcasted_iota(jnp.int32, (n, n), 1)
    return jnp.sum(jnp.where(eye, jnp.broadcast_to(column, (n, n)), 0.0), axis=0, keepdims=True)


def strip_reader(refs):
    *refs, last = refs
    first_half = pl.program_id(0) < NX // 2

    def read(i, rows):
        value = refs[i][0, rows, :]
        if i == len(refs) - 1:
            value = jnp.where(first_half, value, last[0, rows, :])
        return value.astype(f32)

    return read


def strip_specs(strips):
    _, tokens, lanes = strips[0].shape
    half = NX // 2
    block = (1, tokens, lanes)
    return [pl.BlockSpec(block, lambda i, s: (i, 0, 0))] * (len(strips) - 2) + [
        pl.BlockSpec(block, lambda i, s: (jnp.minimum(i, half - 1), 0, 0)),
        pl.BlockSpec(block, lambda i, s: (jnp.maximum(i - half, 0), 0, 0)),
    ]


def along_kernel(plan_ref, *refs):
    *layer_refs, scaled_ref, out_ref = refs
    tokens = layer_refs[0].shape[1]
    group = len(layer_refs) - 1
    read = strip_reader(layer_refs)
    first = plan_ref[pl.program_id(0)]
    for s in range(tokens // SEQ):
        rows = slice(s * SEQ, (s + 1) * SEQ)
        along = None
        for i in range(group):
            scaled = scaled_ref[plan_ref[NX + i], pl.ds(first + s, 1), :]
            term = read(i, rows) * scaled
            along = term if along is None else along + term
        out_ref[0, s : s + 1, :] = column_to_row(jnp.sum(along, axis=1, keepdims=True))


def along_part(strips, scaled, plan):
    _, tokens, lanes = strips[0].shape
    group = len(strips) - 1
    seqs_here = tokens // SEQ
    return pl.pallas_call(
        along_kernel,
        grid_spec=pltpu.PrefetchScalarGridSpec(
            num_scalar_prefetch=1,
            grid=(NX,),
            in_specs=strip_specs(strips) + [pl.BlockSpec(scaled.shape, lambda i, s: (0, 0, 0))],
            out_specs=pl.BlockSpec((1, seqs_here, SEQ), lambda i, s: (s[NX + 3 * group + i], 0, 0)),
        ),
        out_shape=jax.ShapeDtypeStruct((NX, seqs_here, SEQ), f32),
        compiler_params=pltpu.CompilerParams(vmem_limit_bytes=16 * MIB),
        cost_estimate=QUICK,
    )(plan, *strips, scaled)


def group_grad_kernel(plan_ref, *refs):
    *layer_refs, scaled_ref, sum_ref, low_ref, coef_ref, factor_ref = refs
    _, tokens, lanes = layer_refs[0].shape
    group = len(layer_refs) - 1
    read = strip_reader(layer_refs)
    seqs_here = tokens // SEQ
    here = pl.program_id(0)
    first = plan_ref[here]

    @pl.when(here == 0)
    def _():
        for i in range(NX):
            position = plan_ref[NX + 3 * group + i]
            along, inverse = sum_ref[position], sum_ref[NX + position]
            coef = inverse * inverse * inverse * along / (NX * group * lanes)
            factor_ref[i, :seqs_here] = inverse
            factor_ref[i, seqs_here:] = coef
            if i == 0:
                coef_ref[...] = coef

    for s in range(seqs_here):
        rows = slice(s * SEQ, (s + 1) * SEQ)
        inverse = row_to_column(factor_ref[here, s : s + 1, :])
        coef = row_to_column(factor_ref[here, seqs_here + s : seqs_here + s + 1, :])
        for i in range(group):
            scaled = scaled_ref[plan_ref[NX + i], pl.ds(first + s, 1), :]
            low = inverse * scaled - read(i, rows) * coef
            side = pl.ds(pl.multiple_of(plan_ref[NX + 2 * group + i], lanes), lanes)
            low_ref[plan_ref[NX + group + i], rows, side] = low.astype(bf16)


def group_grad(strips, scaled, sums, plan):
    _, tokens, lanes = strips[0].shape
    group = len(strips) - 1
    quarter = group * lanes // 4
    seqs_here = tokens // SEQ
    return pl.pallas_call(
        group_grad_kernel,
        grid_spec=pltpu.PrefetchScalarGridSpec(
            num_scalar_prefetch=1,
            grid=(NX,),
            in_specs=strip_specs(strips)
            + [pl.BlockSpec(scaled.shape, lambda i, s: (0, 0, 0))]
            + [pl.BlockSpec(sums.shape, lambda i, s: (0, 0, 0))],
            out_specs=[
                pl.BlockSpec((4, tokens, quarter), lambda i, s: (0, i, 0)),
                pl.BlockSpec((seqs_here, SEQ), lambda i, s: (0, 0)),
            ],
            scratch_shapes=[pltpu.VMEM((NX, 2 * seqs_here, SEQ), f32)],
        ),
        out_shape=(
            jax.ShapeDtypeStruct((4, NX * tokens, quarter), bf16),
            jax.ShapeDtypeStruct((seqs_here, SEQ), f32),
        ),
        compiler_params=pltpu.CompilerParams(vmem_limit_bytes=24 * MIB),
        cost_estimate=QUICK,
    )(plan, *strips, scaled, sums)


def hidden_grad_kernel(plan_ref, *refs):
    refs, outs = refs[:-5], refs[-5:]
    out_ref, resid_ref, gain_ref, low_ref, gains_ref = outs
    *refs, scaled_ref, block_gain_ref, inverse_ref, coef_ref, weight_ref = refs
    tokens = out_ref.shape[0]
    seqs_here = tokens // SEQ
    group = len(refs) // 2
    row_refs, rest_ref, strip_refs = refs[:group], refs[group], refs[group + 1 :]
    others, _, lanes = refs[0].shape
    width = resid_ref.shape[1]
    rank, x, first = [plan_ref[2 * NX + 3 * group + i] for i in range(3)]

    @pl.when(pl.program_id(0) == 0)
    def _():
        factors = [
            [jnp.broadcast_to(row_to_column(ref[s : s + 1, :]), (SEQ, lanes)) for ref in (inverse_ref, coef_ref)]
            for s in range(seqs_here)
        ]
        for i in range(group):
            place = plan_ref[NX + i]
            row_ref, strip_ref = row_refs[i], strip_refs[i]
            last = i == group - 1
            tail_ref, tail_start = (rest_ref, tokens // 2) if last else (row_ref, tokens)
            for j in range(others + 1):
                block = lax.rem(x + j, others + 1)
                column = pl.ds(pl.multiple_of((block * group + place) * lanes, lanes), lanes)
                if j:
                    tail = tail_ref[j - 1, tail_start:, :].astype(f32)
                    tail = tail[:8] + tail[8:]
                    gains_ref[place, pl.ds(block, 1), :] = tail[seqs_here : seqs_here + 1]
                else:
                    gains_ref[place, pl.ds(block, 1), :] = block_gain_ref[pl.ds(place, 1), :]
                for s in range(seqs_here):
                    rows = slice(s * SEQ, (s + 1) * SEQ)
                    if j and last and 2 * s >= seqs_here:
                        rest = slice(rows.start - tokens // 2, rows.stop - tokens // 2)
                        layer, scaled = rest_ref[j - 1, rest, :], tail[s : s + 1]
                    elif j:
                        layer, scaled = row_ref[j - 1, rows, :], tail[s : s + 1]
                    else:
                        layer, scaled = strip_ref[0, rows, :], scaled_ref[place, pl.ds(first + s, 1), :]
                    inverse, coef = factors[s]
                    low_ref[rows, column] = (inverse * scaled - layer.astype(f32) * coef).astype(bf16)
        first_place = rank % 2 * (group // 2)
        for j in range(group // 2):
            gain_ref[j : j + 1, :] = gains_ref[first_place + j, pl.ds(rank // 2, 1), :]
        resid_ref[...] = low_ref[:, pl.ds(pl.multiple_of(rank * width, width), width)]

    out_ref[...] = lax.dot_general(
        low_ref[...], weight_ref[...], (((1,), (1,)), ((), ())), preferred_element_type=f32
    ).astype(out_ref.dtype)


def hidden_grad(rows, strips, scaled, block_gain, inverse, coef, weight, plan):
    others, height, lanes = rows[0].shape
    group = len(strips)
    seqs_here = inverse.shape[0]
    tokens = seqs_here * SEQ
    units, model_width = weight.shape
    chunk = units // GRAD_STEPS
    width = model_width // group
    whole = lambda shape: pl.BlockSpec(shape, lambda i, s: (0,) * len(shape))
    return pl.pallas_call(
        hidden_grad_kernel,
        grid_spec=pltpu.PrefetchScalarGridSpec(
            num_scalar_prefetch=1,
            grid=(GRAD_STEPS,),
            in_specs=[whole(row.shape) for row in rows]
            + [whole((1, tokens, lanes))] * group
            + [whole(v.shape) for v in (scaled, block_gain, inverse, coef)]
            + [pl.BlockSpec((chunk, model_width), lambda i, s: (i, 0))],
            out_specs=[
                pl.BlockSpec((tokens, chunk), lambda i, s: (0, i)),
                whole((tokens, width)),
                whole((group // 2, lanes)),
            ],
            scratch_shapes=[
                pltpu.VMEM((tokens, model_width), bf16),
                pltpu.VMEM((group, others + 1, lanes), f32),
            ],
        ),
        out_shape=(
            jax.ShapeDtypeStruct((tokens, units), bf16),
            jax.ShapeDtypeStruct((tokens, width), bf16),
            jax.ShapeDtypeStruct((group // 2, lanes), f32),
        ),
        compiler_params=pltpu.CompilerParams(vmem_limit_bytes=56 * MIB),
        cost_estimate=QUICK,
    )(plan, *rows, *strips, scaled, block_gain, inverse, coef, weight)


def tie(*values):
    return lax.optimization_barrier(values)


def gather_start(value):
    return {
        (0, 0): value,
        (1, 0): over_zl(value),
        (0, 1): over_y(value, -1),
        (0, 3): over_y(value, 1),
    }


def gather_next(got):
    got = dict(got)
    got[1, 1] = over_y(got[1, 0], -1)
    got[1, 3] = over_zl(got[0, 3])
    got[0, 2] = over_y(got[0, 3], 1)
    return got


def gather_last(got, cut):
    got = dict(got)
    got[1, 2] = over_y(got[1, 1][:, :cut], -1)
    got["rest"] = over_y(got[1, 3][:, cut:], 1)
    return got


def tie_gather(got, *values):
    keys = list(got)
    tied = tie(*got.values(), *values)
    return (dict(zip(keys, tied)),) + tuple(tied[len(keys) :])


def per_device(resid, hidden, down_weight, gain, domain_ids):
    tokens, units = hidden.shape
    model_width = down_weight.shape[1]
    group = lax.axis_size("tensor")
    shards = lax.axis_size("dp")
    width = model_width // group
    lanes = width // NX
    seqs_here = tokens // SEQ
    seqs = seqs_here * shards
    rank = lax.axis_index("tensor")
    zl, y = rank // NY, rank % NY
    place = y * NZL + zl
    shard = lax.axis_index("dp")
    x, zh, core = shard // (NZH * NCORE), (shard // NCORE) % NZH, shard % NCORE

    def place_of(part, step):
        return ((y + step) % NY) * NZL + (zl + part) % NZL

    with jax.named_scope("tables"):
        owner = jnp.repeat(domain_ids, seqs_here)
        same = (owner[:, None] == owner[None, :]).astype(f32)
        gain_blocks = gain.reshape(NX, group, lanes)
        gain_own = lax.dynamic_slice_in_dim(gain_blocks, place, 1, 1).reshape(1, width)
        peers = [((x + step) % NX) * (NZH * NCORE) + zh * NCORE + core for step in (0, -1, 1, 2)]
        places = [place_of(*key) for key in KEYS]
        plan = [p * seqs_here for p in peers] + places
        plan += [(p // 2) ^ (zh * NCORE + core) for p in places] + [p % 2 * lanes for p in places]
        plan += [(x + step) % NX for step in (0, -1, 1, 2)]
        plan += [rank, x, shard * seqs_here]
        plan = jnp.stack([jnp.asarray(v, jnp.int32) for v in plan])

    with jax.named_scope("hidden_exchange"):
        hidden_left = over_x(hidden, 1)
        hidden_right = over_x(hidden, -1)
        hidden_far = over_x(hidden, 2)

    with jax.named_scope("resid_exchange"):
        pieces = resid.reshape(tokens, 2, NZL, lanes).transpose(2, 1, 0, 3)[:, None]
        pieces = jnp.broadcast_to(pieces, (NZL, NY // 2, 2, tokens, lanes))
        pieces = lax.all_to_all(pieces.reshape(group, tokens, lanes), "tensor", 0, 0)
        pieces = pieces.reshape(NX, 2, tokens, lanes)

    with jax.named_scope("layer_sum"):
        def dot_for(steps, dtypes):
            columns = [(y + step) % NY for step in steps]
            return layer_dot(hidden, down_weight, columns, zl, group, dtypes)

        *sums, pieces = tie(*dot_for((2, 1, 3, 0), (bf16, bf16, bf16, f32)), pieces)
        term = dict(zip([(part, step) for step in (2, 1, 3, 0) for part in (0, 1)], sums))

        def add(*values):
            return sum(value.astype(f32) for value in values)

        from_12 = over_y(term[1, 2], -1)
        from_11 = over_y(term[1, 1], 1)
        from_02 = over_y(term[0, 2], 1)
        from_12, from_11, hidden_left, hidden_right = tie(from_12, from_11, hidden_left, hidden_right)
        from_13 = over_zl(add(term[1, 3], from_12).astype(bf16))
        own_other = add(term[1, 0], from_11).astype(bf16)
        from_13, from_02 = tie(from_13, from_02)
        from_03 = over_y(add(term[0, 3], from_13).astype(bf16), -1)
        from_01 = over_y(add(term[0, 1], from_02).astype(bf16), 1)
        from_10 = over_zl(own_other)
        from_03, from_10, from_01 = tie(from_03, from_10, from_01)
        resid_strips = lax.dynamic_slice_in_dim(pieces, y // 2, 1, 1)[:, 0]
        layer = add(term[0, 0], resid_strips, from_01, from_03, from_10)

    with jax.named_scope("strip_exchange"):
        low_layer = layer.astype(bf16)
        strips_x = [lax.dynamic_slice_in_dim(low_layer, x, 1, 0)]
        for step in (1, -1, 2):
            strip = lax.dynamic_slice_in_dim(low_layer, (x + step) % NX, 1, 0)
            strips_x.append(over_x(strip, step))
        message = jnp.concatenate(strips_x, axis=0)

    with jax.named_scope("norm"):
        squares = jnp.sum(layer * layer, axis=(0, 2)).reshape(seqs_here, SEQ)
        squares = jnp.sum(gather_small(squares, "tensor"), axis=0)
        message, squares, hidden_far = tie(message, squares, hidden_far)
        hidden_rows = jnp.concatenate([hidden, hidden_left, hidden_right, hidden_far], axis=0)
        got = gather_start(message)
        inverse = lax.rsqrt(squares / model_width + eps_norm)
        weighted = layer.reshape(NX, seqs_here, SEQ, lanes) * inverse[None, :, :, None]
        means = jnp.mean(weighted, axis=2).transpose(1, 0, 2).reshape(seqs_here, width)

    with jax.named_scope("contrast"):
        means_all = gather_small(means, "dp")
        got, means_all = tie_gather(got, means_all)
        got = gather_next(got)
        means_all = means_all.reshape(seqs, width)
        parts = gather_small(gram_part(means_all, gain_own, x), "tensor")
        row_blocks = jnp.concatenate([low_layer, low_layer], axis=0)
        row_blocks = lax.dynamic_slice_in_dim(row_blocks, x + 1, NX - 1, 0)
        row_blocks = jnp.pad(row_blocks, ((0, 0), (0, 16), (0, 0)))
        got, parts, row_blocks, hidden_rows = tie_gather(got, parts, row_blocks, hidden_rows)
        half = NX // 2
        got[1, 2] = over_y(got[1, 1][:half], -1)
        strips = [got[key] for key in KEYS] + [over_y(got[1, 3][half:], 1)]
        scaled, gain_grad_x, scaled_own, gain_grad = contrast(
            parts, same, gain_blocks, means_all, gain_own, x
        )

    with jax.named_scope("row_gather"):
        own_rows = lax.dynamic_slice_in_dim(scaled_own, shard * seqs_here, seqs_here, 0)
        own_rows = jnp.pad(jnp.concatenate([own_rows, gain_grad], axis=0), ((0, 8 - seqs_here - 1), (0, 0)))
        high = lax.reduce_precision(own_rows, exponent_bits=8, mantissa_bits=7)
        tail = jnp.concatenate([high, own_rows - high], axis=0).astype(bf16)
        tail = tail.reshape(16, NX, lanes).transpose(1, 0, 2)
        tail = lax.dynamic_slice_in_dim(jnp.concatenate([tail, tail], axis=0), x + 1, NX - 1, 0)
        rows = gather_start(lax.dynamic_update_slice(row_blocks, tail, (0, tokens, 0)))

    with jax.named_scope("along"):
        own_inverse = jnp.where(jnp.arange(NX)[:, None, None] == x, inverse[None], 0.0)
        sums = jnp.concatenate([along_part(strips, scaled, plan), own_inverse], axis=0)
        sums = sums + lax.ppermute(sums, "dp", swap_route(1))
        rows, sums = tie_gather(rows, sums)
        rows = gather_next(rows)
        sums = sums + lax.ppermute(sums, "dp", swap_route(2))

    with jax.named_scope("down_grad"):
        low_x, coef = group_grad(strips, scaled, sums, plan)
        rows, low_x = tie_gather(rows, low_x)
        rows = gather_last(rows, tokens // 2)

        def down(low):
            return lax.dot_general(
                hidden_rows, low, (((0,), (0,)), ((), ())), preferred_element_type=f32
            )

        part3, low_x = tie(down(low_x[3]), low_x)
        part1, low_x = tie(down(low_x[1]), low_x)
        from_core = over_core(part3), over_core(part1)
        summed = (down(low_x[2]) + from_core[0]).astype(bf16)
        summed, low0 = tie(summed, low_x[0])
        across = over_zh(summed)
        rows, low0 = tie_gather(rows, low0)
        near = down(low0) + from_core[1]

    with jax.named_scope("hidden_grad"):
        rows, near = tie_gather(rows, near)
        rows = [rows[key] for key in KEYS + ("rest",)]
        grad_hidden, grad_resid, gain_grad = hidden_grad(
            rows, strips[:group], scaled, gain_grad_x, inverse, coef, down_weight, plan
        )
        grad_gain = gain_grad.reshape(width)

    with jax.named_scope("down_grad"):
        across, grad_hidden = tie(across, grad_hidden)
        grad_down = near + across.astype(f32)

    return (grad_hidden, grad_resid, grad_down, grad_gain)


def solution(mesh):
    return jax.shard_map(
        per_device,
        mesh=mesh,
        in_specs=(P("dp", "tensor"), P("dp", "tensor"), P("tensor", None), P(), P()),
        out_specs=(P("dp", "tensor"), P("dp", "tensor"), P("tensor", "dp"), P("tensor")),
        check_vma=False,
    )
```

```python
import functools
import jax
import jax.numpy as jnp
from jax import lax
from jax.experimental import pallas as pl
from jax.experimental.pallas import tpu as pltpu
from jax.sharding import PartitionSpec as P

SEQ = 128
NX, NZH, NCORE, NZL, NY = 4, 2, 2, 2, 4
GRAD_STEPS = 7
KEYS = ((0, 0), (1, 0), (0, 1), (0, 3), (0, 2), (1, 1), (1, 3), (1, 2))

score_scale = 20.0
loss_scale = 8192.0
eps_norm = 1e-05
eps_embed = 1e-06
highest = lax.Precision.HIGHEST
f32 = jnp.float32
bf16 = jnp.bfloat16
MIB = 1024 * 1024
QUICK = pl.CostEstimate(flops=1024, bytes_accessed=1024, transcendentals=0)


def dp_route(dx, dz, dc):
    pairs = []
    for x in range(NX):
        for z in range(NZH):
            for c in range(NCORE):
                to = (((x + dx) % NX) * NZH + (z + dz) % NZH) * NCORE + (c + dc) % NCORE
                pairs.append(((x * NZH + z) * NCORE + c, to))
    return pairs


def tensor_route(dz, dy):
    pairs = []
    for z in range(NZL):
        for y in range(NY):
            pairs.append((z * NY + y, ((z + dz) % NZL) * NY + (y + dy) % NY))
    return pairs


def swap_route(bit):
    size = NZH * NCORE
    return [(d, (d // size ^ bit) * size + d % size) for d in range(NX * size)]


def over_x(value, step):
    return lax.ppermute(value, "dp", dp_route(step, 0, 0))


def over_zh(value):
    return lax.ppermute(value, "dp", dp_route(0, 1, 0))


def over_core(value):
    return lax.ppermute(value, "dp", dp_route(0, 0, 1))


def over_y(value, step):
    return lax.ppermute(value, "tensor", tensor_route(0, step))


def over_zl(value):
    return lax.ppermute(value, "tensor", tensor_route(1, 0))


def gather_small(value, axis):
    n = lax.axis_size(axis)
    copies = jnp.broadcast_to(value[None], (n,) + value.shape)
    return lax.all_to_all(copies, axis, 0, 0)


def layer_dot_kernel(plan_ref, hidden_ref, weight_ref, *refs):
    *out_refs, total_ref = refs
    lanes = out_refs[0].shape[-1]
    flip = plan_ref[0] == 1
    total_ref[...] = jnp.dot(hidden_ref[...], weight_ref[...], preferred_element_type=f32)
    for c in range(len(out_refs) // 2):
        same_ref, other_ref = out_refs[2 * c : 2 * c + 2]
        start = pl.multiple_of(plan_ref[1 + c] * 2 * lanes, 2 * lanes)
        pair = total_ref[:, pl.ds(start, 2 * lanes)]
        first, second = pair[:, :lanes], pair[:, lanes:]
        same_ref[0] = jnp.where(flip, second, first).astype(same_ref.dtype)
        other_ref[0] = jnp.where(flip, first, second).astype(other_ref.dtype)


def layer_dot(hidden, weight, columns, zl, group, dtypes):
    tokens, units = hidden.shape
    model_width = weight.shape[1]
    lanes = model_width // (NX * group)
    out = pl.BlockSpec((1, tokens, lanes), lambda b, s: (b, 0, 0))
    return pl.pallas_call(
        layer_dot_kernel,
        grid_spec=pltpu.PrefetchScalarGridSpec(
            num_scalar_prefetch=1,
            grid=(NX,),
            in_specs=[
                pl.BlockSpec((tokens, units), lambda b, s: (0, 0)),
                pl.BlockSpec((units, group * lanes), lambda b, s: (0, b)),
            ],
            out_specs=[out] * (2 * len(columns)),
            scratch_shapes=[pltpu.VMEM((tokens, group * lanes), f32)],
        ),
        out_shape=[
            jax.ShapeDtypeStruct((NX, tokens, lanes), dtype) for dtype in dtypes for _ in range(2)
        ],
        compiler_params=pltpu.CompilerParams(vmem_limit_bytes=56 * MIB),
        cost_estimate=pl.CostEstimate(
            flops=2 * tokens * units * model_width,
            bytes_accessed=2 * (tokens * units + units * model_width + tokens * model_width),
            transcendentals=0,
        ),
    )(jnp.stack([zl] + columns).astype(jnp.int32), hidden, weight)


def pair_picks(seqs):
    rows = lax.broadcasted_iota(jnp.int32, (seqs // 2, seqs), 0)
    cols = lax.broadcasted_iota(jnp.int32, (seqs // 2, seqs), 1)
    return (cols == 2 * rows).astype(f32), (cols == 2 * rows + 1).astype(f32)


def exact_dot(left, right, contract):
    return lax.dot_general(left, right, (contract, ((), ())), precision=highest, preferred_element_type=f32)


def cut_kernel(slab_ref, out_ref):
    lanes = out_ref.shape[-1]
    for r in range(out_ref.shape[0]):
        j = r % NY % 2 * 2 + r // NY
        out_ref[r] = slab_ref[:, j * lanes : (j + 1) * lanes]


def cut_strips(slab, group):
    tokens, width = slab.shape
    return pl.pallas_call(
        cut_kernel,
        out_shape=jax.ShapeDtypeStruct((group, tokens, width // NX), slab.dtype),
        compiler_params=pltpu.CompilerParams(vmem_limit_bytes=16 * MIB),
        cost_estimate=QUICK,
    )(slab)


def gram_kernel(plan_ref, mean_ref, gain_ref, strip_ref, out_ref):
    seqs, width = mean_ref.shape
    pooled = mean_ref[...] * gain_ref[...]
    queries, passages = [exact_dot(pick, pooled, ((1,), (0,))) for pick in pair_picks(seqs)]
    dots = exact_dot(queries, passages, ((1,), (1,)))
    squares = exact_dot(jnp.ones((8, width), f32), pooled * pooled, ((1,), (1,)))
    out_ref[:seqs, :] = strip_ref[...]
    out_ref[seqs : seqs + 8, :] = jnp.concatenate([dots[8 * i : 8 * i + 8] for i in range(4)], axis=1)
    out_ref[seqs + 8 :, :] = jnp.concatenate([squares, jnp.zeros_like(squares)], axis=1)


def gram_part(means, gain, x):
    seqs, width = means.shape
    lanes = 2 * seqs
    return pl.pallas_call(
        gram_kernel,
        grid_spec=pltpu.PrefetchScalarGridSpec(
            num_scalar_prefetch=1,
            grid=(1,),
            in_specs=[
                pl.BlockSpec((seqs, width), lambda i, s: (0, 0)),
                pl.BlockSpec((1, width), lambda i, s: (0, 0)),
                pl.BlockSpec((seqs, lanes), lambda i, s: (0, s[0])),
            ],
            out_specs=pl.BlockSpec((seqs + 16, lanes), lambda i, s: (0, 0)),
        ),
        out_shape=jax.ShapeDtypeStruct((seqs + 16, lanes), f32),
        compiler_params=pltpu.CompilerParams(vmem_limit_bytes=16 * MIB),
        cost_estimate=QUICK,
    )(x.astype(jnp.int32).reshape(1), means, gain, means)


def contrast_kernel(
    plan_ref, part_ref, same_ref, gain_block_ref, mean_ref, gain_ref, block_ref, block_gain_ref, own_ref, gain_grad_ref
):
    group = part_ref.shape[0]
    seqs = mean_ref.shape[0]
    rows = lax.broadcasted_iota(jnp.int32, (seqs, seqs), 0)
    cols = lax.broadcasted_iota(jnp.int32, (seqs, seqs), 1)
    total = part_ref[0, seqs:, :]
    for r in range(1, group):
        total += part_ref[r, seqs:, :]
    half = seqs // 2
    dots = jnp.concatenate([total[:8, half * i : half * (i + 1)] for i in range(4)], axis=0)
    pick_query, pick_passage = pair_picks(seqs)
    gram = exact_dot(pick_query, exact_dot(dots, pick_passage, ((1,), (0,))), ((0,), (0,)))
    gram = gram + gram.T
    norm_row = jnp.sqrt(total[8:9, :seqs] + eps_embed)
    norm_col = row_to_column(norm_row)
    norms = norm_col * norm_row
    scores = score_scale * gram / norms
    query = rows % 2 == 0
    valid = query & (cols % 2 == 1) & (same_ref[...] > 0.5)
    weights = jnp.where(valid, jnp.exp(scores), 0.0)
    totals = jnp.sum(weights, axis=1, keepdims=True)
    soft = weights / jnp.where(totals > 0.0, totals, 1.0)
    target = jnp.where(query & (cols == rows + 1), 1.0, 0.0)
    d_score = loss_scale * (soft - target)
    both = d_score + d_score.T
    coef = jnp.sum(both * scores, axis=1, keepdims=True)
    mix = score_scale * both / norms - jnp.where(rows == cols, coef / (norm_col * norm_col), 0.0)
    mean, gain = mean_ref[...], gain_ref[...]
    d_pooled = jnp.dot(mix, mean * gain, precision=highest, preferred_element_type=f32)
    gain_grad_ref[...] = jnp.sum(d_pooled * mean, axis=0, keepdims=True)
    own_ref[...] = d_pooled * gain * (1.0 / SEQ)
    for place in range(group):
        part = part_ref[(place % NZL) * NY + place // NZL, :seqs, :]
        gain = gain_block_ref[0, place : place + 1, :]
        d_pooled = jnp.dot(mix, part * gain, precision=highest, preferred_element_type=f32)
        block_ref[place] = d_pooled * gain * (1.0 / SEQ)
        block_gain_ref[place : place + 1, :] = jnp.sum(d_pooled * part, axis=0, keepdims=True)


def contrast(parts, same, gain_blocks, means, gain, x):
    group, _, lanes = parts.shape
    seqs, width = means.shape
    whole = lambda shape: pl.BlockSpec(shape, lambda i, s: (0,) * len(shape))
    return pl.pallas_call(
        contrast_kernel,
        grid_spec=pltpu.PrefetchScalarGridSpec(
            num_scalar_prefetch=1,
            grid=(1,),
            in_specs=[
                whole(parts.shape),
                whole(same.shape),
                pl.BlockSpec((1, group, lanes), lambda i, s: (s[0], 0, 0)),
                whole(means.shape),
                whole(gain.shape),
            ],
            out_specs=[whole((group, seqs, lanes)), whole((group, lanes)), whole((seqs, width)), whole((1, width))],
        ),
        out_shape=(
            jax.ShapeDtypeStruct((group, seqs, lanes), f32),
            jax.ShapeDtypeStruct((group, lanes), f32),
            jax.ShapeDtypeStruct((seqs, width), f32),
            jax.ShapeDtypeStruct((1, width), f32),
        ),
        compiler_params=pltpu.CompilerParams(vmem_limit_bytes=16 * MIB),
        cost_estimate=QUICK,
    )(x.astype(jnp.int32).reshape(1), parts, same, gain_blocks, means, gain)


def row_to_column(row):
    n = row.shape[1]
    eye = lax.broadcasted_iota(jnp.int32, (n, n), 0) == lax.broadcasted_iota(jnp.int32, (n, n), 1)
    return jnp.sum(jnp.where(eye, jnp.broadcast_to(row, (n, n)), 0.0), axis=1, keepdims=True)


def column_to_row(column):
    n = column.shape[0]
    eye = lax.broadcasted_iota(jnp.int32, (n, n), 0) == lax.broadcasted_iota(jnp.int32, (n, n), 1)
    return jnp.sum(jnp.where(eye, jnp.broadcast_to(column, (n, n)), 0.0), axis=0, keepdims=True)


def strip_reader(refs):
    *refs, last = refs
    first_half = pl.program_id(0) < NX // 2

    def read(i, rows):
        value = refs[i][0, rows, :]
        if i == len(refs) - 1:
            value = jnp.where(first_half, value, last[0, rows, :])
        return value.astype(f32)

    return read


def strip_specs(strips):
    _, tokens, lanes = strips[0].shape
    half = NX // 2
    block = (1, tokens, lanes)
    return [pl.BlockSpec(block, lambda i, s: (i, 0, 0))] * (len(strips) - 2) + [
        pl.BlockSpec(block, lambda i, s: (jnp.minimum(i, half - 1), 0, 0)),
        pl.BlockSpec(block, lambda i, s: (jnp.maximum(i - half, 0), 0, 0)),
    ]


def along_kernel(plan_ref, *refs):
    *layer_refs, scaled_ref, out_ref = refs
    tokens = layer_refs[0].shape[1]
    group = len(layer_refs) - 1
    read = strip_reader(layer_refs)
    first = plan_ref[pl.program_id(0)]
    for s in range(tokens // SEQ):
        rows = slice(s * SEQ, (s + 1) * SEQ)
        along = None
        for i in range(group):
            scaled = scaled_ref[plan_ref[NX + i], pl.ds(first + s, 1), :]
            term = read(i, rows) * scaled
            along = term if along is None else along + term
        out_ref[0, s : s + 1, :] = column_to_row(jnp.sum(along, axis=1, keepdims=True))


def along_part(strips, scaled, plan):
    _, tokens, lanes = strips[0].shape
    group = len(strips) - 1
    seqs_here = tokens // SEQ
    return pl.pallas_call(
        along_kernel,
        grid_spec=pltpu.PrefetchScalarGridSpec(
            num_scalar_prefetch=1,
            grid=(NX,),
            in_specs=strip_specs(strips) + [pl.BlockSpec(scaled.shape, lambda i, s: (0, 0, 0))],
            out_specs=pl.BlockSpec((1, seqs_here, SEQ), lambda i, s: (s[NX + 3 * group + i], 0, 0)),
        ),
        out_shape=jax.ShapeDtypeStruct((NX, seqs_here, SEQ), f32),
        compiler_params=pltpu.CompilerParams(vmem_limit_bytes=16 * MIB),
        cost_estimate=QUICK,
    )(plan, *strips, scaled)


def group_grad_kernel(plan_ref, *refs):
    *layer_refs, scaled_ref, sum_ref, low_ref, coef_ref, factor_ref = refs
    _, tokens, lanes = layer_refs[0].shape
    group = len(layer_refs) - 1
    read = strip_reader(layer_refs)
    seqs_here = tokens // SEQ
    here = pl.program_id(0)
    first = plan_ref[here]

    @pl.when(here == 0)
    def _():
        for i in range(NX):
            position = plan_ref[NX + 3 * group + i]
            along, inverse = sum_ref[position], sum_ref[NX + position]
            coef = inverse * inverse * inverse * along / (NX * group * lanes)
            factor_ref[i, :seqs_here] = inverse
            factor_ref[i, seqs_here:] = coef
            if i == 0:
                coef_ref[...] = coef

    for s in range(seqs_here):
        rows = slice(s * SEQ, (s + 1) * SEQ)
        inverse = row_to_column(factor_ref[here, s : s + 1, :])
        coef = row_to_column(factor_ref[here, seqs_here + s : seqs_here + s + 1, :])
        for i in range(group):
            scaled = scaled_ref[plan_ref[NX + i], pl.ds(first + s, 1), :]
            low = inverse * scaled - read(i, rows) * coef
            side = pl.ds(pl.multiple_of(plan_ref[NX + 2 * group + i], lanes), lanes)
            low_ref[plan_ref[NX + group + i], rows, side] = low.astype(bf16)


def group_grad(strips, scaled, sums, plan):
    _, tokens, lanes = strips[0].shape
    group = len(strips) - 1
    quarter = group * lanes // 4
    seqs_here = tokens // SEQ
    return pl.pallas_call(
        group_grad_kernel,
        grid_spec=pltpu.PrefetchScalarGridSpec(
            num_scalar_prefetch=1,
            grid=(NX,),
            in_specs=strip_specs(strips)
            + [pl.BlockSpec(scaled.shape, lambda i, s: (0, 0, 0))]
            + [pl.BlockSpec(sums.shape, lambda i, s: (0, 0, 0))],
            out_specs=[
                pl.BlockSpec((4, tokens, quarter), lambda i, s: (0, i, 0)),
                pl.BlockSpec((seqs_here, SEQ), lambda i, s: (0, 0)),
            ],
            scratch_shapes=[pltpu.VMEM((NX, 2 * seqs_here, SEQ), f32)],
        ),
        out_shape=(
            jax.ShapeDtypeStruct((4, NX * tokens, quarter), bf16),
            jax.ShapeDtypeStruct((seqs_here, SEQ), f32),
        ),
        compiler_params=pltpu.CompilerParams(vmem_limit_bytes=24 * MIB),
        cost_estimate=QUICK,
    )(plan, *strips, scaled, sums)


def hidden_grad_kernel(plan_ref, *refs):
    refs, outs = refs[:-5], refs[-5:]
    out_ref, resid_ref, gain_ref, low_ref, gains_ref = outs
    *refs, scaled_ref, block_gain_ref, inverse_ref, coef_ref, weight_ref = refs
    tokens = out_ref.shape[0]
    seqs_here = tokens // SEQ
    group = len(refs) // 2
    row_refs, rest_ref, strip_refs = refs[:group], refs[group], refs[group + 1 :]
    others, _, lanes = refs[0].shape
    width = resid_ref.shape[1]
    rank, x, first = [plan_ref[2 * NX + 3 * group + i] for i in range(3)]

    @pl.when(pl.program_id(0) == 0)
    def _():
        factors = [
            [jnp.broadcast_to(row_to_column(ref[s : s + 1, :]), (SEQ, lanes)) for ref in (inverse_ref, coef_ref)]
            for s in range(seqs_here)
        ]
        for i in range(group):
            place = plan_ref[NX + i]
            row_ref, strip_ref = row_refs[i], strip_refs[i]
            last = i == group - 1
            tail_ref, tail_start = (rest_ref, tokens // 2) if last else (row_ref, tokens)
            for j in range(others + 1):
                block = lax.rem(x + j, others + 1)
                column = pl.ds(pl.multiple_of((block * group + place) * lanes, lanes), lanes)
                if j:
                    tail = tail_ref[j - 1, tail_start:, :].astype(f32)
                    tail = tail[:8] + tail[8:]
                    gains_ref[place, pl.ds(block, 1), :] = tail[seqs_here : seqs_here + 1]
                else:
                    gains_ref[place, pl.ds(block, 1), :] = block_gain_ref[pl.ds(place, 1), :]
                for s in range(seqs_here):
                    rows = slice(s * SEQ, (s + 1) * SEQ)
                    if j and last and 2 * s >= seqs_here:
                        rest = slice(rows.start - tokens // 2, rows.stop - tokens // 2)
                        layer, scaled = rest_ref[j - 1, rest, :], tail[s : s + 1]
                    elif j:
                        layer, scaled = row_ref[j - 1, rows, :], tail[s : s + 1]
                    else:
                        layer, scaled = strip_ref[0, rows, :], scaled_ref[place, pl.ds(first + s, 1), :]
                    inverse, coef = factors[s]
                    low_ref[rows, column] = (inverse * scaled - layer.astype(f32) * coef).astype(bf16)
        first_place = rank % 2 * (group // 2)
        for j in range(group // 2):
            gain_ref[j : j + 1, :] = gains_ref[first_place + j, pl.ds(rank // 2, 1), :]
        resid_ref[...] = low_ref[:, pl.ds(pl.multiple_of(rank * width, width), width)]

    out_ref[...] = lax.dot_general(
        low_ref[...], weight_ref[...], (((1,), (1,)), ((), ())), preferred_element_type=f32
    ).astype(out_ref.dtype)


def hidden_grad(rows, strips, scaled, block_gain, inverse, coef, weight, plan):
    others, height, lanes = rows[0].shape
    group = len(strips)
    seqs_here = inverse.shape[0]
    tokens = seqs_here * SEQ
    units, model_width = weight.shape
    chunk = units // GRAD_STEPS
    width = model_width // group
    whole = lambda shape: pl.BlockSpec(shape, lambda i, s: (0,) * len(shape))
    return pl.pallas_call(
        hidden_grad_kernel,
        grid_spec=pltpu.PrefetchScalarGridSpec(
            num_scalar_prefetch=1,
            grid=(GRAD_STEPS,),
            in_specs=[whole(row.shape) for row in rows]
            + [whole((1, tokens, lanes))] * group
            + [whole(v.shape) for v in (scaled, block_gain, inverse, coef)]
            + [pl.BlockSpec((chunk, model_width), lambda i, s: (i, 0))],
            out_specs=[
                pl.BlockSpec((tokens, chunk), lambda i, s: (0, i)),
                whole((tokens, width)),
                whole((group // 2, lanes)),
            ],
            scratch_shapes=[
                pltpu.VMEM((tokens, model_width), bf16),
                pltpu.VMEM((group, others + 1, lanes), f32),
            ],
        ),
        out_shape=(
            jax.ShapeDtypeStruct((tokens, units), bf16),
            jax.ShapeDtypeStruct((tokens, width), bf16),
            jax.ShapeDtypeStruct((group // 2, lanes), f32),
        ),
        compiler_params=pltpu.CompilerParams(vmem_limit_bytes=56 * MIB),
        cost_estimate=QUICK,
    )(plan, *rows, *strips, scaled, block_gain, inverse, coef, weight)


def tie(*values):
    return lax.optimization_barrier(values)


def gather_start(value):
    return {
        (0, 0): value,
        (1, 0): over_zl(value),
        (0, 1): over_y(value, -1),
        (0, 3): over_y(value, 1),
    }


def gather_next(got):
    got = dict(got)
    got[1, 1] = over_y(got[1, 0], -1)
    got[1, 3] = over_zl(got[0, 3])
    got[0, 2] = over_y(got[0, 3], 1)
    return got


def gather_last(got, cut):
    got = dict(got)
    got[1, 2] = over_y(got[1, 1][:, :cut], -1)
    got["rest"] = over_y(got[1, 3][:, cut:], 1)
    return got


def tie_gather(got, *values):
    keys = list(got)
    tied = tie(*got.values(), *values)
    return (dict(zip(keys, tied)),) + tuple(tied[len(keys) :])


def per_device(resid, hidden, down_weight, gain, domain_ids):
    tokens, units = hidden.shape
    model_width = down_weight.shape[1]
    group = lax.axis_size("tensor")
    shards = lax.axis_size("dp")
    width = model_width // group
    lanes = width // NX
    seqs_here = tokens // SEQ
    seqs = seqs_here * shards
    rank = lax.axis_index("tensor")
    zl, y = rank // NY, rank % NY
    place = y * NZL + zl
    shard = lax.axis_index("dp")
    x, zh, core = shard // (NZH * NCORE), (shard // NCORE) % NZH, shard % NCORE

    def place_of(part, step):
        return ((y + step) % NY) * NZL + (zl + part) % NZL

    with jax.named_scope("tables"):
        owner = jnp.repeat(domain_ids, seqs_here)
        same = (owner[:, None] == owner[None, :]).astype(f32)
        gain_blocks = gain.reshape(NX, group, lanes)
        gain_own = lax.dynamic_slice_in_dim(gain_blocks, place, 1, 1).reshape(1, width)
        peers = [((x + step) % NX) * (NZH * NCORE) + zh * NCORE + core for step in (0, -1, 1, 2)]
        places = [place_of(*key) for key in KEYS]
        plan = [p * seqs_here for p in peers] + places
        plan += [(p // 2) ^ (zh * NCORE + core) for p in places] + [p % 2 * lanes for p in places]
        plan += [(x + step) % NX for step in (0, -1, 1, 2)]
        plan += [rank, x, shard * seqs_here]
        plan = jnp.stack([jnp.asarray(v, jnp.int32) for v in plan])

    with jax.named_scope("hidden_exchange"):
        hidden_left = over_x(hidden, 1)
        hidden_right = over_x(hidden, -1)
        hidden_far = over_x(hidden, 2)

    with jax.named_scope("resid_exchange"):
        pieces = lax.all_to_all(cut_strips(resid, group), "tensor", 0, 0)
        pieces = pieces.reshape(NX, 2, tokens, lanes)

    with jax.named_scope("layer_sum"):
        def dot_for(steps, dtypes):
            columns = [(y + step) % NY for step in steps]
            return layer_dot(hidden, down_weight, columns, zl, group, dtypes)

        *sums, pieces = tie(*dot_for((2, 1, 3, 0), (bf16, bf16, bf16, f32)), pieces)
        term = dict(zip([(part, step) for step in (2, 1, 3, 0) for part in (0, 1)], sums))

        def add(*values):
            return sum(value.astype(f32) for value in values)

        from_12 = over_y(term[1, 2], -1)
        from_11 = over_y(term[1, 1], 1)
        from_02 = over_y(term[0, 2], 1)
        from_12, from_11, hidden_left, hidden_right = tie(from_12, from_11, hidden_left, hidden_right)
        from_13 = over_zl(add(term[1, 3], from_12).astype(bf16))
        own_other = add(term[1, 0], from_11).astype(bf16)
        from_13, from_02 = tie(from_13, from_02)
        from_03 = over_y(add(term[0, 3], from_13).astype(bf16), -1)
        from_01 = over_y(add(term[0, 1], from_02).astype(bf16), 1)
        from_10 = over_zl(own_other)
        from_03, from_10, from_01 = tie(from_03, from_10, from_01)
        resid_strips = lax.dynamic_slice_in_dim(pieces, y // 2, 1, 1)[:, 0]
        layer = add(term[0, 0], resid_strips, from_01, from_03, from_10)

    with jax.named_scope("strip_exchange"):
        low_layer = layer.astype(bf16)
        strips_x = [lax.dynamic_slice_in_dim(low_layer, x, 1, 0)]
        for step in (1, -1, 2):
            strip = lax.dynamic_slice_in_dim(low_layer, (x + step) % NX, 1, 0)
            strips_x.append(over_x(strip, step))
        message = jnp.concatenate(strips_x, axis=0)

    with jax.named_scope("norm"):
        squares = jnp.sum(layer * layer, axis=(0, 2)).reshape(seqs_here, SEQ)
        squares = jnp.sum(gather_small(squares, "tensor"), axis=0)
        message, squares, hidden_far = tie(message, squares, hidden_far)
        hidden_rows = jnp.concatenate([hidden, hidden_left, hidden_right, hidden_far], axis=0)
        got = gather_start(message)
        inverse = lax.rsqrt(squares / model_width + eps_norm)
        weighted = layer.reshape(NX, seqs_here, SEQ, lanes) * inverse[None, :, :, None]
        means = jnp.mean(weighted, axis=2).transpose(1, 0, 2).reshape(seqs_here, width)

    with jax.named_scope("contrast"):
        means_all = gather_small(means, "dp")
        got, means_all = tie_gather(got, means_all)
        got = gather_next(got)
        means_all = means_all.reshape(seqs, width)
        parts = gather_small(gram_part(means_all, gain_own, x), "tensor")
        row_blocks = jnp.concatenate([low_layer, low_layer], axis=0)
        row_blocks = lax.dynamic_slice_in_dim(row_blocks, x + 1, NX - 1, 0)
        row_blocks = jnp.pad(row_blocks, ((0, 0), (0, 16), (0, 0)))
        got, parts, row_blocks, hidden_rows = tie_gather(got, parts, row_blocks, hidden_rows)
        half = NX // 2
        got[1, 2] = over_y(got[1, 1][:half], -1)
        strips = [got[key] for key in KEYS] + [over_y(got[1, 3][half:], 1)]
        scaled, gain_grad_x, scaled_own, gain_grad = contrast(
            parts, same, gain_blocks, means_all, gain_own, x
        )

    with jax.named_scope("row_gather"):
        own_rows = lax.dynamic_slice_in_dim(scaled_own, shard * seqs_here, seqs_here, 0)
        own_rows = jnp.pad(jnp.concatenate([own_rows, gain_grad], axis=0), ((0, 8 - seqs_here - 1), (0, 0)))
        high = lax.reduce_precision(own_rows, exponent_bits=8, mantissa_bits=7)
        tail = jnp.concatenate([high, own_rows - high], axis=0).astype(bf16)
        tail = tail.reshape(16, NX, lanes).transpose(1, 0, 2)
        tail = lax.dynamic_slice_in_dim(jnp.concatenate([tail, tail], axis=0), x + 1, NX - 1, 0)
        rows = gather_start(lax.dynamic_update_slice(row_blocks, tail, (0, tokens, 0)))

    with jax.named_scope("along"):
        own_inverse = jnp.where(jnp.arange(NX)[:, None, None] == x, inverse[None], 0.0)
        sums = jnp.concatenate([along_part(strips, scaled, plan), own_inverse], axis=0)
        sums = sums + lax.ppermute(sums, "dp", swap_route(1))
        rows, sums = tie_gather(rows, sums)
        rows = gather_next(rows)
        sums = sums + lax.ppermute(sums, "dp", swap_route(2))

    with jax.named_scope("down_grad"):
        low_x, coef = group_grad(strips, scaled, sums, plan)
        rows, low_x = tie_gather(rows, low_x)
        rows = gather_last(rows, tokens // 2)

        def down(low):
            return lax.dot_general(
                hidden_rows, low, (((0,), (0,)), ((), ())), preferred_element_type=f32
            )

        part3, low_x = tie(down(low_x[3]), low_x)
        part1, low_x = tie(down(low_x[1]), low_x)
        from_core = over_core(part3), over_core(part1)
        summed = (down(low_x[2]) + from_core[0]).astype(bf16)
        summed, low0 = tie(summed, low_x[0])
        across = over_zh(summed)
        rows, low0 = tie_gather(rows, low0)
        near = down(low0) + from_core[1]

    with jax.named_scope("hidden_grad"):
        rows, near = tie_gather(rows, near)
        rows = [rows[key] for key in KEYS + ("rest",)]
        grad_hidden, grad_resid, gain_grad = hidden_grad(
            rows, strips[:group], scaled, gain_grad_x, inverse, coef, down_weight, plan
        )
        grad_gain = gain_grad.reshape(width)

    with jax.named_scope("down_grad"):
        across, grad_hidden = tie(across, grad_hidden)
        grad_down = near + across.astype(f32)

    return (grad_hidden, grad_resid, grad_down, grad_gain)


def solution(mesh):
    return jax.shard_map(
        per_device,
        mesh=mesh,
        in_specs=(P("dp", "tensor"), P("dp", "tensor"), P("tensor", None), P(), P()),
        out_specs=(P("dp", "tensor"), P("dp", "tensor"), P("tensor", "dp"), P("tensor")),
        check_vma=False,
    )
```
